32 devices in a mesh: replica: 8 (over y, x, core), shard: 4 (over z).
Axes of the slice: x: 2, y: 2, z: 4, core: 2. Of those that a mesh axis runs over, the one named last changes fastest.
Arguments:
- clips: bfloat16 [16, 256, 1024], P('replica', 'shard'), may hold values from -6 to 6
- cotangent: bfloat16 [16, 256, 1024], P('replica', 'shard'), may hold values from -6 to 6
- live_count: int32 [8], P('replica'), may hold values from 1 to 2, 12 in all
- w_qkv: bfloat16 [1024, 3072], P('shard'), may hold values from -0.1875 to 0.1875
- w_out: bfloat16 [1024, 1024], P('shard'), may hold values from -1.5 to 1.5
- w_fc1: bfloat16 [1024, 4096], P('shard'), may hold values from -0.1875 to 0.1875
- w_fc2: bfloat16 [4096, 1024], P('shard'), may hold values from -0.09375 to 0.09375
- norm_gain: bfloat16 [2, 1024], P(None, 'shard'), may hold values from 0.5 to 1.5
- norm_bias: bfloat16 [2, 1024], P(None, 'shard'), may hold values from -1.796875 to 1.796875
- proj_bias: bfloat16 [4, 1024], P(None, 'shard'), may hold values from -1.796875 to 1.796875
- fc1_bias: bfloat16 [4096], P('shard'), may hold values from -1.796875 to 1.796875
Outputs:
- out: bfloat16 [16, 256, 1024], P('replica', 'shard')
- clips_grad: float32 [16, 256, 1024], P('replica', 'shard')
- w_qkv_grad: float32 [1024, 3072], P('shard')
- w_out_grad: float32 [1024, 1024], P('shard')
- w_fc1_grad: float32 [1024, 4096], P('shard')
- w_fc2_grad: float32 [4096, 1024], P('shard')
- norm_gain_grad: float32 [2, 1024], P(None, 'shard')
- norm_bias_grad: float32 [2, 1024], P(None, 'shard')
- proj_bias_grad: float32 [4, 1024], P(None, 'shard')
- fc1_bias_grad: float32 [4096], P('shard')
The draws below stay inside these ranges and needn't reach their ends.
Inputs may be any that keep to these rules, and one draw needn't show every extreme that they name: `live_count`: each replica group holds its clips in its first places; some group holds 2, and there are 12 clips in all.
All inputs are finite; a program needn't handle non-finite values.
Results may differ from the reference program's by a relative error of at most 0.0085.
Values may be sent and summed in bfloat16 or wider, within the bound.
A program may use at most 192 MiB of HBM per device.

```python
import math
import jax
import jax.numpy as jnp
import numpy as np
from jax import lax

D = 1024
FF = 4096
HEADS = 16
HEAD_DIM = 64
SLOTS = 2
LEN = 256
CLIP_SLOTS = 16
CLIPS = 12
N_REPLICA = 8


def block_levels(stream_key, dims, pieces, low, high):
    loudness = 1.0
    for axis_at, shards_of in pieces:
        draws = jax.random.uniform(jax.random.fold_in(jax.random.fold_in(stream_key, 6), axis_at), (shards_of,), jnp.float32, low / len(pieces), high / len(pieces))
        loudness = loudness * jnp.repeat(jnp.exp(draws), dims[axis_at] // shards_of).reshape((-1,) + (1,) * (len(dims) - 1 - axis_at))
    return loudness


def profile(amount, total, limit, skew):
    portions = [(1 << 20) // math.isqrt(rank ** skew) + 1 for rank in range(2, amount + 1)]
    rest, given = total - limit - (amount - 1), [1] * (amount - 1)
    while rest > 0:
        candidates = [i for i in range(amount - 1) if given[i] < limit]
        whole, remaining = sum([portions[i] for i in candidates]), rest
        for i in candidates:
            more = min(limit - given[i], max(1, remaining * portions[i] // whole), rest)
            given[i] = given[i] + more
            rest = rest - more
    return np.array([limit] + given)


def uneven_parts(own_key, number_of, total, most, lean):
    if number_of == 2:
        one = jax.random.randint(own_key, (), max(1, total - most), min(most, total - 1) + 1)
        return jnp.stack([one, total - one])
    sizes = jnp.asarray(profile(number_of, total, most, lean), jnp.int32)
    twos = (number_of - 1) // 2
    giver, receiver = sizes[1:1 + 2 * twos:2], sizes[2:2 + 2 * twos:2]
    room = jnp.minimum(giver - 1, most - receiver)
    passed = jax.random.randint(jax.random.fold_in(own_key, 1), (twos,), 0, 1 << 20) % (room + 1)
    sizes = sizes.at[1:1 + 2 * twos:2].set(giver - passed).at[2:2 + 2 * twos:2].set(receiver + passed)
    return sizes[jax.random.permutation(jax.random.fold_in(own_key, 2), number_of)]


def gaussian(key, extent, scale, reach, shards=(), held_as=jnp.bfloat16):
    values = jax.random.normal(key, extent, jnp.float32) * scale
    if len(shards) > 0:
        values = block_levels(key, extent, shards, -0.22, 0.18) * values
    return jnp.clip(values, min=-reach, max=reach).astype(held_as)


def setup_inputs(seed: int = 0) -> dict:
    arg_keys = jax.random.split(jax.random.key(seed), 12)
    clips = gaussian(arg_keys[0], (CLIP_SLOTS, LEN, D), 1.0, 6.0, ((0, 8), (1, 4)))
    cotangent = gaussian(arg_keys[1], (CLIP_SLOTS, LEN, D), 1.0, 6.0, ((0, 8), (1, 4)))
    live_count = uneven_parts(arg_keys[2], N_REPLICA, CLIPS, SLOTS, 2).astype(jnp.int32)
    w_qkv = gaussian(arg_keys[3], (D, 3 * D), D ** -0.5, 0.1875, ((0, 4),))
    w_out = gaussian(arg_keys[4], (D, D), (D // 64) ** -0.5, 1.5, ((0, 4),))
    w_fc1 = gaussian(arg_keys[5], (D, FF), D ** -0.5, 0.1875, ((0, 4),))
    w_fc2 = gaussian(arg_keys[6], (FF, D), FF ** -0.5, 0.09375, ((0, 4),))
    norm_gain = jnp.clip(1.0 + 0.1 * jax.random.normal(arg_keys[7], (2, D), jnp.float32), 0.5, 1.5).astype(jnp.bfloat16)
    norm_bias = gaussian(arg_keys[8], (2, D), 0.3, 1.796875, ((1, 4),))
    proj_bias = gaussian(arg_keys[9], (4, D), 0.3, 1.796875, ((1, 4),))
    fc1_bias = gaussian(arg_keys[10], (FF,), 0.3, 1.796875, ((0, 4),))
    return dict(clips=clips, cotangent=cotangent, live_count=live_count, w_qkv=w_qkv, w_out=w_out, w_fc1=w_fc1, w_fc2=w_fc2, norm_gain=norm_gain, norm_bias=norm_bias, proj_bias=proj_bias, fc1_bias=fc1_bias)


@jax.custom_vjp
def low(v):
    return lax.optimization_barrier(v.astype(jnp.bfloat16)).astype(jnp.float32)

@jax.custom_vjp
def low_back(v):
    return v

def low_keep(v):
    return (low(v), None)

def low_pass(kept, grad):
    return (grad,)

def back_keep(v):
    return (v, None)

def back_low(kept, grad):
    return (low(grad),)
low.defvjp(low_keep, low_pass)
low_back.defvjp(back_keep, back_low)

def normed(value):
    centre = value - lax.optimization_barrier(jnp.mean(value, axis=-1, keepdims=True))
    spread = lax.optimization_barrier(jnp.mean(centre * centre, axis=-1, keepdims=True))
    return centre * lax.rsqrt(spread + 1e-06)

def layer(params, clip, alive):
    w_qkv, w_out, w_fc1, w_fc2, gain_vectors, norm_shift_bias, pbias, fbias = params
    hp = lax.Precision.HIGHEST
    width = clip.shape[1]
    length = clip.shape[0]
    scale = 1.0 / math.sqrt(HEAD_DIM)
    first_branch = low(normed(clip) * gain_vectors[0] + norm_shift_bias[0])
    joint = jnp.dot(first_branch, w_qkv, precision=hp)
    query = low(low_back(joint[:, :width] + pbias[0]))
    keys = low(low_back(joint[:, width:2 * width]))
    values = low(low_back(joint[:, 2 * width:] + pbias[1]))
    qh = query.reshape(length, HEADS, HEAD_DIM)
    kh = keys.reshape(length, HEADS, HEAD_DIM)
    vh = values.reshape(length, HEADS, HEAD_DIM)
    scores = low_back(jnp.einsum('qhd,khd->hqk', qh, kh, precision=hp) * scale)
    probs = low(jax.nn.softmax(scores, axis=-1))
    mixed = jnp.einsum('hqk,khd->qhd', probs, vh, precision=hp).reshape(length, width)
    mixed = low(low_back(mixed))
    branch = low_back(jnp.dot(mixed, w_out, precision=hp) + pbias[2])
    residual_stream = clip + branch
    second_branch = low(normed(residual_stream) * gain_vectors[1] + norm_shift_bias[1])
    pre = low_back(jnp.dot(second_branch, w_fc1, precision=hp) + fbias)
    act = low(jax.nn.gelu(pre, approximate=False))
    mlp = low_back(jnp.dot(act, w_fc2, precision=hp) + pbias[3])
    return (residual_stream + mlp) * alive

def reference(clips, cotangent, live_count, w_qkv, w_out, w_fc1, w_fc2, norm_gain, norm_bias, proj_bias, fc1_bias):
    places = jnp.arange(CLIP_SLOTS, dtype=jnp.int32)
    alive = (places % SLOTS < live_count[places // SLOTS]).astype(jnp.float32)
    params = tuple((p.astype(jnp.float32) for p in (w_qkv, w_out, w_fc1, w_fc2, norm_gain, norm_bias, proj_bias, fc1_bias)))
    inputs = clips.astype(jnp.float32)
    stepper = jax.checkpoint(layer)

    def whole(w_a, w_b, w_c, w_d, g_a, g_b, g_c, g_d, xs):
        plist = (w_a, w_b, w_c, w_d, g_a, g_b, g_c, g_d)
        return lax.map(lambda item: stepper(plist, item[0], item[1]), (xs, alive))
    result, pull = jax.vjp(whole, *params, inputs)
    grads = pull(cotangent.astype(jnp.float32))
    return (result.astype(jnp.bfloat16), grads[8], grads[0], grads[1], grads[2], grads[3], grads[4], grads[5], grads[6], grads[7])
```

```python
import functools
import math

import jax
import jax.numpy as jnp
from jax import lax
from jax.experimental import pallas as pl
from jax.experimental.pallas import tpu as pltpu
from jax.sharding import PartitionSpec as P

MESH = pl.DeviceIdType.MESH
F32 = jnp.float32
BF16 = jnp.bfloat16
HEAD = 64
PLANE = 8
RANKS = 4
SLOTS = 2
SEMS = 192


def mm(a, b):
    return jnp.dot(a, b, preferred_element_type=F32)


def mm_nt(a, b):
    return lax.dot_general(a, b, (((1,), (1,)), ((), ())), preferred_element_type=F32)


def mm_tn(a, b):
    return lax.dot_general(a, b, (((0,), (0,)), ((), ())), preferred_element_type=F32)


def normed(v):
    centre = v - jnp.mean(v, axis=-1, keepdims=True)
    spread = jnp.mean(centre * centre, axis=-1, keepdims=True)
    inverse = lax.rsqrt(spread + 1e-6)
    return centre * inverse, inverse


def norm_back(e, xh, inverse):
    first = jnp.mean(e, axis=-1, keepdims=True)
    second = jnp.mean(e * xh, axis=-1, keepdims=True)
    return inverse * (e - first - xh * second)


def kernel(
    Z,
    live, clips, cot, smalls, w_qkv, w_out, w_fc1, w_fc2,
    out_k, cg_k, oq, oo, o1, o2, sm_out,
    rc, cm, dmt, smg, tmp, wq, wo, w1, w2,
    n1, n2, dmb, dab, qkv, probs, ob, ab, mb, d2b, d1b, ra, rm, rd2, rd1,
    h1, dh1, slope, gb, dub, dob, dqkv, gq, go, g1, g2,
    cq, co, c1, c2, zq, zo, z1, z2, fq, fo, f1, f2,
    outb, cgb, sms, smc, smz, smx, outr, cgr,
    ssem, rsem, lsem,
):
    replica = lax.axis_index("replica")
    z = lax.axis_index("shard")
    r8 = replica % PLANE
    base = replica - r8
    q = r8 // 2
    c = r8 % 2
    qx = (q // 2) * 2 + (1 - q % 2)
    qy = (1 - q // 2) * 2 + q % 2
    peers = (qx, qy, 3 - q)

    def dev(rank, core, plane):
        return (base + 2 * rank + core, plane)

    partner = dev(q, 1 - c, z)

    sems = iter(range(SEMS))

    def take(n):
        first = next(sems)
        for _ in range(n - 1):
            next(sems)
        return first

    pending = []

    def send(src, dst, sem, device, when=None):
        def go_():
            pltpu.make_async_remote_copy(src, dst, ssem.at[sem], rsem.at[sem], device_id=device, device_id_type=MESH).start()

        def end_():
            pltpu.make_async_remote_copy(src, dst, ssem.at[sem], rsem.at[sem], device_id=device, device_id_type=MESH).wait_send()

        if when is None:
            go_()
            pending.append(end_)
        else:
            pl.when(when)(go_)
            pending.append(lambda: pl.when(when)(end_))

    def arrive(dst, sem, when=None):
        def go_():
            pltpu.make_async_remote_copy(dst, dst, ssem.at[sem], rsem.at[sem], device_id=partner, device_id_type=MESH).wait_recv()

        if when is None:
            go_()
        else:
            pl.when(when)(go_)

    def target(s):
        return (q + z) % RANKS, (q + 2 * s + c) % RANKS

    def origin(s):
        a = (z - 2 * s - c + 2 * RANKS) % RANKS
        return a, (q - a + RANKS) % RANKS

    moves = [target(s) for s in range(SLOTS)]
    backs = [origin(s) for s in range(SLOTS)]

    def stays(place):
        return jnp.logical_and(place[0] == q, place[1] == z)

    barrier = pltpu.get_barrier_semaphore()
    for rank in peers:
        pl.semaphore_signal(barrier, inc=1, device_id=dev(rank, c, z), device_id_type=MESH)
    pl.semaphore_signal(barrier, inc=1, device_id=partner, device_id_type=MESH)
    for d in range(1, Z):
        pl.semaphore_signal(barrier, inc=1, device_id=(replica, (z + d) % Z), device_id_type=MESH)
    count = RANKS - 1 + 1 + Z - 1
    for place in moves + backs:

        @pl.when(jnp.logical_not(stays(place)))
        def _(place=place):
            pl.semaphore_signal(barrier, inc=1, device_id=dev(place[0], c, place[1]), device_id_type=MESH)

        count = count + jnp.where(stays(place), 0, 1)
    pl.semaphore_wait(barrier, count)

    def exchange(src, dst, sem, places):
        for s in range(SLOTS):
            to = dev(places[s][0], c, places[s][1])
            send(src.at[s], dst.at[s], sem + s, to, when=jnp.logical_not(stays(places[s])))

            @pl.when(stays(places[s]))
            def _(s=s):
                pltpu.make_async_copy(src.at[s], dst.at[s], rsem.at[sem + s]).start()

    def exchange_wait(dst, sem):
        for s in range(SLOTS):
            arrive(dst.at[s], sem + s)

    loads = []

    def load(src, dst, k):
        cp = pltpu.make_async_copy(src, dst, lsem.at[k])
        cp.start()
        return cp

    e_clips, e_cot, e_out, e_cg = take(2), take(2), take(2), take(2)
    exchange(clips, rc, e_clips, moves)

    strip = (q // 2) * 128
    loads_q = [
        load(w_qkv.at[:, pl.ds(pl.multiple_of(t * 1024 + zz * 256 + strip, 128), 128)], tmp.at[t * RANKS + zz], t * RANKS + zz)
        for t in range(3)
        for zz in range(RANKS)
    ]
    loads_o = [
        load(w_out.at[pl.ds(pl.multiple_of(q * HEAD, HEAD), HEAD), :], wo.at[z], 12),
    ]
    loads_1 = [
        load(w_fc1.at[:, pl.ds(pl.multiple_of(zz * 1024 + q * 256, 256), 256)], w1.at[z, :, pl.ds(zz * 256, 256)], 13 + zz)
        for zz in range(RANKS)
    ]
    loads_2 = [load(w_fc2.at[pl.ds(pl.multiple_of(q * 256, 256), 256), :], w2.at[z], 17)]

    s_small = take(3)
    smg[z] = smalls[...]
    for d in range(1, Z):
        send(smalls, smg.at[z], s_small + d - 1, (replica, (z + d) % Z))

    for s in range(SLOTS):
        alive = jnp.where(live[0] > s, 1.0, 0.0).astype(F32)
        cm[s] = (cot[s].astype(F32) * alive).astype(BF16)

    def line_step(w, half, sem, i):
        rows = pl.ds(pl.multiple_of(c * half, half), half)
        up = jnp.logical_and(z - i >= 0, z < Z - 1)
        uc = jnp.maximum(z - i, 0)
        send(w.at[uc, rows], w.at[uc, rows], sem + i, (replica, jnp.minimum(z + 1, Z - 1)), when=up)
        down = jnp.logical_and(z + i <= Z - 1, z > 0)
        dc = jnp.minimum(z + i, Z - 1)
        send(w.at[dc, rows], w.at[dc, rows], sem + Z - 1 + i, (replica, jnp.maximum(z - 1, 0)), when=down)

    def line_wait(w, half, sem, i):
        rows = pl.ds(pl.multiple_of(c * half, half), half)
        arrive(w.at[jnp.maximum(z - 1 - i, 0), rows], sem + i, when=z - 1 - i >= 0)
        arrive(w.at[jnp.minimum(z + 1 + i, Z - 1), rows], sem + Z - 1 + i, when=z + 1 + i <= Z - 1)

    def core_share(w, half, sem):
        rows = pl.ds(pl.multiple_of(c * half, half), half)
        for d in range(1, Z):
            zz = (z + d) % Z
            send(w.at[zz, rows], w.at[zz, rows], sem + zz, partner)

    def core_share_wait(w, half, sem):
        rows = pl.ds(pl.multiple_of((1 - c) * half, half), half)
        for d in range(1, Z):
            zz = (z + d) % Z
            arrive(w.at[zz, rows], sem + zz)

    a_q, a_o, a_1, a_2 = (take(2 * (Z - 1)) for _ in range(4))
    k_q, k_o, k_1, k_2 = (take(Z) for _ in range(4))

    for cp in loads_q:
        cp.wait()
    lane = lax.broadcasted_iota(jnp.int32, (256, 128), 1)
    even = q % 2 == 0
    for t in range(3):
        for pair in range(2):
            left = tmp[t * RANKS + 2 * pair].astype(F32)
            right = tmp[t * RANKS + 2 * pair + 1].astype(F32)
            lo = jnp.where(even, left, pltpu.roll(left, HEAD, 1))
            hi = jnp.where(even, pltpu.roll(right, HEAD, 1), right)
            wq[z, :, t * 256 + pair * 128 : t * 256 + pair * 128 + 128] = jnp.where(lane < HEAD, lo, hi).astype(BF16)
    for cp in loads_o:
        cp.wait()
    line_step(wq, 128, a_q, 0)
    line_step(wo, 32, a_o, 0)

    def plane_gather(buf, sem):
        for k, rank in enumerate(peers):
            send(buf.at[:, q], buf.at[:, q], sem + k, dev(rank, c, z))

    def plane_gather_wait(buf, sem):
        for k, rank in enumerate(peers):
            arrive(buf.at[:, rank], sem + k)

    def plane_scatter(buf, dst, sem):
        for k, rank in enumerate(peers):
            send(buf.at[:, rank], dst.at[k], sem + k, dev(rank, c, z))

    def plane_scatter_sum(buf, dst, sem):
        for k in range(RANKS - 1):
            arrive(dst.at[k], sem + k)
        total = buf[:, q].astype(F32)
        for k in range(RANKS - 1):
            total = total + dst[k].astype(F32)
        return total.reshape(SLOTS * 64, 1024)

    for d in range(1, Z):
        arrive(smg.at[(z - d + Z) % Z], s_small + d - 1)

    def row(i):
        return jnp.concatenate([smg[zz, i : i + 1, :] for zz in range(Z)], axis=1)

    exchange_wait(rc, e_clips)
    x = rc[...].astype(F32).reshape(128, 1024)
    xh, _ = normed(x)
    p_n1, p_a, p_n2, p_dm, p_m, p_d2, p_da, p_d1 = (take(3) for _ in range(8))
    n1[:, q] = (xh * row(0) + row(2)).astype(BF16).reshape(SLOTS, 64, 1024)
    plane_gather(n1, p_n1)

    line_wait(wq, 128, a_q, 0)
    line_step(wq, 128, a_q, 1)
    line_wait(wo, 32, a_o, 0)
    line_step(wo, 32, a_o, 1)
    line_wait(wq, 128, a_q, 1)
    line_step(wq, 128, a_q, 2)
    line_wait(wo, 32, a_o, 1)
    line_step(wo, 32, a_o, 2)
    for cp in loads_1 + loads_2:
        cp.wait()
    line_step(w1, 128, a_1, 0)
    line_wait(wq, 128, a_q, 2)
    core_share(wq, 128, k_q)
    line_wait(wo, 32, a_o, 2)
    core_share(wo, 32, k_o)
    plane_gather_wait(n1, p_n1)
    exchange(cm, dmt, e_cot, moves)
    core_share_wait(wq, 128, k_q)

    bias_q = smg[0, 12:13, :] + smg[1, 12:13, :] + smg[2, 12:13, :] + smg[3, 12:13, :]
    bias_v = smg[0, 13:14, :] + smg[1, 13:14, :] + smg[2, 13:14, :] + smg[3, 13:14, :]

    def qkv_step(s, _):
        left = n1[s].reshape(256, 1024)
        for t in range(3):
            val = mm(left, wq[:, :, t * 256 : t * 256 + 256].reshape(1024, 256))
            if t == 0:
                val = val + bias_q
            if t == 2:
                val = val + bias_v
            qkv[t, s] = val.astype(BF16)
        return 0

    lax.fori_loop(0, SLOTS, qkv_step, 0)
    line_wait(w1, 128, a_1, 0)
    line_step(w1, 128, a_1, 1)

    def attend(i, _):
        s = i // 2
        pair = i % 2
        cols = pl.ds(pl.multiple_of(pair * 128, 128), 128)
        qq, kk, vv = qkv[0, s, :, cols], qkv[1, s, :, cols], qkv[2, s, :, cols]
        outs = []
        for j in range(2):
            h = slice(j * HEAD, j * HEAD + HEAD)
            score = mm_nt(qq[:, h], kk[:, h]) * (1.0 / math.sqrt(HEAD))
            e = jnp.exp(score - jnp.max(score, axis=-1, keepdims=True))
            p = e / jnp.sum(e, axis=-1, keepdims=True)
            probs[i, j] = p
            outs.append(mm(p.astype(BF16), vv[:, h]))
        ob[s, :, cols] = jnp.concatenate(outs, axis=1).astype(BF16)
        return 0

    lax.fori_loop(0, 2 * SLOTS, attend, 0)
    core_share_wait(wo, 32, k_o)

    def proj_step(s, _):
        val = mm(ob[s], wo[...].reshape(256, 1024))
        ab[s] = val.astype(BF16).reshape(RANKS, 64, 1024)
        return 0

    lax.fori_loop(0, SLOTS, proj_step, 0)
    plane_scatter(ab, ra, p_a)
    line_wait(w1, 128, a_1, 1)
    line_step(w1, 128, a_1, 2)
    line_step(w2, 128, a_2, 0)
    a = plane_scatter_sum(ab, ra, p_a) + row(6)
    hh = x + a
    h1[...] = hh
    xh2, _ = normed(hh)
    n2[:, q] = (xh2 * row(1) + row(3)).astype(BF16).reshape(SLOTS, 64, 1024)
    plane_gather(n2, p_n2)
    exchange_wait(dmt, e_cot)
    dmb[:, q] = dmt[...]
    plane_gather(dmb, p_dm)
    line_wait(w1, 128, a_1, 2)
    core_share(w1, 128, k_1)
    line_wait(w2, 128, a_2, 0)
    line_step(w2, 128, a_2, 1)
    core_share_wait(w1, 128, k_1)
    plane_gather_wait(n2, p_n2)

    def fc1_step(i, _):
        s = i // RANKS
        zz = i % RANKS
        cols = pl.ds(pl.multiple_of(zz * 256, 256), 256)
        u = mm(n2[s].reshape(256, 1024), w1[:, :, cols].reshape(1024, 256)) + smg[zz, pl.ds(8 + q, 1), :]
        cdf = 0.5 * (1.0 + lax.erf(u * (1.0 / math.sqrt(2.0))))
        gb[s, :, cols] = (u * cdf).astype(BF16)
        slope[s, :, cols] = cdf + u * jnp.exp(-0.5 * u * u) * (1.0 / math.sqrt(2.0 * math.pi))
        return 0

    lax.fori_loop(0, SLOTS * RANKS, fc1_step, 0)
    line_wait(w2, 128, a_2, 1)
    line_step(w2, 128, a_2, 2)
    plane_gather_wait(dmb, p_dm)
    line_wait(w2, 128, a_2, 2)
    core_share(w2, 128, k_2)
    core_share_wait(w2, 128, k_2)

    def du_step(i, _):
        s = i // RANKS
        zz = i % RANKS
        cols = pl.ds(pl.multiple_of(zz * 256, 256), 256)
        dg = mm_nt(dmb[s].reshape(256, 1024), w2[zz])
        dub[s, :, cols] = (dg * slope[s, :, cols]).astype(BF16)
        return 0

    lax.fori_loop(0, SLOTS * RANKS, du_step, 0)

    def dn2_step(i, _):
        s = i // RANKS
        zz = i % RANKS
        cols = pl.ds(pl.multiple_of(zz * 256, 256), 256)
        d2b[s, :, :, cols] = mm_nt(dub[s], w1[zz]).astype(BF16).reshape(RANKS, 64, 256)
        return 0

    lax.fori_loop(0, SLOTS * RANKS, dn2_step, 0)
    plane_scatter(d2b, rd2, p_d2)

    t_core = [take(1) for _ in range(4)]
    t_line = [take(Z - 1) for _ in range(4)]
    t_rank = [take(3) for _ in range(4)]
    t_pass = [take(4) for _ in range(4)]
    halves = (128, 32, 128, 128)
    grads = (gq, go, g1, g2)
    cores = (cq, co, c1, c2)
    lines = (zq, zo, z1, z2)
    finals = (fq, fo, f1, f2)
    results = (oq, oo, o1, o2)

    def reduce_a(w):
        half = halves[w]
        other = pl.ds(pl.multiple_of((1 - c) * half, half), half)
        send(grads[w].at[:, other], cores[w], t_core[w], partner)

    def reduce_b(w):
        half = halves[w]
        mine = pl.ds(pl.multiple_of(c * half, half), half)
        arrive(cores[w], t_core[w])

        def step(zz, _):
            grads[w][zz, mine] = (grads[w][zz, mine].astype(F32) + cores[w][zz].astype(F32)).astype(BF16)
            return 0

        lax.fori_loop(0, Z, step, 0)
        for d in range(1, Z):
            zz = (z + d) % Z
            send(grads[w].at[zz, mine], lines[w].at[d - 1], t_line[w] + d - 1, (replica, zz))

    def reduce_c(w):
        half = halves[w]
        mine = pl.ds(pl.multiple_of(c * half, half), half)
        for d in range(Z - 1):
            arrive(lines[w].at[d], t_line[w] + d)
        total = grads[w][z, mine].astype(F32)
        for d in range(Z - 1):
            total = total + lines[w][d].astype(F32)
        finals[w][...] = total.astype(BF16)
        place = results[w].at[q, mine]
        for k, rank in enumerate(peers):
            send(finals[w], place, t_rank[w] + k, dev(rank, c, z))
        send(finals[w], place, t_pass[w] + 3, partner)
        cp = pltpu.make_async_copy(finals[w], place, lsem.at[18 + w])
        cp.start()
        pending.append(cp.wait)

    def reduce_d(w):
        half = halves[w]
        mine = pl.ds(pl.multiple_of(c * half, half), half)
        for k, rank in enumerate(peers):
            arrive(results[w].at[rank, mine], t_rank[w] + k)
            send(results[w].at[rank, mine], results[w].at[rank, mine], t_pass[w] + k, partner)

    def reduce_e(w):
        half = halves[w]
        theirs = pl.ds(pl.multiple_of((1 - c) * half, half), half)
        for k, rank in enumerate(peers):
            arrive(results[w].at[rank, theirs], t_pass[w] + k)
        arrive(results[w].at[q, theirs], t_pass[w] + 3)

    def dw2_step(zz, _):
        cols = pl.ds(pl.multiple_of(zz * 256, 256), 256)
        left = gb[:, :, cols].reshape(512, 256)
        g2[zz] = mm_tn(left, dmb[...].reshape(512, 1024)).astype(BF16)
        return 0

    lax.fori_loop(0, RANKS, dw2_step, 0)
    reduce_a(3)

    def dw1_step(zz, _):
        cols = pl.ds(pl.multiple_of(zz * 256, 256), 256)
        left = n2[:, :, :, cols].reshape(512, 256)
        g1[zz] = mm_tn(left, dub[...].reshape(512, 1024)).astype(BF16)
        return 0

    lax.fori_loop(0, RANKS, dw1_step, 0)
    reduce_a(2)
    reduce_b(3)

    def m_step(s, _):
        mb[s] = mm(gb[s], w2[...].reshape(1024, 1024)).astype(BF16).reshape(RANKS, 64, 1024)
        return 0

    lax.fori_loop(0, SLOTS, m_step, 0)
    reduce_b(2)

    sms[...] = jnp.zeros((16, 1024), F32)
    fc1_sum = jnp.sum(dub[...].astype(F32).reshape(512, 1024), axis=0, keepdims=True)
    sms[pl.ds(9 + 2 * q, 1), :] = fc1_sum

    def own(i, val):
        sms[i : i + 1, :] = jnp.sum(val, axis=0, keepdims=True)

    dy = dmt[...].astype(F32).reshape(128, 1024)
    own(7, dy)
    dn2 = plane_scatter_sum(d2b, rd2, p_d2)
    xh2, inv2 = normed(h1[...])
    own(1, dn2 * xh2)
    own(3, dn2)
    res = dy + norm_back(dn2 * row(1), xh2, inv2)
    dh1[...] = res
    da = res.astype(BF16)
    dab[:, q] = da.reshape(SLOTS, 64, 1024)
    plane_gather(dab, p_da)
    own(6, da.astype(F32))
    plane_scatter(mb, rm, p_m)
    plane_gather_wait(dab, p_da)

    def do_step(s, _):
        dob[s] = mm_nt(dab[s].reshape(256, 1024), wo[...].reshape(256, 1024)).astype(BF16)
        return 0

    lax.fori_loop(0, SLOTS, do_step, 0)

    def attend_back(i, _):
        s = i // 2
        pair = i % 2
        cols = pl.ds(pl.multiple_of(pair * 128, 128), 128)
        qq, kk, vv, dd = qkv[0, s, :, cols], qkv[1, s, :, cols], qkv[2, s, :, cols], dob[s, :, cols]
        dqs, dks, dvs = [], [], []
        for j in range(2):
            h = slice(j * HEAD, j * HEAD + HEAD)
            p = probs[i, j]
            dp = mm_nt(dd[:, h], vv[:, h])
            ds = (p * (dp - jnp.sum(p * dp, axis=-1, keepdims=True))).astype(BF16)
            dqs.append(mm(ds, kk[:, h]) * (1.0 / math.sqrt(HEAD)))
            dks.append(mm_tn(ds, qq[:, h]) * (1.0 / math.sqrt(HEAD)))
            dvs.append(mm_tn(p.astype(BF16), dd[:, h]))
        dqkv[0, s, :, cols] = jnp.concatenate(dqs, axis=1).astype(BF16)
        dqkv[1, s, :, cols] = jnp.concatenate(dks, axis=1).astype(BF16)
        dqkv[2, s, :, cols] = jnp.concatenate(dvs, axis=1).astype(BF16)
        return 0

    lax.fori_loop(0, 2 * SLOTS, attend_back, 0)

    def dn1_step(i, _):
        s = i // RANKS
        zz = i % RANKS
        cols = pl.ds(pl.multiple_of(zz * 256, 256), 256)
        val = mm_nt(dqkv[0, s], wq[zz, :, 0:256])
        val = val + mm_nt(dqkv[1, s], wq[zz, :, 256:512])
        val = val + mm_nt(dqkv[2, s], wq[zz, :, 512:768])
        d1b[s, :, :, cols] = val.astype(BF16).reshape(RANKS, 64, 256)
        return 0

    lax.fori_loop(0, SLOTS * RANKS, dn1_step, 0)
    plane_scatter(d1b, rd1, p_d1)

    def dwq_step(zz, _):
        cols = pl.ds(pl.multiple_of(zz * 256, 256), 256)
        left = n1[:, :, :, cols].reshape(512, 256)
        for t in range(3):
            gq[zz, :, t * 256 : t * 256 + 256] = mm_tn(left, dqkv[t].reshape(512, 256)).astype(BF16)
        return 0

    lax.fori_loop(0, RANKS, dwq_step, 0)
    reduce_a(0)
    go[...] = mm_tn(ob[...].reshape(512, 256), dab[...].reshape(512, 1024)).astype(BF16).reshape(Z, HEAD, 1024)
    reduce_a(1)
    reduce_b(0)
    reduce_b(1)
    reduce_c(3)
    reduce_c(2)

    m = plane_scatter_sum(mb, rm, p_m) + row(7)
    outb[...] = (h1[...] + m).astype(BF16).reshape(SLOTS, 64, 1024)
    exchange(outb, outr, e_out, backs)

    dq_sum = jnp.sum(dqkv[0].astype(F32).reshape(512, 256), axis=0, keepdims=True)
    dv_sum = jnp.sum(dqkv[2].astype(F32).reshape(512, 256), axis=0, keepdims=True)
    gap = jnp.zeros((1, 128), F32)
    pieces = []
    for zz in range(Z):
        h = slice(zz * HEAD, zz * HEAD + HEAD)
        pieces += [dq_sum[:, h], dv_sum[:, h], gap]
    sms[pl.ds(8 + 2 * q, 1), :] = jnp.concatenate(pieces, axis=1)

    dn1 = plane_scatter_sum(d1b, rd1, p_d1)
    xh, inv = normed(rc[...].astype(F32).reshape(128, 1024))
    own(0, dn1 * xh)
    own(2, dn1)
    cgb[...] = (dh1[...] + norm_back(dn1 * row(0), xh, inv)).astype(BF16).reshape(SLOTS, 64, 1024)
    exchange(cgb, cgr, e_cg, backs)

    u_core, u_line, u_rank = take(1), take(3), take(3)
    send(sms, smc, u_core, partner)
    reduce_c(0)
    reduce_c(1)
    arrive(smc, u_core)
    both = sms[...] + smc[...]
    for zz in range(Z):
        smx[0, zz] = both[:, zz * 256 : zz * 256 + 256]
    for d in range(1, Z):
        send(smx.at[0, (z + d) % Z], smz.at[d - 1], u_line + d - 1, (replica, (z + d) % Z))
    reduce_d(3)
    reduce_d(2)
    for d in range(Z - 1):
        arrive(smz.at[d], u_line + d)
    smx[1, 0] = smx[0, z] + smz[0] + smz[1] + smz[2]
    for k, rank in enumerate(peers):
        send(smx.at[1, 0], smx.at[1, 1 + k], u_rank + k, dev(rank, c, z))
    reduce_d(0)
    reduce_d(1)
    for k in range(RANKS - 1):
        arrive(smx.at[1, 1 + k], u_rank + k)
    sm_out[...] = smx[1, 0] + smx[1, 1] + smx[1, 2] + smx[1, 3]

    exchange_wait(outr, e_out)
    out_k[...] = outr[...]
    exchange_wait(cgr, e_cg)
    cg_k[...] = cgr[...]
    for w in (3, 2, 0, 1):
        reduce_e(w)
    for end in pending:
        end()


def local(
    n_replica,
    Z,
    clips, cotangent, live_count, w_qkv, w_out, w_fc1, w_fc2, norm_gain, norm_bias, proj_bias, fc1_bias,
):
    z = lax.axis_index("shard")
    q = (lax.axis_index("replica") % PLANE) // 2
    spread = lax.dynamic_slice(proj_bias, (0, q * HEAD), (2, HEAD))
    spread = lax.dynamic_update_slice(jnp.zeros((2, 256), BF16), spread, (0, z * HEAD))
    smalls = jnp.concatenate(
        [norm_gain, norm_bias, proj_bias, fc1_bias.reshape(4, 256), spread, jnp.zeros((2, 256), BF16)], axis=0
    ).astype(F32)
    vm = pl.BlockSpec(memory_space=pltpu.VMEM)
    anyspace = pl.BlockSpec(memory_space=pl.ANY)
    shape = jax.ShapeDtypeStruct
    tile = (SLOTS, 64, 1024)
    group = (SLOTS, RANKS, 64, 1024)
    V = pltpu.VMEM
    scratch = [
        V(tile, BF16), V(tile, BF16), V(tile, BF16), V((4, 16, 256), F32), V((12, 256, 128), BF16),
        V((4, 256, 768), BF16), V((4, 64, 1024), BF16), V((4, 256, 1024), BF16), V((4, 256, 1024), BF16),
        V(group, BF16), V(group, BF16), V(group, BF16), V(group, BF16),
        V((3, SLOTS, 256, 256), BF16), V((4, 2, 256, 256), F32), V((SLOTS, 256, 256), BF16),
        V(group, BF16), V(group, BF16), V(group, BF16), V(group, BF16),
        V((3,) + tile, BF16), V((3,) + tile, BF16), V((3,) + tile, BF16), V((3,) + tile, BF16),
        V((128, 1024), F32), V((128, 1024), F32), V((SLOTS, 256, 1024), F32), V((SLOTS, 256, 1024), BF16),
        V((SLOTS, 256, 1024), BF16), V((SLOTS, 256, 256), BF16), V((3, SLOTS, 256, 256), BF16),
        V((4, 256, 768), BF16), V((4, 64, 1024), BF16), V((4, 256, 1024), BF16), V((4, 256, 1024), BF16),
        V((4, 128, 768), BF16), V((4, 32, 1024), BF16), V((4, 128, 1024), BF16), V((4, 128, 1024), BF16),
        V((3, 128, 768), BF16), V((3, 32, 1024), BF16), V((3, 128, 1024), BF16), V((3, 128, 1024), BF16),
        V((128, 768), BF16), V((32, 1024), BF16), V((128, 1024), BF16), V((128, 1024), BF16),
        V(tile, BF16), V(tile, BF16), V((16, 1024), F32), V((16, 1024), F32), V((3, 16, 256), F32), V((2, 4, 16, 256), F32),
        V(tile, BF16), V(tile, BF16),
        pltpu.SemaphoreType.DMA((SEMS,)), pltpu.SemaphoreType.DMA((SEMS,)), pltpu.SemaphoreType.DMA((24,)),
    ]
    out_k, cg_k, oq, oo, o1, o2, sm = pl.pallas_call(
        functools.partial(kernel, Z),
        out_shape=(
            shape(tile, BF16), shape(tile, BF16), shape((4, 256, 768), BF16), shape((4, 64, 1024), BF16),
            shape((4, 256, 1024), BF16), shape((4, 256, 1024), BF16), shape((16, 256), F32),
        ),
        in_specs=[pl.BlockSpec(memory_space=pltpu.SMEM), vm, vm, vm, anyspace, anyspace, anyspace, anyspace],
        out_specs=(vm, vm, anyspace, anyspace, anyspace, anyspace, vm),
        scratch_shapes=scratch,
        compiler_params=pltpu.CompilerParams(
            collective_id=0, has_side_effects=True, vmem_limit_bytes=60 * 2**20
        ),
        cost_estimate=pl.CostEstimate(flops=10**10, bytes_accessed=2**25, transcendentals=2**21),
    )(live_count, clips, cotangent, smalls, w_qkv, w_out, w_fc1, w_fc2)
    alive = (jnp.arange(SLOTS, dtype=jnp.int32) < live_count[0]).astype(BF16)[:, None, None]
    out = out_k * alive
    clips_grad = cg_k.astype(F32)
    d_wq = oq.astype(F32).reshape(4, 256, 3, 4, HEAD).transpose(1, 2, 3, 0, 4).reshape(256, 3072)
    d_wo = oo.astype(F32).reshape(256, 1024)
    d_w1 = o1.astype(F32).reshape(4, 256, 4, 256).transpose(1, 2, 0, 3).reshape(256, 4096)
    d_w2 = o2.astype(F32).reshape(1024, 1024)
    d_q = sm[8::2, 0:HEAD].reshape(1, 256)
    d_v = sm[8::2, HEAD : 2 * HEAD].reshape(1, 256)
    d_gain, d_nbias = sm[0:2], sm[2:4]
    d_pbias = jnp.concatenate([d_q, d_v, sm[6:8]], axis=0)
    d_fbias = sm[9::2].reshape(1024)
    summed = (d_wq, d_wo, d_w1, d_w2, d_gain, d_nbias, d_pbias, d_fbias)
    if n_replica > PLANE:
        groups = [list(range(i, n_replica, PLANE)) for i in range(PLANE)]
        summed = lax.psum(summed, "replica", axis_index_groups=groups)
    return (out, clips_grad) + tuple(summed)


def solution(mesh):
    in_specs = (
        P("replica", "shard", None),
        P("replica", "shard", None),
        P("replica"),
        P("shard", None),
        P("shard", None),
        P("shard", None),
        P("shard", None),
        P(None, "shard"),
        P(None, "shard"),
        P(None, "shard"),
        P("shard"),
    )
    out_specs = (
        P("replica", "shard", None),
        P("replica", "shard", None),
        P("shard", None),
        P("shard", None),
        P("shard", None),
        P("shard", None),
        P(None, "shard"),
        P(None, "shard"),
        P(None, "shard"),
        P("shard"),
    )
    body = functools.partial(local, mesh.shape["replica"], mesh.shape["shard"])
    return jax.shard_map(body, mesh=mesh, in_specs=in_specs, out_specs=out_specs, check_vma=False)
```

```python
import functools
import math

import jax
import jax.numpy as jnp
from jax import lax
from jax.experimental import pallas as pl
from jax.experimental.pallas import tpu as pltpu
from jax.sharding import PartitionSpec as P

MESH = pl.DeviceIdType.MESH
F32 = jnp.float32
BF16 = jnp.bfloat16
HEAD = 64
PLANE = 8
RANKS = 4
SLOTS = 2
SEMS = 198
LOADS = 18
SCALE = 1.0 / math.sqrt(HEAD)


def mm(a, b):
    return jnp.dot(a, b, preferred_element_type=F32)


def mm_nt(a, b):
    return lax.dot_general(a, b, (((1,), (1,)), ((), ())), preferred_element_type=F32)


def mm_tn(a, b):
    return lax.dot_general(a, b, (((0,), (0,)), ((), ())), preferred_element_type=F32)


def normed(v):
    centre = v - jnp.mean(v, axis=-1, keepdims=True)
    spread = jnp.mean(centre * centre, axis=-1, keepdims=True)
    inverse = lax.rsqrt(spread + 1e-6)
    return centre * inverse, inverse


def norm_back(e, xh, inverse):
    first = jnp.mean(e, axis=-1, keepdims=True)
    second = jnp.mean(e * xh, axis=-1, keepdims=True)
    return inverse * (e - first - xh * second)


def strip(i, width=256):
    return pl.ds(pl.multiple_of(i * width, width), width)


def kernel(
    clips, cot, live, gains, nbias, pbias, fbias, w_qkv, w_out, w_fc1, w_fc2,
    out_k, cg_k, oq, oo, o1, o2, sm_out,
    rc, cm, dmt, sml, smg, tmp, wq, wo, w1, w2,
    n1, n2, dmb, dab, qkv, probs, ob, ab, mb, d2b, d1b, ra, rm, rd2, rd1,
    h1, dh1, slope, gb, dub, dob, dqkv, gq, go, g1, g2,
    cq, co, c1, c2, zq, zo, z1, z2, fq, fo, f1, f2,
    outb, cgb, sms, smc, smz, smx, outr, cgr,
    ssem, rsem, lsem,
):
    Z = 4
    replica = lax.axis_index("replica")
    z = lax.axis_index("shard")
    r8 = replica % PLANE
    base = replica - r8
    q = r8 // 2
    c = r8 % 2
    qx = (q // 2) * 2 + (1 - q % 2)
    qy = (1 - q // 2) * 2 + q % 2
    qd = 3 - q
    lower = z // 2
    mate = 2 * lower + 1 - z % 2
    far_middle = 2 - lower
    far = 2 * (1 - lower)
    middle = jnp.logical_or(z == 1, z == 2)
    end = jnp.logical_not(middle)

    def dev(rank, core, plane):
        return (base + 2 * rank + core, plane)

    px, py, partner = dev(qx, c, z), dev(qy, c, z), dev(q, 1 - c, z)

    counter = [0]

    def take(n):
        counter[0] += n
        return counter[0] - n

    pending = []

    def send(src, dst, sem, device, when=None, out=None, got=None):
        done = sem if out is None else out

        def copy():
            return pltpu.make_async_remote_copy(
                src, dst, ssem.at[done], rsem.at[sem], device_id=device, device_id_type=MESH
            )

        if when is None:
            copy().start()
            pending.append(lambda: copy().wait_send())
        else:
            pl.when(when)(lambda: copy().start())
            pending.append(lambda: pl.when(when)(lambda: copy().wait_send()))

    def arrive(dst, sem):
        pltpu.make_async_remote_copy(
            dst, dst, ssem.at[sem], rsem.at[sem], device_id=partner, device_id_type=MESH
        ).wait_recv()

    def target(s):
        return (q + z) % RANKS, (q + 2 * s + c) % RANKS

    def origin(s):
        a = (z - 2 * s - c + 2 * RANKS) % RANKS
        return a, (q - a + RANKS) % RANKS

    moves = [target(s) for s in range(SLOTS)]
    backs = [origin(s) for s in range(SLOTS)]

    def stays(place):
        return jnp.logical_and(place[0] == q, place[1] == z)

    loads = []

    def load(src, dst):
        cp = pltpu.make_async_copy(src, dst, lsem.at[len(loads)])
        cp.start()
        loads.append(cp)

    pair = (q // 2) * 128
    for t in range(3):
        for zz in range(RANKS):
            load(w_qkv.at[:, pl.ds(pl.multiple_of(t * 1024 + zz * 256 + pair, 128), 128)], tmp.at[t * RANKS + zz])
    load(w_out.at[strip(q, HEAD), :], wo.at[z])

    barrier = pltpu.get_barrier_semaphore()
    for device in (px, py, dev(qd, c, z), partner):
        pl.semaphore_signal(barrier, inc=1, device_id=device, device_id_type=MESH)
    for d in range(1, Z):
        pl.semaphore_signal(barrier, inc=1, device_id=(replica, (z + d) % Z), device_id_type=MESH)
    count = 4 + Z - 1
    for place in moves + backs:

        @pl.when(jnp.logical_not(stays(place)))
        def _(place=place):
            pl.semaphore_signal(barrier, inc=1, device_id=dev(place[0], c, place[1]), device_id_type=MESH)

        count = count + jnp.where(stays(place), 0, 1)

    sml[...] = jnp.zeros((16, 256), F32)
    sml[0:2] = gains[...].astype(F32)
    sml[2:4] = nbias[...].astype(F32)
    sml[4:8] = pbias[...].astype(F32)
    for k in range(RANKS):
        sml[8 + k : 9 + k] = fbias[pl.ds(k * 256, 256)].astype(F32).reshape(1, 256)
    lane = lax.broadcasted_iota(jnp.int32, (8, 256), 1)
    turned = pltpu.roll(sml[0:8], (z * HEAD - q * HEAD + 256) % 256, 1)
    kept = jnp.where(jnp.logical_and(lane >= z * HEAD, lane < z * HEAD + HEAD), turned, 0.0)
    sml[12:14] = kept[4:6]

    pl.semaphore_wait(barrier, count)

    def exchange(src, dst, sem, places):
        for s in range(SLOTS):
            to = dev(places[s][0], c, places[s][1])
            send(src.at[s], dst.at[s], sem + s, to, when=jnp.logical_not(stays(places[s])))

            @pl.when(stays(places[s]))
            def _(s=s):
                pltpu.make_async_copy(src.at[s], dst.at[s], rsem.at[sem + s]).start()

    def exchange_wait(dst, sem):
        for s in range(SLOTS):
            arrive(dst.at[s], sem + s)

    e_clips, e_cot, e_out, e_cg = take(2), take(2), take(2), take(2)
    exchange(clips, rc, e_clips, moves)
    s_small = take(3)
    smg[z] = sml[...]
    for d in range(1, Z):
        send(sml, smg.at[z], s_small + d - 1, (replica, (z + d) % Z))
    n_first = len(loads)
    for zz in range(RANKS):
        load(w_fc1.at[:, pl.ds(pl.multiple_of(zz * 1024 + q * 256, 256), 256)], w1.at[z, :, pl.ds(zz * 256, 256)])
    load(w_fc2.at[strip(q), :], w2.at[z])

    def mine(half):
        return pl.ds(pl.multiple_of(c * half, half), half)

    def theirs(half):
        return pl.ds(pl.multiple_of((1 - c) * half, half), half)

    def line_a(w, half, sem):
        own_part = w.at[z, mine(half)]
        send(own_part, own_part, sem, (replica, mate))
        send(own_part, own_part, sem + 1 + z % 2, (replica, far_middle), got=middle)

    def share(w, half, sem, zz, when=None):
        part = w.at[zz, mine(half)]
        send(part, part, sem + 4 + (zz - z + Z) % Z, partner, when=when)

    def line_b(w, half, sem):
        for f in (lower, 1 - lower):

            @pl.when(middle)
            def _(f=f):
                arrive(w.at[far + f, mine(half)], sem + 1 + f)

            part = w.at[far + f, mine(half)]
            send(part, part, sem + 1 + f, (replica, mate), when=middle, out=sem + 3 + f, got=end)
            share(w, half, sem, far + f, when=middle)

    def line_c(w, half, sem):
        arrive(w.at[mate, mine(half)], sem)
        share(w, half, sem, mate)
        for f in (lower, 1 - lower):

            @pl.when(end)
            def _(f=f):
                arrive(w.at[far + f, mine(half)], sem + 1 + f)

            share(w, half, sem, far + f, when=end)

    def line_d(w, half, sem):
        for zz in (mate, far + lower, far + 1 - lower):
            arrive(w.at[zz, theirs(half)], sem + 4 + (zz - z + Z) % Z)

    a_q, a_o, a_1, a_2 = (take(8) for _ in range(4))

    CUT = 2
    ROWS = 64 // CUT

    def gather_a(buf, sem):
        for j in range(CUT):
            rows = pl.ds(j * ROWS, ROWS)
            send(buf.at[0, q, rows], buf.at[0, q, rows], sem + j, px)
            send(buf.at[1, q, rows], buf.at[1, q, rows], sem + CUT + j, py)
        send(buf.at[1, q], buf.at[1, q], sem + 2 * CUT, px)
        send(buf.at[0, q], buf.at[0, q], sem + 2 * CUT + 1, py)

    def gather_b(buf, sem):
        for j in range(CUT):
            rows = pl.ds(j * ROWS, ROWS)
            arrive(buf.at[0, qx, rows], sem + j)
            send(buf.at[0, qx, rows], buf.at[0, qx, rows], sem + 2 * CUT + 2 + j, py)
            arrive(buf.at[1, qy, rows], sem + CUT + j)
            send(buf.at[1, qy, rows], buf.at[1, qy, rows], sem + 3 * CUT + 2 + j, px)

    def gather_c(buf, sem):
        arrive(buf.at[1, qx], sem + 2 * CUT)
        arrive(buf.at[0, qy], sem + 2 * CUT + 1)
        for j in range(CUT):
            rows = pl.ds(j * ROWS, ROWS)
            arrive(buf.at[0, qd, rows], sem + 2 * CUT + 2 + j)
            arrive(buf.at[1, qd, rows], sem + 3 * CUT + 2 + j)

    def scatter_a(buf, rb, sem):
        send(buf.at[0, qd], rb.at[0], sem, px)
        send(buf.at[1, qd], rb.at[1], sem + 1, py)
        send(buf.at[0, qx], rb.at[2], sem + 2, px)
        send(buf.at[1, qy], rb.at[3], sem + 3, py)

    def scatter_b(buf, rb, sem):
        arrive(rb.at[0], sem)
        rb[6] = (buf[0, qy].astype(F32) + rb[0].astype(F32)).astype(BF16)
        send(rb.at[6], rb.at[4], sem + 4, py)
        arrive(rb.at[1], sem + 1)
        rb[7] = (buf[1, qx].astype(F32) + rb[1].astype(F32)).astype(BF16)
        send(rb.at[7], rb.at[5], sem + 5, px)

    def scatter_c(buf, rb, sem):
        for k in range(2, 6):
            arrive(rb.at[k], sem + k)
        first = buf[0, q].astype(F32) + rb[2].astype(F32) + rb[4].astype(F32)
        second = buf[1, q].astype(F32) + rb[3].astype(F32) + rb[5].astype(F32)
        return jnp.concatenate([first, second], axis=0)

    p_n1, p_n2, p_dm, p_da = (take(4 * CUT + 2) for _ in range(4))
    p_a, p_m, p_d2, p_d1 = (take(6) for _ in range(4))

    WAYS = 6
    t_core = [take(1) for _ in range(WAYS)]
    t_line = [take(6) for _ in range(WAYS)]
    t_rank = [take(6) for _ in range(WAYS)]
    t_pass = [take(1) for _ in range(WAYS)]
    stored = [None] * WAYS
    halves = (128, 32, 128, 128, 128, 128)
    grads = (gq.at[0], go, g1, g2, gq.at[1], gq.at[2])
    cores = (cq.at[0], co, c1, c2, cq.at[1], cq.at[2])
    lines = (zq.at[0], zo, z1, z2, zq.at[1], zq.at[2])
    finals = (fq.at[0], fo, f1, f2, fq.at[1], fq.at[2])
    results = (oq.at[0], oo, o1, o2, oq.at[1], oq.at[2])

    def reduce_a(w):
        send(grads[w].at[:, theirs(halves[w])], cores[w], t_core[w], partner)

    def reduce_b(w):
        rows = mine(halves[w])
        arrive(cores[w], t_core[w])

        def step(zz, _):
            grads[w][zz, rows] = (grads[w][zz, rows].astype(F32) + cores[w][zz].astype(F32)).astype(BF16)
            return 0

        lax.fori_loop(0, Z, step, 0)
        for f in range(2):
            send(grads[w].at[far + f, rows], lines[w].at[2 + f], t_line[w] + 2 + f, (replica, mate), when=end, got=middle)
        send(grads[w].at[mate, rows], lines[w].at[0], t_line[w], (replica, mate))

    def reduce_m(w):
        rows = mine(halves[w])
        for f in range(2):

            @pl.when(middle)
            def _(f=f):
                arrive(lines[w].at[2 + f], t_line[w] + 2 + f)
                grads[w][far + f, rows] = (grads[w][far + f, rows].astype(F32) + lines[w][2 + f].astype(F32)).astype(BF16)

            send(grads[w].at[far + f, rows], lines[w].at[1], t_line[w] + 1, (replica, far + f), when=middle, out=t_line[w] + 4 + f)

    def spots(w, rank, core):
        half = halves[w]
        first = pl.multiple_of(core * half, half)
        second = pl.multiple_of(core * half + half // 2, half // 2)
        return (
            results[w].at[rank, pl.ds(first, half // 2)],
            results[w].at[rank, pl.ds(second, half // 2)],
            results[w].at[rank, pl.ds(first, half)],
        )

    def reduce_c(w):
        half = halves[w]
        for k in range(2):
            arrive(lines[w].at[k], t_line[w] + k)
        total = grads[w][z, mine(half)].astype(F32)
        for k in range(2):
            total = total + lines[w][k].astype(F32)
        finals[w][...] = total.astype(BF16)
        one, two, both = spots(w, q, c)
        a, b = finals[w].at[pl.ds(0, half // 2)], finals[w].at[pl.ds(half // 2, half // 2)]
        send(a, one, t_rank[w], px)
        send(b, two, t_rank[w] + 1, py)
        send(b, two, t_rank[w] + 2, px)
        send(a, one, t_rank[w] + 3, py)
        stored[w] = pltpu.make_async_copy(finals[w], both, lsem.at[LOADS + w])
        stored[w].start()

    def reduce_d(w):
        one = spots(w, qx, c)[0]
        arrive(one, t_rank[w])
        send(one, one, t_rank[w] + 4, py)
        two = spots(w, qy, c)[1]
        arrive(two, t_rank[w] + 1)
        send(two, two, t_rank[w] + 5, px)

    def reduce_e(w):
        arrive(spots(w, qx, c)[1], t_rank[w] + 2)
        arrive(spots(w, qy, c)[0], t_rank[w] + 3)
        arrive(spots(w, qd, c)[0], t_rank[w] + 4)
        arrive(spots(w, qd, c)[1], t_rank[w] + 5)
        stored[w].wait()
        part = results[w].at[:, mine(halves[w])]
        send(part, part, t_pass[w], partner)

    def reduce_f(w):
        arrive(results[w].at[:, theirs(halves[w])], t_pass[w])

    for cp in loads[:n_first]:
        cp.wait()
    lane = lax.broadcasted_iota(jnp.int32, (256, 128), 1)
    even = q % 2 == 0
    for t in range(3):
        for m in range(2):
            left = tmp[t * RANKS + 2 * m].astype(F32)
            right = tmp[t * RANKS + 2 * m + 1].astype(F32)
            lo = jnp.where(even, left, pltpu.roll(left, HEAD, 1))
            hi = jnp.where(even, pltpu.roll(right, HEAD, 1), right)
            wq[z, :, t * 256 + m * 128 : t * 256 + m * 128 + 128] = jnp.where(lane < HEAD, lo, hi).astype(BF16)
    line_a(wq, 128, a_q)

    for s in range(SLOTS):
        alive = jnp.where(live[0] > s, 1.0, 0.0).astype(F32)
        cm[s] = (cot[s].astype(F32) * alive).astype(BF16)

    for d in range(1, Z):
        arrive(smg.at[(z - d + Z) % Z], s_small + d - 1)

    def row(i):
        return jnp.concatenate([smg[zz, i : i + 1, :] for zz in range(Z)], axis=1)

    bias_q = smg[0, 12:13, :] + smg[1, 12:13, :] + smg[2, 12:13, :] + smg[3, 12:13, :]
    bias_v = smg[0, 13:14, :] + smg[1, 13:14, :] + smg[2, 13:14, :] + smg[3, 13:14, :]

    exchange_wait(rc, e_clips)
    x = rc[...].astype(F32).reshape(128, 1024)
    xh, _ = normed(x)
    n1[:, q] = (xh * row(0) + row(2)).astype(BF16).reshape(SLOTS, 64, 1024)
    gather_a(n1, p_n1)
    gather_b(n1, p_n1)
    line_b(wq, 128, a_q)
    line_a(wo, 32, a_o)
    exchange(cm, dmt, e_cot, moves)
    gather_c(n1, p_n1)
    line_c(wq, 128, a_q)
    line_b(wo, 32, a_o)
    for cp in loads[n_first:]:
        cp.wait()
    line_a(w1, 128, a_1)
    line_d(wq, 128, a_q)

    def qkv_step(t, _):
        bias = jnp.where(t == 0, bias_q, jnp.where(t == 2, bias_v, 0.0))
        val = mm(n1[...].reshape(512, 1024), wq[:, :, strip(t)].reshape(1024, 256)) + bias
        qkv[t] = val.astype(BF16).reshape(SLOTS, 256, 256)
        return 0

    lax.fori_loop(0, 3, qkv_step, 0)
    line_c(wo, 32, a_o)
    exchange_wait(dmt, e_cot)
    dmb[:, q] = dmt[...]
    gather_a(dmb, p_dm)

    def attend(i, _):
        s = i // 2
        cols = strip(i % 2, 128)
        qq, kk, vv = qkv[0, s, :, cols], qkv[1, s, :, cols], qkv[2, s, :, cols]
        outs = []
        for j in range(2):
            h = slice(j * HEAD, j * HEAD + HEAD)
            score = mm_nt(qq[:, h], kk[:, h]) * SCALE
            e = jnp.exp(score - jnp.max(score, axis=-1, keepdims=True))
            p = e / jnp.sum(e, axis=-1, keepdims=True)
            probs[i, j] = p
            outs.append(mm(p.astype(BF16), vv[:, h]))
        ob[s, :, cols] = jnp.concatenate(outs, axis=1).astype(BF16)
        return 0

    lax.fori_loop(0, 2 * SLOTS, attend, 0)
    line_d(wo, 32, a_o)

    def proj_step(s, _):
        val = mm(ob[s], wo[...].reshape(256, 1024))
        ab[s] = val.astype(BF16).reshape(RANKS, 64, 1024)
        return 0

    lax.fori_loop(0, SLOTS, proj_step, 0)
    scatter_a(ab, ra, p_a)
    gather_b(dmb, p_dm)
    scatter_b(ab, ra, p_a)
    line_b(w1, 128, a_1)
    line_a(w2, 128, a_2)
    a = scatter_c(ab, ra, p_a) + row(6)
    hh = x + a
    h1[...] = hh
    xh2, _ = normed(hh)
    n2[:, q] = (xh2 * row(1) + row(3)).astype(BF16).reshape(SLOTS, 64, 1024)
    gather_a(n2, p_n2)
    gather_b(n2, p_n2)
    line_c(w1, 128, a_1)
    line_b(w2, 128, a_2)
    line_d(w1, 128, a_1)
    gather_c(n2, p_n2)

    def fc1_step(i, _):
        s = i // RANKS
        zz = i % RANKS
        cols = strip(zz)
        u = mm(n2[s].reshape(256, 1024), w1[:, :, cols].reshape(1024, 256)) + smg[zz, pl.ds(8 + q, 1), :]
        cdf = 0.5 * (1.0 + lax.erf(u * (1.0 / math.sqrt(2.0))))
        gb[s, :, cols] = (u * cdf).astype(BF16)
        slope[s, :, cols] = cdf + u * jnp.exp(-0.5 * u * u) * (1.0 / math.sqrt(2.0 * math.pi))
        return 0

    lax.fori_loop(0, SLOTS * RANKS, fc1_step, 0)
    gather_c(dmb, p_dm)

    def dw2_step(zz, _):
        g2[zz] = mm_tn(gb[:, :, strip(zz)].reshape(512, 256), dmb[...].reshape(512, 1024)).astype(BF16)
        return 0

    lax.fori_loop(0, RANKS, dw2_step, 0)
    reduce_a(3)
    line_c(w2, 128, a_2)
    reduce_b(3)
    line_d(w2, 128, a_2)

    def du_step(zz, _):
        cols = strip(zz)
        dg = mm_nt(dmb[...].reshape(512, 1024), w2[zz]).reshape(SLOTS, 256, 256)
        dub[:, :, cols] = (dg * slope[:, :, cols]).astype(BF16)
        return 0

    lax.fori_loop(0, RANKS, du_step, 0)

    def dn2_step(zz, _):
        val = mm_nt(dub[...].reshape(512, 1024), w1[zz])
        d2b[:, :, :, strip(zz)] = val.astype(BF16).reshape(SLOTS, RANKS, 64, 256)
        return 0

    lax.fori_loop(0, RANKS, dn2_step, 0)
    scatter_a(d2b, rd2, p_d2)

    def dw1_step(zz, _):
        g1[zz] = mm_tn(n2[:, :, :, strip(zz)].reshape(512, 256), dub[...].reshape(512, 1024)).astype(BF16)
        return 0

    lax.fori_loop(0, RANKS, dw1_step, 0)
    reduce_a(2)
    scatter_b(d2b, rd2, p_d2)
    reduce_b(2)

    sms[...] = jnp.zeros((16, 1024), F32)

    def own(i, val):
        sms[i : i + 1, :] = jnp.sum(val, axis=0, keepdims=True)

    dy = dmt[...].astype(F32).reshape(128, 1024)
    own(7, dy)
    xh2, inv2 = normed(h1[...])
    dn2 = scatter_c(d2b, rd2, p_d2)
    res = dy + norm_back(dn2 * row(1), xh2, inv2)
    da = res.astype(BF16)
    dab[:, q] = da.reshape(SLOTS, 64, 1024)
    gather_a(dab, p_da)
    reduce_m(3)
    dh1[...] = res
    own(1, dn2 * xh2)
    own(3, dn2)
    own(6, da.astype(F32))
    fc1_sum = jnp.sum(dub[...].astype(F32).reshape(512, 1024), axis=0, keepdims=True)
    sms[pl.ds(9 + 2 * q, 1), :] = fc1_sum

    def m_step(s, _):
        mb[s] = mm(gb[s], w2[...].reshape(1024, 1024)).astype(BF16).reshape(RANKS, 64, 1024)
        return 0

    lax.fori_loop(0, SLOTS, m_step, 0)
    gather_b(dab, p_da)
    scatter_a(mb, rm, p_m)
    gather_c(dab, p_da)
    go[...] = mm_tn(ob[...].reshape(512, 256), dab[...].reshape(512, 1024)).astype(BF16).reshape(Z, HEAD, 1024)
    reduce_a(1)

    def do_step(s, _):
        dob[s] = mm_nt(dab[s].reshape(256, 1024), wo[...].reshape(256, 1024)).astype(BF16)
        return 0

    lax.fori_loop(0, SLOTS, do_step, 0)
    reduce_b(1)

    def attend_back(i, _):
        s = i // 2
        cols = strip(i % 2, 128)
        qq, kk, vv, dd = qkv[0, s, :, cols], qkv[1, s, :, cols], qkv[2, s, :, cols], dob[s, :, cols]
        dqs, dks, dvs = [], [], []
        for j in range(2):
            h = slice(j * HEAD, j * HEAD + HEAD)
            p = probs[i, j]
            dp = mm_nt(dd[:, h], vv[:, h])
            ds = (p * (dp - jnp.sum(p * dp, axis=-1, keepdims=True))).astype(BF16)
            dqs.append(mm(ds, kk[:, h]) * SCALE)
            dks.append(mm_tn(ds, qq[:, h]) * SCALE)
            dvs.append(mm_tn(p.astype(BF16), dd[:, h]))
        dqkv[0, s, :, cols] = jnp.concatenate(dqs, axis=1).astype(BF16)
        dqkv[1, s, :, cols] = jnp.concatenate(dks, axis=1).astype(BF16)
        dqkv[2, s, :, cols] = jnp.concatenate(dvs, axis=1).astype(BF16)
        return 0

    lax.fori_loop(0, SLOTS, attend_back, 0)
    scatter_b(mb, rm, p_m)
    reduce_c(3)
    lax.fori_loop(SLOTS, 2 * SLOTS, attend_back, 0)
    reduce_m(2)

    def dwq_step(zz, _):
        left = n1[:, :, :, strip(zz)].reshape(512, 256)
        for t in range(3):
            gq[t, zz] = mm_tn(left, dqkv[t].reshape(512, 256)).astype(BF16)
        return 0

    lax.fori_loop(0, RANKS, dwq_step, 0)
    for w in (0, 4, 5):
        reduce_a(w)

    def dn1_step(zz, _):
        val = mm_nt(dqkv[0].reshape(512, 256), wq[zz, :, 0:256])
        val = val + mm_nt(dqkv[1].reshape(512, 256), wq[zz, :, 256:512])
        val = val + mm_nt(dqkv[2].reshape(512, 256), wq[zz, :, 512:768])
        d1b[:, :, :, strip(zz)] = val.astype(BF16).reshape(SLOTS, RANKS, 64, 256)
        return 0

    lax.fori_loop(0, RANKS, dn1_step, 0)
    scatter_a(d1b, rd1, p_d1)
    for w in (0, 4, 5):
        reduce_b(w)
    reduce_d(3)
    m = scatter_c(mb, rm, p_m) + row(7)
    outb[...] = (h1[...] + m).astype(BF16).reshape(SLOTS, 64, 1024)
    exchange(outb, outr, e_out, backs)
    scatter_b(d1b, rd1, p_d1)

    dq_sum = jnp.sum(dqkv[0].astype(F32).reshape(512, 256), axis=0, keepdims=True)
    dv_sum = jnp.sum(dqkv[2].astype(F32).reshape(512, 256), axis=0, keepdims=True)
    gap = jnp.zeros((1, 128), F32)
    pieces = []
    for zz in range(Z):
        h = slice(zz * HEAD, zz * HEAD + HEAD)
        pieces += [dq_sum[:, h], dv_sum[:, h], gap]
    sms[pl.ds(8 + 2 * q, 1), :] = jnp.concatenate(pieces, axis=1)
    xh, inv = normed(rc[...].astype(F32).reshape(128, 1024))
    reduce_m(1)
    reduce_m(0)
    reduce_m(4)
    reduce_c(2)

    dn1 = scatter_c(d1b, rd1, p_d1)
    own(0, dn1 * xh)
    own(2, dn1)
    u_core, u_line, u_rank = take(1), take(3), take(3)
    send(sms, smc, u_core, partner)
    cgb[...] = (dh1[...] + norm_back(dn1 * row(0), xh, inv)).astype(BF16).reshape(SLOTS, 64, 1024)
    exchange(cgb, cgr, e_cg, backs)

    arrive(smc, u_core)
    both = sms[...] + smc[...]
    for zz in range(Z):
        smx[0, zz] = both[:, zz * 256 : zz * 256 + 256]
    for d in range(1, Z):
        send(smx.at[0, (z + d) % Z], smz.at[d - 1], u_line + d - 1, (replica, (z + d) % Z))
    reduce_m(5)
    reduce_c(1)
    reduce_c(0)
    reduce_d(2)
    reduce_e(3)
    reduce_c(4)
    reduce_c(5)
    reduce_e(2)
    for d in range(Z - 1):
        arrive(smz.at[d], u_line + d)
    smx[1, 0] = smx[0, z] + smz[0] + smz[1] + smz[2]
    for k, rank in enumerate((qx, qy, qd)):
        send(smx.at[1, 0], smx.at[1, 1 + k], u_rank + k, dev(rank, c, z))
    for w in (1, 0, 4, 5):
        reduce_d(w)
    for w in (1, 0, 4, 5):
        reduce_e(w)
    for k in range(RANKS - 1):
        arrive(smx.at[1, 1 + k], u_rank + k)
    sm_out[...] = smx[1, 0] + smx[1, 1] + smx[1, 2] + smx[1, 3]

    exchange_wait(outr, e_out)
    out_k[...] = outr[...].reshape(128, 1024)
    exchange_wait(cgr, e_cg)
    cg_k[...] = cgr[...].reshape(128, 1024)
    for w in (3, 2, 1, 0, 4, 5):
        reduce_f(w)
    assert counter[0] <= SEMS, counter[0]
    for finish in pending:
        finish()


def finish_kernel(
    live, out_k, cg_k, oq, oo, o1, o2, sm,
    out, cg, dwq, dwo, dw1, dw2, dgain, dnbias, dpbias, dfbias,
    b_out, b_cg, bq, bo, b1, b2, f_out, f_cg, fq, fo, f1, f2, isem, osem,
):
    ins, outs = [], []

    def fetch(src, dst):
        cp = pltpu.make_async_copy(src, dst, isem.at[len(ins)])
        cp.start()
        ins.append(cp)

    def store(src, dst):
        cp = pltpu.make_async_copy(src, dst, osem.at[len(outs)])
        cp.start()
        outs.append(cp)

    for h in range(2):
        fetch(o2.at[pl.ds(2 * h, 2)], b2.at[pl.ds(2 * h, 2)])
    for h in range(2):
        fetch(o1.at[:, pl.ds(128 * h, 128)], b1.at[:, pl.ds(128 * h, 128)])
    for h in range(2):
        fetch(oq.at[:, :, pl.ds(128 * h, 128)], bq.at[:, :, pl.ds(128 * h, 128)])
    fetch(oo, bo)
    fetch(cg_k, b_cg)
    fetch(out_k, b_out)

    dgain[...] = sm[0:2]
    dnbias[...] = sm[2:4]
    lane = lax.broadcasted_iota(jnp.int32, (1, 128), 1)
    rows = [sm[8 + 2 * k : 9 + 2 * k, 0:128] for k in range(RANKS)]
    turn = [pltpu.roll(r, HEAD, 1) for r in rows]
    for g in range(2):
        a, b = 2 * g, 2 * g + 1
        dpbias[0:1, g * 128 : g * 128 + 128] = jnp.where(lane < HEAD, rows[a], turn[b])
        dpbias[1:2, g * 128 : g * 128 + 128] = jnp.where(lane < HEAD, turn[a], rows[b])
    dpbias[2:4] = sm[6:8]
    for k in range(RANKS):
        dfbias[pl.ds(k * 256, 256)] = sm[9 + 2 * k : 10 + 2 * k, :].reshape(256)

    for h in range(2):
        ins[h].wait()

        def two(i, _, h=h):
            f2[pl.ds(512 * h + 64 * i, 64), :] = b2[2 * h + i // 4, strip(i % 4, 64), :].astype(F32)
            return 0

        lax.fori_loop(0, 8, two, 0)
        store(f2.at[pl.ds(512 * h, 512)], dw2.at[pl.ds(512 * h, 512)])
    for h in range(2):
        ins[2 + h].wait()

        def one(i, _, h=h):
            at = pl.ds(pl.multiple_of(128 * h + 16 * i, 16), 16)
            for k in range(RANKS):
                for zz in range(RANKS):
                    f1[at, zz * 1024 + k * 256 : zz * 1024 + k * 256 + 256] = b1[k, at, zz * 256 : zz * 256 + 256].astype(F32)
            return 0

        lax.fori_loop(0, 8, one, 0)
        store(f1.at[pl.ds(128 * h, 128)], dw1.at[pl.ds(128 * h, 128)])
    lane = lax.broadcasted_iota(jnp.int32, (16, 128), 1)
    for h in range(2):
        ins[4 + h].wait()

        def attn(i, _, h=h):
            at = pl.ds(pl.multiple_of(128 * h + 16 * i, 16), 16)
            for t in range(3):
                for m in range(2):
                    part = [bq[t, k, at, m * 128 : m * 128 + 128].astype(F32) for k in range(RANKS)]
                    turn = [pltpu.roll(p, HEAD, 1) for p in part]
                    col = t * 1024 + m * 512
                    for g in range(2):
                        a, b = 2 * g, 2 * g + 1
                        fq[at, col + g * 128 : col + g * 128 + 128] = jnp.where(lane < HEAD, part[a], turn[b])
                        fq[at, col + 256 + g * 128 : col + 384 + g * 128] = jnp.where(lane < HEAD, turn[a], part[b])
            return 0

        lax.fori_loop(0, 8, attn, 0)
        store(fq.at[pl.ds(128 * h, 128)], dwq.at[pl.ds(128 * h, 128)])
    ins[6].wait()
    fo[...] = bo[...].astype(F32).reshape(256, 1024)
    store(fo, dwo)
    ins[7].wait()
    f_cg[...] = b_cg[...].astype(F32)
    store(f_cg, cg)
    ins[8].wait()
    for s in range(SLOTS):
        alive = jnp.where(live[0] > s, 1.0, 0.0).astype(F32)
        f_out[s * 64 : s * 64 + 64] = (b_out[s * 64 : s * 64 + 64].astype(F32) * alive).astype(BF16)
    store(f_out, out)
    for cp in outs:
        cp.wait()


def local(
    n_replica,
    clips, cotangent, live_count, w_qkv, w_out, w_fc1, w_fc2, norm_gain, norm_bias, proj_bias, fc1_bias,
):
    vm = pl.BlockSpec(memory_space=pltpu.VMEM)
    smem = pl.BlockSpec(memory_space=pltpu.SMEM)
    anyspace = pl.BlockSpec(memory_space=pl.ANY)
    shape = jax.ShapeDtypeStruct
    tile = (SLOTS, 64, 1024)
    group = (SLOTS, RANKS, 64, 1024)
    V = pltpu.VMEM
    scratch = [
        V(tile, BF16), V(tile, BF16), V(tile, BF16), V((16, 256), F32), V((4, 16, 256), F32), V((12, 256, 128), BF16),
        V((4, 256, 768), BF16), V((4, 64, 1024), BF16), V((4, 256, 1024), BF16), V((4, 256, 1024), BF16),
        V(group, BF16), V(group, BF16), V(group, BF16), V(group, BF16),
        V((3, SLOTS, 256, 256), BF16), V((4, 2, 256, 256), F32), V((SLOTS, 256, 256), BF16),
        V(group, BF16), V(group, BF16), V(group, BF16), V(group, BF16),
        V((8, 64, 1024), BF16), V((8, 64, 1024), BF16), V((8, 64, 1024), BF16), V((8, 64, 1024), BF16),
        V((128, 1024), F32), V((128, 1024), F32), V((SLOTS, 256, 1024), F32), V((SLOTS, 256, 1024), BF16),
        V((SLOTS, 256, 1024), BF16), V((SLOTS, 256, 256), BF16), V((3, SLOTS, 256, 256), BF16),
        V((3, 4, 256, 256), BF16), V((4, 64, 1024), BF16), V((4, 256, 1024), BF16), V((4, 256, 1024), BF16),
        V((3, 4, 128, 256), BF16), V((4, 32, 1024), BF16), V((4, 128, 1024), BF16), V((4, 128, 1024), BF16),
        V((3, 4, 128, 256), BF16), V((4, 32, 1024), BF16), V((4, 128, 1024), BF16), V((4, 128, 1024), BF16),
        V((3, 128, 256), BF16), V((32, 1024), BF16), V((128, 1024), BF16), V((128, 1024), BF16),
        V(tile, BF16), V(tile, BF16), V((16, 1024), F32), V((16, 1024), F32), V((3, 16, 256), F32), V((2, 4, 16, 256), F32),
        V(tile, BF16), V(tile, BF16),
        pltpu.SemaphoreType.DMA((SEMS,)), pltpu.SemaphoreType.DMA((SEMS,)), pltpu.SemaphoreType.DMA((LOADS + 6,)),
    ]
    parts = pl.pallas_call(
        kernel,
        out_shape=(
            shape((128, 1024), BF16), shape((128, 1024), BF16), shape((3, 4, 256, 256), BF16), shape((4, 64, 1024), BF16),
            shape((4, 256, 1024), BF16), shape((4, 256, 1024), BF16), shape((16, 256), F32),
        ),
        in_specs=[vm, vm, smem, vm, vm, vm, vm, anyspace, anyspace, anyspace, anyspace],
        out_specs=(vm, vm, anyspace, anyspace, anyspace, anyspace, vm),
        scratch_shapes=scratch,
        compiler_params=pltpu.CompilerParams(
            collective_id=0, has_side_effects=True, vmem_limit_bytes=60 * 2**20
        ),
        cost_estimate=pl.CostEstimate(flops=10**10, bytes_accessed=2**25, transcendentals=2**21),
    )(clips, cotangent, live_count, norm_gain, norm_bias, proj_bias, fc1_bias, w_qkv, w_out, w_fc1, w_fc2)

    out, clips_grad, *summed = pl.pallas_call(
        finish_kernel,
        out_shape=(
            shape((128, 1024), BF16), shape((128, 1024), F32), shape((256, 3072), F32), shape((256, 1024), F32),
            shape((256, 4096), F32), shape((1024, 1024), F32), shape((2, 256), F32), shape((2, 256), F32),
            shape((4, 256), F32), shape((1024,), F32),
        ),
        in_specs=[smem] + [anyspace] * 6 + [vm],
        out_specs=[anyspace] * 6 + [vm] * 4,
        scratch_shapes=[
            V((128, 1024), BF16), V((128, 1024), BF16), V((3, 4, 256, 256), BF16), V((4, 64, 1024), BF16),
            V((4, 256, 1024), BF16), V((4, 256, 1024), BF16), V((128, 1024), BF16), V((128, 1024), F32),
            V((256, 3072), F32), V((256, 1024), F32), V((256, 4096), F32), V((1024, 1024), F32),
            pltpu.SemaphoreType.DMA((9,)), pltpu.SemaphoreType.DMA((9,)),
        ],
        compiler_params=pltpu.CompilerParams(vmem_limit_bytes=60 * 2**20),
        cost_estimate=pl.CostEstimate(flops=2**22, bytes_accessed=20 * 2**20, transcendentals=0),
    )(live_count, *parts)
    if n_replica > PLANE:
        groups = [list(range(i, n_replica, PLANE)) for i in range(PLANE)]
        summed = lax.psum(tuple(summed), "replica", axis_index_groups=groups)
    return (out.reshape(tile), clips_grad.reshape(tile)) + tuple(summed)


def solution(mesh):
    in_specs = (
        P("replica", "shard", None),
        P("replica", "shard", None),
        P("replica"),
        P("shard", None),
        P("shard", None),
        P("shard", None),
        P("shard", None),
        P(None, "shard"),
        P(None, "shard"),
        P(None, "shard"),
        P("shard"),
    )
    out_specs = (
        P("replica", "shard", None),
        P("replica", "shard", None),
        P("shard", None),
        P("shard", None),
        P("shard", None),
        P("shard", None),
        P(None, "shard"),
        P(None, "shard"),
        P(None, "shard"),
        P("shard"),
    )
    body = functools.partial(local, mesh.shape["replica"])
    return jax.shard_map(body, mesh=mesh, in_specs=in_specs, out_specs=out_specs, check_vma=False)
```

```python
import functools
import math

import jax
import jax.numpy as jnp
from jax import lax
from jax.experimental import pallas as pl
from jax.experimental.pallas import tpu as pltpu
from jax.sharding import PartitionSpec as P

MESH = pl.DeviceIdType.MESH
F32 = jnp.float32
BF16 = jnp.bfloat16
HEAD = 64
PLANE = 8
RANKS = 4
SLOTS = 2
ARRIVALS = 116
SENDS = 56
LOADS = 18
SCALE = 1.0 / math.sqrt(HEAD)


def mm(a, b):
    return jnp.dot(a, b, preferred_element_type=F32)


def mm_nt(a, b):
    return lax.dot_general(a, b, (((1,), (1,)), ((), ())), preferred_element_type=F32)


def mm_tn(a, b):
    return lax.dot_general(a, b, (((0,), (0,)), ((), ())), preferred_element_type=F32)


def normed(v):
    centre = v - jnp.mean(v, axis=-1, keepdims=True)
    spread = jnp.mean(centre * centre, axis=-1, keepdims=True)
    inverse = lax.rsqrt(spread + 1e-6)
    return centre * inverse, inverse


def norm_back(e, xh, inverse):
    first = jnp.mean(e, axis=-1, keepdims=True)
    second = jnp.mean(e * xh, axis=-1, keepdims=True)
    return inverse * (e - first - xh * second)


def strip(i, width=256):
    return pl.ds(pl.multiple_of(i * width, width), width)


def kernel(
    clips, cot, live, gains, nbias, pbias, fbias, w_qkv, w_out, w_fc1, w_fc2,
    out_k, cg_k, oq, oo, o1, o2, sm_out,
    rc, cm, dmt, sml, smg, tmp, wq, wo, w1, w2,
    n1, n2, dmb, dab, qkv, probs, ob, ab, mb, d2b, d1b, ra, rm, rd2, rd1,
    h1, dh1, slope, gb, dub, dob, dqkv, gq, go, g1, g2,
    cq, co, c1, c2, zq, zo, z1, z2, fq, fo, f1, f2,
    outb, cgb, sms, smc, smz, smx, outr, cgr, total2,
    ssem, rsem, lsem,
):
    Z = 4
    replica = lax.axis_index("replica")
    z = lax.axis_index("shard")
    r8 = replica % PLANE
    base = replica - r8
    q = r8 // 2
    c = r8 % 2
    qx = (q // 2) * 2 + (1 - q % 2)
    qy = (1 - q // 2) * 2 + q % 2
    qd = 3 - q
    lower = z // 2
    mate = 2 * lower + 1 - z % 2
    far_middle = 2 - lower
    far = 2 * (1 - lower)
    middle = jnp.logical_or(z == 1, z == 2)
    end = jnp.logical_not(middle)

    def dev(rank, core, plane):
        return (base + 2 * rank + core, plane)

    px, py, partner = dev(qx, c, z), dev(qy, c, z), dev(q, 1 - c, z)

    counter = [0, 0]

    def take(n):
        counter[0] += n
        return counter[0] - n

    pending = []

    def track(ref, when=None):
        counter[1] += 1
        sem = counter[1] - 1

        def finish():
            pltpu.make_async_remote_copy(
                ref, ref, ssem.at[sem], rsem.at[0], device_id=partner, device_id_type=MESH
            ).wait_send()

        pending.append(finish if when is None else lambda: pl.when(when)(finish))
        return sem

    def send(src, dst, sem, device, out, when=None, got=None):
        def start():
            pltpu.make_async_remote_copy(
                src, dst, ssem.at[out], rsem.at[sem], device_id=device, device_id_type=MESH
            ).start()

        if when is None:
            start()
        else:
            pl.when(when)(start)

    def arrive(dst, sem):
        pltpu.make_async_remote_copy(
            dst, dst, ssem.at[sem], rsem.at[sem], device_id=partner, device_id_type=MESH
        ).wait_recv()

    def flip(a, b):
        return (a // 2 + b // 2) % 2 * 2 + (a + b) % 2

    def target(s):
        plane = (q + 2 * s + c) % RANKS
        return flip(q, (z + plane) % RANKS), plane

    def origin(s):
        a = (z - 2 * s - c + 2 * RANKS) % RANKS
        return a, (flip(q, a) - z + RANKS) % RANKS

    moves = [target(s) for s in range(SLOTS)]
    backs = [origin(s) for s in range(SLOTS)]

    def stays(place):
        return jnp.logical_and(place[0] == q, place[1] == z)

    loads = []

    def load(src, dst):
        cp = pltpu.make_async_copy(src, dst, lsem.at[len(loads)])
        cp.start()
        loads.append(cp)

    pair = (q // 2) * 128
    for t in range(3):
        for zz in range(RANKS):
            load(w_qkv.at[:, pl.ds(pl.multiple_of(t * 1024 + zz * 256 + pair, 128), 128)], tmp.at[t * RANKS + zz])
    load(w_out.at[strip(q, HEAD), :], wo.at[z])

    barrier = pltpu.get_barrier_semaphore()
    for device in (px, py, dev(qd, c, z), partner):
        pl.semaphore_signal(barrier, inc=1, device_id=device, device_id_type=MESH)
    for d in range(1, Z):
        pl.semaphore_signal(barrier, inc=1, device_id=(replica, (z + d) % Z), device_id_type=MESH)
    count = 4 + Z - 1
    for place in moves + backs:

        @pl.when(jnp.logical_not(stays(place)))
        def _(place=place):
            pl.semaphore_signal(barrier, inc=1, device_id=dev(place[0], c, place[1]), device_id_type=MESH)

        count = count + jnp.where(stays(place), 0, 1)

    sml[...] = jnp.zeros((16, 256), F32)
    sml[0:2] = gains[...].astype(F32)
    sml[2:4] = nbias[...].astype(F32)
    sml[4:8] = pbias[...].astype(F32)
    for k in range(RANKS):
        sml[8 + k : 9 + k] = fbias[pl.ds(k * 256, 256)].astype(F32).reshape(1, 256)
    lane = lax.broadcasted_iota(jnp.int32, (8, 256), 1)
    turned = pltpu.roll(sml[0:8], (z * HEAD - q * HEAD + 256) % 256, 1)
    kept = jnp.where(jnp.logical_and(lane >= z * HEAD, lane < z * HEAD + HEAD), turned, 0.0)
    sml[12:14] = kept[4:6]

    pl.semaphore_wait(barrier, count)

    def exchange(src, dst, sem, places):
        for s in range(SLOTS):
            to = dev(places[s][0], c, places[s][1])
            leaves = jnp.logical_not(stays(places[s]))
            send(src.at[s], dst.at[s], sem + s, to, track(src.at[s], leaves), when=leaves)

            @pl.when(stays(places[s]))
            def _(s=s):
                pltpu.make_async_copy(src.at[s], dst.at[s], rsem.at[sem + s]).start()

    def exchange_wait(dst, sem):
        for s in range(SLOTS):
            arrive(dst.at[s], sem + s)

    e_clips, e_cot, e_out, e_cg = take(2), take(2), take(2), take(2)
    exchange(clips, rc, e_clips, moves)
    s_small, o_small = take(1), track(smg.at[pl.ds(0, 3)])
    smg[z] = sml[...]
    for d in range(1, Z):
        send(sml, smg.at[z], s_small, (replica, (z + d) % Z), o_small)
    n_first = len(loads)
    for zz in range(RANKS):
        load(w_fc1.at[:, pl.ds(pl.multiple_of(zz * 1024 + q * 256, 256), 256)], w1.at[z, :, pl.ds(zz * 256, 256)])
    load(w_fc2.at[strip(q), :], w2.at[z])

    def mine(half):
        return pl.ds(pl.multiple_of(c * half, half), half)

    def theirs(half):
        return pl.ds(pl.multiple_of((1 - c) * half, half), half)

    def line(w, half):
        rows = pl.ds(0, half)
        return w, half, take(6), (track(w.at[pl.ds(0, 2), rows]), track(w.at[pl.ds(0, 2), rows], middle), track(w.at[pl.ds(0, 3), rows]))

    def line_a(way):
        w, half, sem, outs = way
        own_part = w.at[z, mine(half)]
        send(own_part, own_part, sem, (replica, mate), outs[0])
        send(own_part, own_part, sem + 1 + z % 2, (replica, far_middle), outs[0])

    def share(way, zz, when=None):
        w, half, sem, outs = way
        part = w.at[zz, mine(half)]
        send(part, part, sem + 2 + (zz - z + Z) % Z, partner, outs[2], when=when)

    def line_b(way):
        w, half, sem, outs = way
        for f in (lower, 1 - lower):

            @pl.when(middle)
            def _(f=f):
                arrive(w.at[far + f, mine(half)], sem + 1 + f)

            part = w.at[far + f, mine(half)]
            send(part, part, sem + 1 + f, (replica, mate), outs[1], when=middle)
            share(way, far + f, when=middle)

    def line_c(way):
        w, half, sem, outs = way
        arrive(w.at[mate, mine(half)], sem)
        share(way, mate)
        for f in (lower, 1 - lower):

            @pl.when(end)
            def _(f=f):
                arrive(w.at[far + f, mine(half)], sem + 1 + f)

            share(way, far + f, when=end)

    order = (z, mate, far + lower, far + 1 - lower)

    def line_d(way, k):
        w, half, sem, outs = way
        arrive(w.at[order[k], theirs(half)], sem + 2 + (order[k] - z + Z) % Z)

    way_q, way_o, way_1, way_2 = line(wq, 128), line(wo, 32), line(w1, 128), line(w2, 128)

    CUT = 2
    ROWS = 64 // CUT

    def gather(buf):
        return buf, take(2 * CUT + 1), track(buf.at[:, pl.ds(0, 3)])

    def gather_a(way):
        buf, sem, out = way
        for j in range(CUT):
            rows = pl.ds(j * ROWS, ROWS)
            send(buf.at[0, q, rows], buf.at[0, q, rows], sem + j, px, out)
            send(buf.at[1, q, rows], buf.at[1, q, rows], sem + CUT + j, py, out)
        send(buf.at[1, q], buf.at[1, q], sem + 2 * CUT, px, out)
        send(buf.at[0, q], buf.at[0, q], sem + 2 * CUT, py, out)

    def gather_b(way):
        buf, sem, out = way
        for j in range(CUT):
            rows = pl.ds(j * ROWS, ROWS)
            arrive(buf.at[0, qx, rows], sem + j)
            send(buf.at[0, qx, rows], buf.at[0, qx, rows], sem + 2 * CUT, py, out)
            arrive(buf.at[1, qy, rows], sem + CUT + j)
            send(buf.at[1, qy, rows], buf.at[1, qy, rows], sem + 2 * CUT, px, out)

    def gather_c(way):
        buf, sem, out = way
        arrive(buf.at[0], sem + 2 * CUT)

    def scatter(buf, rb):
        return buf, rb, take(3), track(rb.at[pl.ds(0, 6)])

    def scatter_a(way):
        buf, rb, sem, out = way
        send(buf.at[0, qd], rb.at[0], sem, px, out)
        send(buf.at[1, qd], rb.at[1], sem + 1, py, out)
        send(buf.at[0, qx], rb.at[2], sem + 2, px, out)
        send(buf.at[1, qy], rb.at[3], sem + 2, py, out)

    def scatter_b(way):
        buf, rb, sem, out = way
        arrive(rb.at[0], sem)
        rb[6] = (buf[0, qy].astype(F32) + rb[0].astype(F32)).astype(BF16)
        send(rb.at[6], rb.at[4], sem + 2, py, out)
        arrive(rb.at[1], sem + 1)
        rb[7] = (buf[1, qx].astype(F32) + rb[1].astype(F32)).astype(BF16)
        send(rb.at[7], rb.at[5], sem + 2, px, out)

    def scatter_c(way):
        buf, rb, sem, out = way
        arrive(rb.at[pl.ds(2, 4)], sem + 2)
        first = buf[0, q].astype(F32) + rb[2].astype(F32) + rb[4].astype(F32)
        second = buf[1, q].astype(F32) + rb[3].astype(F32) + rb[5].astype(F32)
        return jnp.concatenate([first, second], axis=0)

    p_n1, p_n2, p_dm, p_da = (gather(buf) for buf in (n1, n2, dmb, dab))
    p_a, p_m, p_d2, p_d1 = scatter(ab, ra), scatter(mb, rm), scatter(d2b, rd2), scatter(d1b, rd1)

    WAYS = 6
    halves = (128, 32, 128, 128, 128, 128)
    grads = (gq.at[0], go, g1, g2, gq.at[1], gq.at[2])
    cores = (cq.at[0], co, c1, c2, cq.at[1], cq.at[2])
    lines = (zq.at[0], zo, z1, z2, zq.at[1], zq.at[2])
    finals = (fq.at[0], fo, f1, f2, fq.at[1], fq.at[2])
    results = (oq.at[0], oo, o1, o2, oq.at[1], oq.at[2])
    t_core = [take(1) for _ in range(WAYS)]
    t_line = [take(3) for _ in range(WAYS)]
    t_rank = [take(3) for _ in range(WAYS)]
    t_pass = [take(1) for _ in range(WAYS)]
    stored = [None] * WAYS
    q_core = [track(cores[w]) for w in range(WAYS)]
    q_line = [track(lines[w].at[pl.ds(0, 3)]) for w in range(WAYS)]
    q_rank = [track(lines[w].at[pl.ds(0, 3)]) for w in range(WAYS)]
    q_pass = [track(cores[w]) for w in range(WAYS)]

    def reduce_a(w):
        send(grads[w].at[:, theirs(halves[w])], cores[w], t_core[w], partner, q_core[w])

    reach = (1 - lower, lower)

    def reduce_b(w):
        rows = mine(halves[w])
        arrive(cores[w], t_core[w])

        def step(zz, _):
            grads[w][zz, rows] = (grads[w][zz, rows].astype(F32) + cores[w][zz].astype(F32)).astype(BF16)
            return 0

        lax.fori_loop(0, Z, step, 0)
        for f in reach:
            send(
                grads[w].at[far + f, rows], lines[w].at[2 + f], t_line[w] + 1 + f, (replica, mate), q_line[w],
                when=end, got=middle,
            )
        send(grads[w].at[mate, rows], lines[w].at[0], t_line[w], (replica, mate), q_line[w])

    def reduce_m(w, k):
        rows = mine(halves[w])
        f = reach[k]

        @pl.when(middle)
        def _():
            arrive(lines[w].at[2 + f], t_line[w] + 1 + f)
            grads[w][far + f, rows] = (grads[w][far + f, rows].astype(F32) + lines[w][2 + f].astype(F32)).astype(BF16)

        send(grads[w].at[far + f, rows], lines[w].at[1], t_line[w], (replica, far + f), q_line[w], when=middle)

    def spots(w, rank, core):
        half = halves[w]
        first = pl.multiple_of(core * half, half)
        second = pl.multiple_of(core * half + half // 2, half // 2)
        return (
            results[w].at[rank, pl.ds(first, half // 2)],
            results[w].at[rank, pl.ds(second, half // 2)],
            results[w].at[rank, pl.ds(first, half)],
        )

    def reduce_c(w):
        half = halves[w]
        arrive(lines[w].at[pl.ds(0, 2)], t_line[w])
        total = grads[w][z, mine(half)].astype(F32)
        for k in range(2):
            total = total + lines[w][k].astype(F32)
        finals[w][...] = total.astype(BF16)
        one, two, both = spots(w, q, c)
        a, b = finals[w].at[pl.ds(0, half // 2)], finals[w].at[pl.ds(half // 2, half // 2)]
        send(a, one, t_rank[w], px, q_rank[w])
        send(b, two, t_rank[w] + 1, py, q_rank[w])
        send(b, two, t_rank[w] + 2, px, q_rank[w])
        send(a, one, t_rank[w] + 2, py, q_rank[w])
        stored[w] = pltpu.make_async_copy(finals[w], both, lsem.at[LOADS + w])
        stored[w].start()

    def reduce_d(w):
        one = spots(w, qx, c)[0]
        arrive(one, t_rank[w])
        send(one, one, t_rank[w] + 2, py, q_rank[w])
        two = spots(w, qy, c)[1]
        arrive(two, t_rank[w] + 1)
        send(two, two, t_rank[w] + 2, px, q_rank[w])

    def reduce_e(w):
        arrive(results[w].at[pl.ds(0, 2), mine(halves[w])], t_rank[w] + 2)
        stored[w].wait()
        part = results[w].at[:, mine(halves[w])]
        send(part, part, t_pass[w], partner, q_pass[w])

    def reduce_f(w):
        arrive(results[w].at[:, theirs(halves[w])], t_pass[w])

    for cp in loads[:n_first]:
        cp.wait()
    lane = lax.broadcasted_iota(jnp.int32, (256, 128), 1)
    even = q % 2 == 0
    for t in range(3):
        for m in range(2):
            left = tmp[t * RANKS + 2 * m].astype(F32)
            right = tmp[t * RANKS + 2 * m + 1].astype(F32)
            lo = jnp.where(even, left, pltpu.roll(left, HEAD, 1))
            hi = jnp.where(even, pltpu.roll(right, HEAD, 1), right)
            wq[z, :, t * 256 + m * 128 : t * 256 + m * 128 + 128] = jnp.where(lane < HEAD, lo, hi).astype(BF16)
    line_a(way_q)

    for s in range(SLOTS):
        alive = jnp.where(live[0] > s, 1.0, 0.0).astype(F32)
        cm[s] = (cot[s].astype(F32) * alive).astype(BF16)

    arrive(smg.at[pl.ds(0, 3)], s_small)

    def row(i):
        return jnp.concatenate([smg[zz, i : i + 1, :] for zz in range(Z)], axis=1)

    bias_q = smg[0, 12:13, :] + smg[1, 12:13, :] + smg[2, 12:13, :] + smg[3, 12:13, :]
    bias_v = smg[0, 13:14, :] + smg[1, 13:14, :] + smg[2, 13:14, :] + smg[3, 13:14, :]

    exchange_wait(rc, e_clips)
    x = rc[...].astype(F32).reshape(128, 1024)
    xh, _ = normed(x)
    n1[:, q] = (xh * row(0) + row(2)).astype(BF16).reshape(SLOTS, 64, 1024)
    gather_a(p_n1)
    gather_b(p_n1)
    line_b(way_q)
    line_a(way_o)
    exchange(cm, dmt, e_cot, moves)
    gather_c(p_n1)
    line_c(way_q)
    line_b(way_o)
    for cp in loads[n_first:]:
        cp.wait()
    line_a(way_1)
    for k in range(1, Z):
        line_d(way_q, k)

    def qkv_step(t, _):
        bias = jnp.where(t == 0, bias_q, jnp.where(t == 2, bias_v, 0.0))
        val = mm(n1[...].reshape(512, 1024), wq[:, :, strip(t)].reshape(1024, 256)) + bias
        qkv[t] = val.astype(BF16).reshape(SLOTS, 256, 256)
        return 0

    lax.fori_loop(0, 3, qkv_step, 0)
    line_c(way_o)
    exchange_wait(dmt, e_cot)
    dmb[:, q] = dmt[...]
    gather_a(p_dm)

    def attend(i, _):
        s = i // 2
        cols = strip(i % 2, 128)
        qq, kk, vv = qkv[0, s, :, cols], qkv[1, s, :, cols], qkv[2, s, :, cols]
        outs = []
        for j in range(2):
            h = slice(j * HEAD, j * HEAD + HEAD)
            score = mm_nt(qq[:, h], kk[:, h]) * SCALE
            e = jnp.exp(score - jnp.max(score, axis=-1, keepdims=True))
            p = e / jnp.sum(e, axis=-1, keepdims=True)
            probs[i, j] = p
            outs.append(mm(p.astype(BF16), vv[:, h]))
        ob[s, :, cols] = jnp.concatenate(outs, axis=1).astype(BF16)
        return 0

    lax.fori_loop(0, 2 * SLOTS, attend, 0)
    for k in range(1, Z):
        line_d(way_o, k)

    def proj_step(s, _):
        val = mm(ob[s], wo[...].reshape(256, 1024))
        ab[s] = val.astype(BF16).reshape(RANKS, 64, 1024)
        return 0

    lax.fori_loop(0, SLOTS, proj_step, 0)
    scatter_a(p_a)
    gather_b(p_dm)
    scatter_b(p_a)
    line_b(way_1)
    line_a(way_2)
    a = scatter_c(p_a) + row(6)
    hh = x + a
    h1[...] = hh
    xh2, _ = normed(hh)
    n2[:, q] = (xh2 * row(1) + row(3)).astype(BF16).reshape(SLOTS, 64, 1024)
    gather_a(p_n2)
    gather_b(p_n2)
    line_c(way_1)
    line_b(way_2)
    for k in range(1, Z):
        line_d(way_1, k)
    gather_c(p_n2)

    def fc1_step(i, _):
        s = i // RANKS
        zz = i % RANKS
        cols = strip(zz)
        u = mm(n2[s].reshape(256, 1024), w1[:, :, cols].reshape(1024, 256)) + smg[zz, pl.ds(8 + q, 1), :]
        cdf = 0.5 * (1.0 + lax.erf(u * (1.0 / math.sqrt(2.0))))
        gb[s, :, cols] = (u * cdf).astype(BF16)
        slope[s, :, cols] = cdf + u * jnp.exp(-0.5 * u * u) * (1.0 / math.sqrt(2.0 * math.pi))
        return 0

    lax.fori_loop(0, SLOTS * RANKS, fc1_step, 0)
    gather_c(p_dm)

    def dw2_step(zz, _):
        g2[zz] = mm_tn(gb[:, :, strip(zz)].reshape(512, 256), dmb[...].reshape(512, 1024)).astype(BF16)
        return 0

    lax.fori_loop(0, RANKS, dw2_step, 0)
    reduce_a(3)
    line_c(way_2)
    reduce_b(3)

    for k in range(RANKS):
        zz = order[k]
        if k > 0:
            line_d(way_2, k)
        cols = strip(zz)
        dg = mm_nt(dmb[...].reshape(512, 1024), w2[zz]).reshape(SLOTS, 256, 256)
        du = (dg * slope[:, :, cols]).astype(BF16)
        dub[:, :, cols] = du

        def dn2_step(i, _, k=k, cols=cols):
            part = mm_nt(dub[:, :, cols].reshape(512, 256), w1[i, :, cols])
            if k > 0:
                part = part + total2[i]
            if k < RANKS - 1:
                total2[i] = part
            else:
                d2b[:, :, :, strip(i)] = part.astype(BF16).reshape(SLOTS, RANKS, 64, 256)
            return 0

        lax.fori_loop(0, RANKS, dn2_step, 0)
    scatter_a(p_d2)

    def dw1_step(zz, _):
        g1[zz] = mm_tn(n2[:, :, :, strip(zz)].reshape(512, 256), dub[...].reshape(512, 1024)).astype(BF16)
        return 0

    lax.fori_loop(0, RANKS, dw1_step, 0)
    reduce_a(2)
    scatter_b(p_d2)
    reduce_b(2)

    sms[...] = jnp.zeros((16, 1024), F32)

    def own(i, val):
        sms[i : i + 1, :] = jnp.sum(val, axis=0, keepdims=True)

    dy = dmt[...].astype(F32).reshape(128, 1024)
    own(7, dy)
    xh2, inv2 = normed(h1[...])
    dn2 = scatter_c(p_d2)
    res = dy + norm_back(dn2 * row(1), xh2, inv2)
    da = res.astype(BF16)
    dab[:, q] = da.reshape(SLOTS, 64, 1024)
    gather_a(p_da)
    for k in range(2):
        reduce_m(3, k)
    dh1[...] = res
    own(1, dn2 * xh2)
    own(3, dn2)
    own(6, da.astype(F32))
    fc1_sum = jnp.sum(dub[...].astype(F32).reshape(512, 1024), axis=0, keepdims=True)
    sms[pl.ds(9 + 2 * q, 1), :] = fc1_sum

    def m_step(s, _):
        mb[s] = mm(gb[s], w2[...].reshape(1024, 1024)).astype(BF16).reshape(RANKS, 64, 1024)
        return 0

    lax.fori_loop(0, SLOTS, m_step, 0)
    gather_b(p_da)
    scatter_a(p_m)
    gather_c(p_da)
    go[...] = mm_tn(ob[...].reshape(512, 256), dab[...].reshape(512, 1024)).astype(BF16).reshape(Z, HEAD, 1024)
    reduce_a(1)

    def do_step(s, _):
        dob[s] = mm_nt(dab[s].reshape(256, 1024), wo[...].reshape(256, 1024)).astype(BF16)
        return 0

    lax.fori_loop(0, SLOTS, do_step, 0)
    reduce_b(1)

    def attend_back(i, _):
        s = i // 2
        cols = strip(i % 2, 128)
        qq, kk, vv, dd = qkv[0, s, :, cols], qkv[1, s, :, cols], qkv[2, s, :, cols], dob[s, :, cols]
        dqs, dks, dvs = [], [], []
        for j in range(2):
            h = slice(j * HEAD, j * HEAD + HEAD)
            p = probs[i, j]
            dp = mm_nt(dd[:, h], vv[:, h])
            ds = (p * (dp - jnp.sum(p * dp, axis=-1, keepdims=True))).astype(BF16)
            dqs.append(mm(ds, kk[:, h]) * SCALE)
            dks.append(mm_tn(ds, qq[:, h]) * SCALE)
            dvs.append(mm_tn(p.astype(BF16), dd[:, h]))
        dqkv[0, s, :, cols] = jnp.concatenate(dqs, axis=1).astype(BF16)
        dqkv[1, s, :, cols] = jnp.concatenate(dks, axis=1).astype(BF16)
        dqkv[2, s, :, cols] = jnp.concatenate(dvs, axis=1).astype(BF16)
        return 0

    reduce_m(2, 0)
    lax.fori_loop(0, SLOTS, attend_back, 0)
    scatter_b(p_m)
    reduce_c(3)
    reduce_m(2, 1)
    lax.fori_loop(SLOTS, 2 * SLOTS, attend_back, 0)

    def dwq_step(zz, _):
        left = n1[:, :, :, strip(zz)].reshape(512, 256)
        for t in range(3):
            gq[t, zz] = mm_tn(left, dqkv[t].reshape(512, 256)).astype(BF16)
        return 0

    lax.fori_loop(0, RANKS, dwq_step, 0)
    for w in (0, 4, 5):
        reduce_a(w)

    def dn1_step(zz, _):
        val = mm_nt(dqkv[0].reshape(512, 256), wq[zz, :, 0:256])
        val = val + mm_nt(dqkv[1].reshape(512, 256), wq[zz, :, 256:512])
        val = val + mm_nt(dqkv[2].reshape(512, 256), wq[zz, :, 512:768])
        d1b[:, :, :, strip(zz)] = val.astype(BF16).reshape(SLOTS, RANKS, 64, 256)
        return 0

    lax.fori_loop(0, RANKS, dn1_step, 0)
    scatter_a(p_d1)
    for w in (0, 4, 5):
        reduce_b(w)
    m = scatter_c(p_m) + row(7)
    outb[...] = (h1[...] + m).astype(BF16).reshape(SLOTS, 64, 1024)
    exchange(outb, outr, e_out, backs)
    for k in range(2):
        reduce_m(1, k)
    scatter_b(p_d1)
    reduce_d(3)
    reduce_m(0, 0)
    reduce_c(2)

    dq_sum = jnp.sum(dqkv[0].astype(F32).reshape(512, 256), axis=0, keepdims=True)
    dv_sum = jnp.sum(dqkv[2].astype(F32).reshape(512, 256), axis=0, keepdims=True)
    gap = jnp.zeros((1, 128), F32)
    pieces = []
    for zz in range(Z):
        h = slice(zz * HEAD, zz * HEAD + HEAD)
        pieces += [dq_sum[:, h], dv_sum[:, h], gap]
    sms[pl.ds(8 + 2 * q, 1), :] = jnp.concatenate(pieces, axis=1)
    xh, inv = normed(rc[...].astype(F32).reshape(128, 1024))
    reduce_m(0, 1)
    reduce_m(4, 0)
    reduce_c(1)

    dn1 = scatter_c(p_d1)
    own(0, dn1 * xh)
    own(2, dn1)
    u_core, u_line, u_rank = take(1), take(1), take(1)
    send(sms, smc, u_core, partner, track(sms))
    cgb[...] = (dh1[...] + norm_back(dn1 * row(0), xh, inv)).astype(BF16).reshape(SLOTS, 64, 1024)
    exchange(cgb, cgr, e_cg, backs)
    reduce_m(4, 1)
    reduce_c(0)
    reduce_m(5, 0)
    reduce_m(5, 1)

    arrive(smc, u_core)
    both = sms[...] + smc[...]
    for zz in range(Z):
        smx[0, zz] = both[:, zz * 256 : zz * 256 + 256]
    o_line, o_rank = track(smz), track(smz)
    for d in range(1, Z):
        send(smx.at[0, (z + d) % Z], smz.at[d - 1], u_line, (replica, (z + d) % Z), o_line)
    reduce_d(2)
    reduce_c(4)
    reduce_e(3)
    reduce_d(1)
    reduce_c(5)
    reduce_d(0)
    reduce_d(4)
    reduce_e(2)
    arrive(smz, u_line)
    smx[1, 0] = smx[0, z] + smz[0] + smz[1] + smz[2]
    for k, rank in enumerate((qx, qy, qd)):
        send(smx.at[1, 0], smx.at[1, 1 + k], u_rank, dev(rank, c, z), o_rank)
    reduce_d(5)
    for w in (1, 0, 4, 5):
        reduce_e(w)
    arrive(smx.at[1, pl.ds(1, 3)], u_rank)
    sm_out[...] = smx[1, 0] + smx[1, 1] + smx[1, 2] + smx[1, 3]

    exchange_wait(outr, e_out)
    out_k[...] = outr[...].reshape(128, 1024)
    exchange_wait(cgr, e_cg)
    cg_k[...] = cgr[...].reshape(128, 1024)
    for w in (3, 2, 1, 0, 4, 5):
        reduce_f(w)
    assert counter == [ARRIVALS, SENDS], counter
    for finish in pending:
        finish()


def finish_kernel(
    live, out_k, cg_k, oq, oo, o1, o2, sm,
    out, cg, dwq, dwo, dw1, dw2, dgain, dnbias, dpbias, dfbias,
    b_out, b_cg, bq, bo, b1, b2, f_out, f_cg, fq, fo, f1, f2, isem, osem,
):
    ins, outs = [], []

    def fetch(src, dst):
        cp = pltpu.make_async_copy(src, dst, isem.at[len(ins)])
        cp.start()
        ins.append(cp)

    def store(src, dst):
        cp = pltpu.make_async_copy(src, dst, osem.at[len(outs)])
        cp.start()
        outs.append(cp)

    for h in range(2):
        fetch(o2.at[pl.ds(2 * h, 2)], b2.at[pl.ds(2 * h, 2)])
    for h in range(2):
        fetch(o1.at[:, pl.ds(128 * h, 128)], b1.at[:, pl.ds(128 * h, 128)])
    for h in range(2):
        fetch(oq.at[:, :, pl.ds(128 * h, 128)], bq.at[:, :, pl.ds(128 * h, 128)])
    fetch(oo, bo)
    fetch(cg_k, b_cg)
    fetch(out_k, b_out)

    dgain[...] = sm[0:2]
    dnbias[...] = sm[2:4]
    lane = lax.broadcasted_iota(jnp.int32, (1, 128), 1)
    rows = [sm[8 + 2 * k : 9 + 2 * k, 0:128] for k in range(RANKS)]
    turn = [pltpu.roll(r, HEAD, 1) for r in rows]
    for g in range(2):
        a, b = 2 * g, 2 * g + 1
        dpbias[0:1, g * 128 : g * 128 + 128] = jnp.where(lane < HEAD, rows[a], turn[b])
        dpbias[1:2, g * 128 : g * 128 + 128] = jnp.where(lane < HEAD, turn[a], rows[b])
    dpbias[2:4] = sm[6:8]
    for k in range(RANKS):
        dfbias[pl.ds(k * 256, 256)] = sm[9 + 2 * k : 10 + 2 * k, :].reshape(256)

    for h in range(2):
        ins[h].wait()

        def two(i, _, h=h):
            f2[pl.ds(512 * h + 64 * i, 64), :] = b2[2 * h + i // 4, strip(i % 4, 64), :].astype(F32)
            return 0

        lax.fori_loop(0, 8, two, 0)
        store(f2.at[pl.ds(512 * h, 512)], dw2.at[pl.ds(512 * h, 512)])
    for h in range(2):
        ins[2 + h].wait()

        def one(i, _, h=h):
            at = pl.ds(pl.multiple_of(128 * h + 16 * i, 16), 16)
            for k in range(RANKS):
                for zz in range(RANKS):
                    f1[at, zz * 1024 + k * 256 : zz * 1024 + k * 256 + 256] = b1[k, at, zz * 256 : zz * 256 + 256].astype(F32)
            return 0

        lax.fori_loop(0, 8, one, 0)
        store(f1.at[pl.ds(128 * h, 128)], dw1.at[pl.ds(128 * h, 128)])
    lane = lax.broadcasted_iota(jnp.int32, (16, 128), 1)
    for h in range(2):
        ins[4 + h].wait()

        def attn(i, _, h=h):
            at = pl.ds(pl.multiple_of(128 * h + 16 * i, 16), 16)
            for t in range(3):
                for m in range(2):
                    part = [bq[t, k, at, m * 128 : m * 128 + 128].astype(F32) for k in range(RANKS)]
                    turn = [pltpu.roll(p, HEAD, 1) for p in part]
                    col = t * 1024 + m * 512
                    for g in range(2):
                        a, b = 2 * g, 2 * g + 1
                        fq[at, col + g * 128 : col + g * 128 + 128] = jnp.where(lane < HEAD, part[a], turn[b])
                        fq[at, col + 256 + g * 128 : col + 384 + g * 128] = jnp.where(lane < HEAD, turn[a], part[b])
            return 0

        lax.fori_loop(0, 8, attn, 0)
        store(fq.at[pl.ds(128 * h, 128)], dwq.at[pl.ds(128 * h, 128)])
    ins[6].wait()
    fo[...] = bo[...].astype(F32).reshape(256, 1024)
    store(fo, dwo)
    ins[7].wait()
    f_cg[...] = b_cg[...].astype(F32)
    store(f_cg, cg)
    ins[8].wait()
    for s in range(SLOTS):
        alive = jnp.where(live[0] > s, 1.0, 0.0).astype(F32)
        f_out[s * 64 : s * 64 + 64] = (b_out[s * 64 : s * 64 + 64].astype(F32) * alive).astype(BF16)
    store(f_out, out)
    for cp in outs:
        cp.wait()


def local(
    n_replica,
    clips, cotangent, live_count, w_qkv, w_out, w_fc1, w_fc2, norm_gain, norm_bias, proj_bias, fc1_bias,
):
    vm = pl.BlockSpec(memory_space=pltpu.VMEM)
    smem = pl.BlockSpec(memory_space=pltpu.SMEM)
    anyspace = pl.BlockSpec(memory_space=pl.ANY)
    shape = jax.ShapeDtypeStruct
    tile = (SLOTS, 64, 1024)
    group = (SLOTS, RANKS, 64, 1024)
    V = pltpu.VMEM
    scratch = [
        V(tile, BF16), V(tile, BF16), V(tile, BF16), V((16, 256), F32), V((4, 16, 256), F32), V((12, 256, 128), BF16),
        V((4, 256, 768), BF16), V((4, 64, 1024), BF16), V((4, 256, 1024), BF16), V((4, 256, 1024), BF16),
        V(group, BF16), V(group, BF16), V(group, BF16), V(group, BF16),
        V((3, SLOTS, 256, 256), BF16), V((4, 2, 256, 256), F32), V((SLOTS, 256, 256), BF16),
        V(group, BF16), V(group, BF16), V(group, BF16), V(group, BF16),
        V((8, 64, 1024), BF16), V((8, 64, 1024), BF16), V((8, 64, 1024), BF16), V((8, 64, 1024), BF16),
        V((128, 1024), F32), V((128, 1024), F32), V((SLOTS, 256, 1024), F32), V((SLOTS, 256, 1024), BF16),
        V((SLOTS, 256, 1024), BF16), V((SLOTS, 256, 256), BF16), V((3, SLOTS, 256, 256), BF16),
        V((3, 4, 256, 256), BF16), V((4, 64, 1024), BF16), V((4, 256, 1024), BF16), V((4, 256, 1024), BF16),
        V((3, 4, 128, 256), BF16), V((4, 32, 1024), BF16), V((4, 128, 1024), BF16), V((4, 128, 1024), BF16),
        V((3, 4, 128, 256), BF16), V((4, 32, 1024), BF16), V((4, 128, 1024), BF16), V((4, 128, 1024), BF16),
        V((3, 128, 256), BF16), V((32, 1024), BF16), V((128, 1024), BF16), V((128, 1024), BF16),
        V(tile, BF16), V(tile, BF16), V((16, 1024), F32), V((16, 1024), F32), V((3, 16, 256), F32), V((2, 4, 16, 256), F32),
        V(tile, BF16), V(tile, BF16), V((4, 512, 256), F32),
        pltpu.SemaphoreType.DMA((SENDS,)), pltpu.SemaphoreType.DMA((ARRIVALS,)), pltpu.SemaphoreType.DMA((LOADS + 6,)),
    ]
    parts = pl.pallas_call(
        kernel,
        out_shape=(
            shape((128, 1024), BF16), shape((128, 1024), BF16), shape((3, 4, 256, 256), BF16), shape((4, 64, 1024), BF16),
            shape((4, 256, 1024), BF16), shape((4, 256, 1024), BF16), shape((16, 256), F32),
        ),
        in_specs=[vm, vm, smem, vm, vm, vm, vm, anyspace, anyspace, anyspace, anyspace],
        out_specs=(vm, vm, anyspace, anyspace, anyspace, anyspace, vm),
        scratch_shapes=scratch,
        compiler_params=pltpu.CompilerParams(
            collective_id=0, has_side_effects=True, vmem_limit_bytes=60 * 2**20
        ),
        cost_estimate=pl.CostEstimate(flops=10**10, bytes_accessed=2**25, transcendentals=2**21),
    )(clips, cotangent, live_count, norm_gain, norm_bias, proj_bias, fc1_bias, w_qkv, w_out, w_fc1, w_fc2)

    out, clips_grad, *summed = pl.pallas_call(
        finish_kernel,
        out_shape=(
            shape((128, 1024), BF16), shape((128, 1024), F32), shape((256, 3072), F32), shape((256, 1024), F32),
            shape((256, 4096), F32), shape((1024, 1024), F32), shape((2, 256), F32), shape((2, 256), F32),
            shape((4, 256), F32), shape((1024,), F32),
        ),
        in_specs=[smem] + [anyspace] * 6 + [vm],
        out_specs=[anyspace] * 6 + [vm] * 4,
        scratch_shapes=[
            V((128, 1024), BF16), V((128, 1024), BF16), V((3, 4, 256, 256), BF16), V((4, 64, 1024), BF16),
            V((4, 256, 1024), BF16), V((4, 256, 1024), BF16), V((128, 1024), BF16), V((128, 1024), F32),
            V((256, 3072), F32), V((256, 1024), F32), V((256, 4096), F32), V((1024, 1024), F32),
            pltpu.SemaphoreType.DMA((9,)), pltpu.SemaphoreType.DMA((9,)),
        ],
        compiler_params=pltpu.CompilerParams(vmem_limit_bytes=60 * 2**20),
        cost_estimate=pl.CostEstimate(flops=2**22, bytes_accessed=20 * 2**20, transcendentals=0),
    )(live_count, *parts)
    if n_replica > PLANE:
        groups = [list(range(i, n_replica, PLANE)) for i in range(PLANE)]
        summed = lax.psum(tuple(summed), "replica", axis_index_groups=groups)
    return (out.reshape(tile), clips_grad.reshape(tile)) + tuple(summed)


def solution(mesh):
    in_specs = (
        P("replica", "shard", None),
        P("replica", "shard", None),
        P("replica"),
        P("shard", None),
        P("shard", None),
        P("shard", None),
        P("shard", None),
        P(None, "shard"),
        P(None, "shard"),
        P(None, "shard"),
        P("shard"),
    )
    out_specs = (
        P("replica", "shard", None),
        P("replica", "shard", None),
        P("shard", None),
        P("shard", None),
        P("shard", None),
        P("shard", None),
        P(None, "shard"),
        P(None, "shard"),
        P(None, "shard"),
        P("shard"),
    )
    body = functools.partial(local, mesh.shape["replica"])
    return jax.shard_map(body, mesh=mesh, in_specs=in_specs, out_specs=out_specs, check_vma=False)
```

```python
import functools
import math

import jax
import jax.numpy as jnp
from jax import lax
from jax.experimental import pallas as pl
from jax.experimental.pallas import tpu as pltpu
from jax.sharding import PartitionSpec as P

MESH = pl.DeviceIdType.MESH
F32 = jnp.float32
BF16 = jnp.bfloat16
HEAD = 64
PLANE = 8
RANKS = 4
SLOTS = 2
ARRIVALS = 128
SENDS = 62
LOADS = 19
SCALE = 1.0 / math.sqrt(HEAD)


def mm(a, b):
    return jnp.dot(a, b, preferred_element_type=F32)


def mm_nt(a, b):
    return lax.dot_general(a, b, (((1,), (1,)), ((), ())), preferred_element_type=F32)


def mm_tn(a, b):
    return lax.dot_general(a, b, (((0,), (0,)), ((), ())), preferred_element_type=F32)


def normed(v):
    centre = v - jnp.mean(v, axis=-1, keepdims=True)
    spread = jnp.mean(centre * centre, axis=-1, keepdims=True)
    inverse = lax.rsqrt(spread + 1e-6)
    return centre * inverse, inverse


def norm_back(e, xh, inverse):
    first = jnp.mean(e, axis=-1, keepdims=True)
    second = jnp.mean(e * xh, axis=-1, keepdims=True)
    return inverse * (e - first - xh * second)


def strip(i, width=256):
    return pl.ds(pl.multiple_of(i * width, width), width)


def kernel(
    clips, cotangent, live, gains, nbias, pbias, fbias, w_qkv, w_out, w_fc1, w_fc2,
    out_k, cg_k, oq, oo, o1, o2, sm_out,
    cot, rc, cm, dmt, sml, smg, tmp, wq, wo, w1, w2,
    n1, n2, dmb, dab, qkv, probs, ob, ab, mb, d2b, d1b, ra, rm, rd2, rd1,
    h1, dh1, slope, gb, dub, dob, dqkv, gq, go, g1, g2,
    cq, co, c1, c2, zq, zo, z1, z2, fq, fo, f1, f2,
    outb, cgb, sms, smc, smz, smx, total2,
    ssem, rsem, lsem,
):
    Z = 4
    replica = lax.axis_index("replica")
    z = lax.axis_index("shard")
    r8 = replica % PLANE
    base = replica - r8
    q = r8 // 2
    c = r8 % 2
    qx = (q // 2) * 2 + (1 - q % 2)
    qy = (1 - q // 2) * 2 + q % 2
    qd = 3 - q
    lower = z // 2
    mate = 2 * lower + 1 - z % 2
    far_middle = 2 - lower
    far = 2 * (1 - lower)
    middle = jnp.logical_or(z == 1, z == 2)
    end = jnp.logical_not(middle)

    def dev(rank, core, plane):
        return (base + 2 * rank + core, plane)

    px, py, partner = dev(qx, c, z), dev(qy, c, z), dev(q, 1 - c, z)

    counter = [0, 0]

    def take(n):
        counter[0] += n
        return counter[0] - n

    pending = []

    def track(ref, when=None):
        counter[1] += 1
        sem = counter[1] - 1

        def finish():
            pltpu.make_async_remote_copy(
                ref, ref, ssem.at[sem], rsem.at[0], device_id=partner, device_id_type=MESH
            ).wait_send()

        pending.append(finish if when is None else lambda: pl.when(when)(finish))
        return sem

    def send(src, dst, sem, device, out, when=None, got=None):
        def start():
            pltpu.make_async_remote_copy(
                src, dst, ssem.at[out], rsem.at[sem], device_id=device, device_id_type=MESH
            ).start()

        if when is None:
            start()
        else:
            pl.when(when)(start)

    def arrive(dst, sem):
        pltpu.make_async_remote_copy(
            dst, dst, ssem.at[sem], rsem.at[sem], device_id=partner, device_id_type=MESH
        ).wait_recv()

    def flip(a, b):
        return (a // 2 + b // 2) % 2 * 2 + (a + b) % 2

    def target(s):
        plane = (q + 2 * s + c) % RANKS
        return flip(q, (z + plane) % RANKS), plane

    def origin(s):
        a = (z - 2 * s - c + 2 * RANKS) % RANKS
        return a, (flip(q, a) - z + RANKS) % RANKS

    moves = [target(s) for s in range(SLOTS)]
    backs = [origin(s) for s in range(SLOTS)]

    def stays(place):
        return jnp.logical_and(place[0] == q, place[1] == z)

    loads = []

    def load(src, dst):
        cp = pltpu.make_async_copy(src, dst, lsem.at[len(loads)])
        cp.start()
        loads.append(cp)

    pair = (q // 2) * 128
    for t in range(3):
        for zz in range(RANKS):
            load(w_qkv.at[:, pl.ds(pl.multiple_of(t * 1024 + zz * 256 + pair, 128), 128)], tmp.at[t * RANKS + zz])
    load(w_out.at[strip(q, HEAD), :], wo.at[z])
    load(cotangent, cot)

    barrier = pltpu.get_barrier_semaphore()
    for device in (px, py, dev(qd, c, z), partner):
        pl.semaphore_signal(barrier, inc=1, device_id=device, device_id_type=MESH)
    for d in range(1, Z):
        pl.semaphore_signal(barrier, inc=1, device_id=(replica, (z + d) % Z), device_id_type=MESH)
    count = 4 + Z - 1
    for place in moves + backs:

        @pl.when(jnp.logical_not(stays(place)))
        def _(place=place):
            pl.semaphore_signal(barrier, inc=1, device_id=dev(place[0], c, place[1]), device_id_type=MESH)

        count = count + jnp.where(stays(place), 0, 1)

    sml[...] = jnp.zeros((16, 256), F32)
    sml[0:2] = gains[...].astype(F32)
    sml[2:4] = nbias[...].astype(F32)
    sml[4:8] = pbias[...].astype(F32)
    for k in range(RANKS):
        sml[8 + k : 9 + k] = fbias[pl.ds(k * 256, 256)].astype(F32).reshape(1, 256)
    lane = lax.broadcasted_iota(jnp.int32, (8, 256), 1)
    turned = pltpu.roll(sml[0:8], (z * HEAD - q * HEAD + 256) % 256, 1)
    kept = jnp.where(jnp.logical_and(lane >= z * HEAD, lane < z * HEAD + HEAD), turned, 0.0)
    sml[12:14] = kept[4:6]

    pl.semaphore_wait(barrier, count)

    def exchange(src, dst, sem, places):
        for s in range(SLOTS):
            to = dev(places[s][0], c, places[s][1])
            leaves = jnp.logical_not(stays(places[s]))
            send(src.at[s], dst.at[s], sem + s, to, track(src.at[s], leaves), when=leaves)

            @pl.when(stays(places[s]))
            def _(s=s):
                pltpu.make_async_copy(src.at[s], dst.at[s], rsem.at[sem + s]).start()

    def exchange_wait(dst, sem):
        for s in range(SLOTS):
            arrive(dst.at[s], sem + s)

    e_clips, e_cot, e_out, e_cg = take(2), take(2), take(2), take(2)
    exchange(clips, rc, e_clips, moves)
    s_small, o_small = take(1), track(smg.at[pl.ds(0, 3)])
    smg[z] = sml[...]
    for d in range(1, Z):
        send(sml, smg.at[z], s_small, (replica, (z + d) % Z), o_small)
    n_first = len(loads)
    for zz in range(RANKS):
        load(w_fc1.at[:, pl.ds(pl.multiple_of(zz * 1024 + q * 256, 256), 256)], w1.at[z, :, pl.ds(zz * 256, 256)])
    load(w_fc2.at[strip(q), :], w2.at[z])

    def mine(half):
        return pl.ds(pl.multiple_of(c * half, half), half)

    def theirs(half):
        return pl.ds(pl.multiple_of((1 - c) * half, half), half)

    def line(w, half):
        rows = pl.ds(0, half)
        return w, half, take(6), (track(w.at[pl.ds(0, 2), rows]), track(w.at[pl.ds(0, 2), rows], middle), track(w.at[pl.ds(0, 3), rows]))

    def line_a(way):
        w, half, sem, outs = way
        own_part = w.at[z, mine(half)]
        send(own_part, own_part, sem, (replica, mate), outs[0])
        send(own_part, own_part, sem + 1 + z % 2, (replica, far_middle), outs[0])

    def share(way, zz, when=None):
        w, half, sem, outs = way
        part = w.at[zz, mine(half)]
        send(part, part, sem + 2 + (zz - z + Z) % Z, partner, outs[2], when=when)

    def line_b(way):
        w, half, sem, outs = way
        for f in (lower, 1 - lower):

            @pl.when(middle)
            def _(f=f):
                arrive(w.at[far + f, mine(half)], sem + 1 + f)

            part = w.at[far + f, mine(half)]
            send(part, part, sem + 1 + f, (replica, mate), outs[1], when=middle)
            share(way, far + f, when=middle)

    def line_c(way):
        w, half, sem, outs = way
        arrive(w.at[mate, mine(half)], sem)
        share(way, mate)
        for f in (lower, 1 - lower):

            @pl.when(end)
            def _(f=f):
                arrive(w.at[far + f, mine(half)], sem + 1 + f)

            share(way, far + f, when=end)

    order = (z, mate, far + lower, far + 1 - lower)

    def line_d(way, k):
        w, half, sem, outs = way
        arrive(w.at[order[k], theirs(half)], sem + 2 + (order[k] - z + Z) % Z)

    ways_q = [line(wq.at[:, :, pl.ds(t * 256, 256)], 128) for t in range(3)]
    way_o = line(wo, 32)
    ways_1 = [line(w1.at[:, :, pl.ds(0, 1024)], 128) for t in range(1)]
    ways_2 = [line(w2.at[:, :, pl.ds(0, 1024)], 128) for t in range(1)]

    CUT = 2
    ROWS = 64 // CUT

    def gather(buf):
        return buf, take(2 * CUT + 1), track(buf.at[:, pl.ds(0, 3)])

    def gather_a(way):
        buf, sem, out = way
        for j in range(CUT):
            rows = pl.ds(j * ROWS, ROWS)
            send(buf.at[0, q, rows], buf.at[0, q, rows], sem + j, px, out)
            send(buf.at[1, q, rows], buf.at[1, q, rows], sem + CUT + j, py, out)
        send(buf.at[1, q], buf.at[1, q], sem + 2 * CUT, px, out)
        send(buf.at[0, q], buf.at[0, q], sem + 2 * CUT, py, out)

    def gather_b(way):
        buf, sem, out = way
        for j in range(CUT):
            rows = pl.ds(j * ROWS, ROWS)
            arrive(buf.at[0, qx, rows], sem + j)
            send(buf.at[0, qx, rows], buf.at[0, qx, rows], sem + 2 * CUT, py, out)
            arrive(buf.at[1, qy, rows], sem + CUT + j)
            send(buf.at[1, qy, rows], buf.at[1, qy, rows], sem + 2 * CUT, px, out)

    def gather_c(way):
        buf, sem, out = way
        arrive(buf.at[0], sem + 2 * CUT)

    def scatter(buf, rb):
        return buf, rb, take(3), track(rb.at[pl.ds(0, 6)])

    def scatter_a(way):
        buf, rb, sem, out = way
        send(buf.at[0, qd], rb.at[0], sem, px, out)
        send(buf.at[1, qd], rb.at[1], sem + 1, py, out)
        send(buf.at[0, qx], rb.at[2], sem + 2, px, out)
        send(buf.at[1, qy], rb.at[3], sem + 2, py, out)

    def scatter_b(way):
        buf, rb, sem, out = way
        arrive(rb.at[0], sem)
        rb[6] = (buf[0, qy].astype(F32) + rb[0].astype(F32)).astype(BF16)
        send(rb.at[6], rb.at[4], sem + 2, py, out)
        arrive(rb.at[1], sem + 1)
        rb[7] = (buf[1, qx].astype(F32) + rb[1].astype(F32)).astype(BF16)
        send(rb.at[7], rb.at[5], sem + 2, px, out)

    def scatter_c(way):
        buf, rb, sem, out = way
        arrive(rb.at[pl.ds(2, 4)], sem + 2)
        first = buf[0, q].astype(F32) + rb[2].astype(F32) + rb[4].astype(F32)
        second = buf[1, q].astype(F32) + rb[3].astype(F32) + rb[5].astype(F32)
        return jnp.concatenate([first, second], axis=0)

    p_n1, p_n2, p_dm, p_da = (gather(buf) for buf in (n1, n2, dmb, dab))
    p_a, p_m, p_d2, p_d1 = scatter(ab, ra), scatter(mb, rm), scatter(d2b, rd2), scatter(d1b, rd1)

    WAYS = 6
    halves = (128, 32, 128, 128, 128, 128)
    grads = (gq.at[0], go, g1, g2, gq.at[1], gq.at[2])
    cores = (cq.at[0], co, c1, c2, cq.at[1], cq.at[2])
    lines = (zq.at[0], zo, z1, z2, zq.at[1], zq.at[2])
    finals = (fq.at[0], fo, f1, f2, fq.at[1], fq.at[2])
    results = (oq.at[0], oo, o1, o2, oq.at[1], oq.at[2])
    t_core = [take(1) for _ in range(WAYS)]
    t_line = [take(3) for _ in range(WAYS)]
    t_rank = [take(3) for _ in range(WAYS)]
    t_pass = [take(1) for _ in range(WAYS)]
    stored = [None] * WAYS
    q_core = [track(cores[w]) for w in range(WAYS)]
    q_line = [track(lines[w].at[pl.ds(0, 3)]) for w in range(WAYS)]
    q_rank = [track(lines[w].at[pl.ds(0, 3)]) for w in range(WAYS)]
    q_pass = [track(cores[w]) for w in range(WAYS)]

    def reduce_a(w):
        send(grads[w].at[:, theirs(halves[w])], cores[w], t_core[w], partner, q_core[w])

    reach = (1 - lower, lower)

    def reduce_b(w):
        rows = mine(halves[w])
        arrive(cores[w], t_core[w])

        def step(zz, _):
            grads[w][zz, rows] = (grads[w][zz, rows].astype(F32) + cores[w][zz].astype(F32)).astype(BF16)
            return 0

        lax.fori_loop(0, Z, step, 0)
        for f in reach:
            send(
                grads[w].at[far + f, rows], lines[w].at[2 + f], t_line[w] + 1 + f, (replica, mate), q_line[w],
                when=end, got=middle,
            )
        send(grads[w].at[mate, rows], lines[w].at[0], t_line[w], (replica, mate), q_line[w])

    def reduce_m(w, k):
        rows = mine(halves[w])
        f = reach[k]

        @pl.when(middle)
        def _():
            arrive(lines[w].at[2 + f], t_line[w] + 1 + f)
            grads[w][far + f, rows] = (grads[w][far + f, rows].astype(F32) + lines[w][2 + f].astype(F32)).astype(BF16)

        send(grads[w].at[far + f, rows], lines[w].at[1], t_line[w], (replica, far + f), q_line[w], when=middle)

    def spots(w, rank, core):
        half = halves[w]
        first = pl.multiple_of(core * half, half)
        second = pl.multiple_of(core * half + half // 2, half // 2)
        return (
            results[w].at[rank, pl.ds(first, half // 2)],
            results[w].at[rank, pl.ds(second, half // 2)],
            results[w].at[rank, pl.ds(first, half)],
        )

    def reduce_c(w):
        half = halves[w]
        arrive(lines[w].at[pl.ds(0, 2)], t_line[w])
        total = grads[w][z, mine(half)].astype(F32)
        for k in range(2):
            total = total + lines[w][k].astype(F32)
        finals[w][...] = total.astype(BF16)
        one, two, both = spots(w, q, c)
        a, b = finals[w].at[pl.ds(0, half // 2)], finals[w].at[pl.ds(half // 2, half // 2)]
        send(a, one, t_rank[w], px, q_rank[w])
        send(b, two, t_rank[w] + 1, py, q_rank[w])
        send(b, two, t_rank[w] + 2, px, q_rank[w])
        send(a, one, t_rank[w] + 2, py, q_rank[w])
        stored[w] = pltpu.make_async_copy(finals[w], both, lsem.at[LOADS + w])
        stored[w].start()

    def reduce_d(w):
        one = spots(w, qx, c)[0]
        arrive(one, t_rank[w])
        send(one, one, t_rank[w] + 2, py, q_rank[w])
        two = spots(w, qy, c)[1]
        arrive(two, t_rank[w] + 1)
        send(two, two, t_rank[w] + 2, px, q_rank[w])

    def reduce_e(w):
        arrive(results[w].at[pl.ds(0, 2), mine(halves[w])], t_rank[w] + 2)
        stored[w].wait()
        part = results[w].at[:, mine(halves[w])]
        send(part, part, t_pass[w], partner, q_pass[w])

    def reduce_f(w):
        arrive(results[w].at[:, theirs(halves[w])], t_pass[w])

    for cp in loads[:n_first]:
        cp.wait()
    lane = lax.broadcasted_iota(jnp.int32, (256, 128), 1)
    even = q % 2 == 0
    for t in range(3):
        for m in range(2):
            left = tmp[t * RANKS + 2 * m].astype(F32)
            right = tmp[t * RANKS + 2 * m + 1].astype(F32)
            lo = jnp.where(even, left, pltpu.roll(left, HEAD, 1))
            hi = jnp.where(even, pltpu.roll(right, HEAD, 1), right)
            wq[z, :, t * 256 + m * 128 : t * 256 + m * 128 + 128] = jnp.where(lane < HEAD, lo, hi).astype(BF16)
    for way in ways_q:
        line_a(way)

    for s in range(SLOTS):
        alive = jnp.where(live[0] > s, 1.0, 0.0).astype(F32)
        cm[s] = (cot[s].astype(F32) * alive).astype(BF16)

    arrive(smg.at[pl.ds(0, 3)], s_small)

    def row(i):
        return jnp.concatenate([smg[zz, i : i + 1, :] for zz in range(Z)], axis=1)

    bias_q = smg[0, 12:13, :] + smg[1, 12:13, :] + smg[2, 12:13, :] + smg[3, 12:13, :]
    bias_v = smg[0, 13:14, :] + smg[1, 13:14, :] + smg[2, 13:14, :] + smg[3, 13:14, :]

    exchange_wait(rc, e_clips)
    x = rc[...].astype(F32).reshape(128, 1024)
    xh, _ = normed(x)
    n1[:, q] = (xh * row(0) + row(2)).astype(BF16).reshape(SLOTS, 64, 1024)
    gather_a(p_n1)
    line_b(ways_q[0])
    gather_b(p_n1)
    line_b(ways_q[1])
    line_b(ways_q[2])
    line_a(way_o)
    exchange(cm, dmt, e_cot, moves)
    gather_c(p_n1)
    for way in ways_q:
        line_c(way)
    line_b(way_o)
    for cp in loads[n_first:]:
        cp.wait()
    for way in ways_1:
        line_a(way)
    for way in ways_q:
        for k in range(1, Z):
            line_d(way, k)

    def qkv_step(t, _):
        bias = jnp.where(t == 0, bias_q, jnp.where(t == 2, bias_v, 0.0))
        val = mm(n1[...].reshape(512, 1024), wq[:, :, strip(t)].reshape(1024, 256)) + bias
        qkv[t] = val.astype(BF16).reshape(SLOTS, 256, 256)
        return 0

    lax.fori_loop(0, 3, qkv_step, 0)
    line_c(way_o)
    exchange_wait(dmt, e_cot)
    dmb[:, q] = dmt[...]
    gather_a(p_dm)

    def attend(i, _):
        s = i // 2
        cols = strip(i % 2, 128)
        qq, kk, vv = qkv[0, s, :, cols], qkv[1, s, :, cols], qkv[2, s, :, cols]
        outs = []
        for j in range(2):
            h = slice(j * HEAD, j * HEAD + HEAD)
            score = mm_nt(qq[:, h], kk[:, h]) * SCALE
            e = jnp.exp(score - jnp.max(score, axis=-1, keepdims=True))
            p = e / jnp.sum(e, axis=-1, keepdims=True)
            probs[i, j] = p
            outs.append(mm(p.astype(BF16), vv[:, h]))
        ob[s, :, cols] = jnp.concatenate(outs, axis=1).astype(BF16)
        return 0

    lax.fori_loop(0, 2 * SLOTS, attend, 0)
    for k in range(1, Z):
        line_d(way_o, k)

    def proj_step(s, _):
        val = mm(ob[s], wo[...].reshape(256, 1024))
        ab[s] = val.astype(BF16).reshape(RANKS, 64, 1024)
        return 0

    lax.fori_loop(0, SLOTS, proj_step, 0)
    scatter_a(p_a)
    gather_b(p_dm)
    scatter_b(p_a)
    for way in ways_1:
        line_b(way)
    for way in ways_2:
        line_a(way)
    a = scatter_c(p_a) + row(6)
    hh = x + a
    h1[...] = hh
    xh2, _ = normed(hh)
    n2[:, q] = (xh2 * row(1) + row(3)).astype(BF16).reshape(SLOTS, 64, 1024)
    gather_a(p_n2)
    gather_b(p_n2)
    for way in ways_1:
        line_c(way)
    for way in ways_2:
        line_b(way)
    for way in ways_1:
        for k in range(1, Z):
            line_d(way, k)
    gather_c(p_n2)

    def fc1_step(i, _):
        s = i // RANKS
        zz = i % RANKS
        cols = strip(zz)
        u = mm(n2[s].reshape(256, 1024), w1[:, :, cols].reshape(1024, 256)) + smg[zz, pl.ds(8 + q, 1), :]
        cdf = 0.5 * (1.0 + lax.erf(u * (1.0 / math.sqrt(2.0))))
        gb[s, :, cols] = (u * cdf).astype(BF16)
        slope[s, :, cols] = cdf + u * jnp.exp(-0.5 * u * u) * (1.0 / math.sqrt(2.0 * math.pi))
        return 0

    lax.fori_loop(0, SLOTS * RANKS, fc1_step, 0)
    gather_c(p_dm)

    def dw2_step(zz, _):
        g2[zz] = mm_tn(gb[:, :, strip(zz)].reshape(512, 256), dmb[...].reshape(512, 1024)).astype(BF16)
        return 0

    lax.fori_loop(0, RANKS, dw2_step, 0)
    reduce_a(3)
    for way in ways_2:
        line_c(way)

    for k in range(RANKS):
        zz = order[k]
        if k == 1:
            reduce_b(3)
        if k > 0:
            for way in ways_2:
                line_d(way, k)
        cols = strip(zz)
        dg = mm_nt(dmb[...].reshape(512, 1024), w2[zz]).reshape(SLOTS, 256, 256)
        du = (dg * slope[:, :, cols]).astype(BF16)
        dub[:, :, cols] = du

        def dn2_step(i, _, k=k, cols=cols):
            part = mm_nt(dub[:, :, cols].reshape(512, 256), w1[i, :, cols])
            if k > 0:
                part = part + total2[i]
            if k < RANKS - 1:
                total2[i] = part
            else:
                d2b[:, :, :, strip(i)] = part.astype(BF16).reshape(SLOTS, RANKS, 64, 256)
            return 0

        lax.fori_loop(0, RANKS, dn2_step, 0)
    scatter_a(p_d2)

    def dw1_step(zz, _):
        g1[zz] = mm_tn(n2[:, :, :, strip(zz)].reshape(512, 256), dub[...].reshape(512, 1024)).astype(BF16)
        return 0

    lax.fori_loop(0, RANKS, dw1_step, 0)
    reduce_a(2)
    scatter_b(p_d2)
    reduce_b(2)

    sms[...] = jnp.zeros((16, 1024), F32)

    def own(i, val):
        sms[i : i + 1, :] = jnp.sum(val, axis=0, keepdims=True)

    dy = dmt[...].astype(F32).reshape(128, 1024)
    own(7, dy)
    xh2, inv2 = normed(h1[...])
    dn2 = scatter_c(p_d2)
    res = dy + norm_back(dn2 * row(1), xh2, inv2)
    da = res.astype(BF16)
    dab[:, q] = da.reshape(SLOTS, 64, 1024)
    gather_a(p_da)
    for k in range(2):
        reduce_m(3, k)
    dh1[...] = res
    own(1, dn2 * xh2)
    own(3, dn2)
    own(6, da.astype(F32))
    fc1_sum = jnp.sum(dub[...].astype(F32).reshape(512, 1024), axis=0, keepdims=True)
    sms[pl.ds(9 + 2 * q, 1), :] = fc1_sum

    def m_step(s, _):
        mb[s] = mm(gb[s], w2[...].reshape(1024, 1024)).astype(BF16).reshape(RANKS, 64, 1024)
        return 0

    lax.fori_loop(0, SLOTS, m_step, 0)
    gather_b(p_da)
    scatter_a(p_m)
    gather_c(p_da)
    go[...] = mm_tn(ob[...].reshape(512, 256), dab[...].reshape(512, 1024)).astype(BF16).reshape(Z, HEAD, 1024)
    reduce_a(1)

    def do_step(s, _):
        dob[s] = mm_nt(dab[s].reshape(256, 1024), wo[...].reshape(256, 1024)).astype(BF16)
        return 0

    lax.fori_loop(0, SLOTS, do_step, 0)
    reduce_b(1)

    def attend_back(i, _):
        s = i // 2
        cols = strip(i % 2, 128)
        qq, kk, vv, dd = qkv[0, s, :, cols], qkv[1, s, :, cols], qkv[2, s, :, cols], dob[s, :, cols]
        dqs, dks, dvs = [], [], []
        for j in range(2):
            h = slice(j * HEAD, j * HEAD + HEAD)
            p = probs[i, j]
            dp = mm_nt(dd[:, h], vv[:, h])
            ds = (p * (dp - jnp.sum(p * dp, axis=-1, keepdims=True))).astype(BF16)
            dqs.append(mm(ds, kk[:, h]) * SCALE)
            dks.append(mm_tn(ds, qq[:, h]) * SCALE)
            dvs.append(mm_tn(p.astype(BF16), dd[:, h]))
        dqkv[0, s, :, cols] = jnp.concatenate(dqs, axis=1).astype(BF16)
        dqkv[1, s, :, cols] = jnp.concatenate(dks, axis=1).astype(BF16)
        dqkv[2, s, :, cols] = jnp.concatenate(dvs, axis=1).astype(BF16)
        return 0

    reduce_m(2, 0)
    lax.fori_loop(0, SLOTS, attend_back, 0)
    scatter_b(p_m)
    reduce_c(3)
    reduce_m(2, 1)
    lax.fori_loop(SLOTS, 2 * SLOTS, attend_back, 0)

    def dn1_step(zz, _):
        val = mm_nt(dqkv[0].reshape(512, 256), wq[zz, :, 0:256])
        val = val + mm_nt(dqkv[1].reshape(512, 256), wq[zz, :, 256:512])
        val = val + mm_nt(dqkv[2].reshape(512, 256), wq[zz, :, 512:768])
        d1b[:, :, :, strip(zz)] = val.astype(BF16).reshape(SLOTS, RANKS, 64, 256)
        return 0

    lax.fori_loop(0, RANKS, dn1_step, 0)
    scatter_a(p_d1)
    def dwq_step(zz, _):
        left = n1[:, :, :, strip(zz)].reshape(512, 256)
        for t in range(3):
            gq[t, zz] = mm_tn(left, dqkv[t].reshape(512, 256)).astype(BF16)
        return 0

    lax.fori_loop(0, RANKS, dwq_step, 0)
    for w in (0, 4, 5):
        reduce_a(w)

    for k in range(2):
        reduce_m(1, k)
    scatter_b(p_d1)
    for w in (0, 4, 5):
        reduce_b(w)
    reduce_d(3)
    m = scatter_c(p_m) + row(7)
    outb[...] = (h1[...] + m).astype(BF16).reshape(SLOTS, 64, 1024)
    xh, inv = normed(rc[...].astype(F32).reshape(128, 1024))

    dn1 = scatter_c(p_d1)
    cgb[...] = (dh1[...] + norm_back(dn1 * row(0), xh, inv)).astype(BF16).reshape(SLOTS, 64, 1024)
    exchange(cgb, cg_k, e_cg, backs)
    reduce_c(2)
    exchange(outb, out_k, e_out, backs)
    own(0, dn1 * xh)
    own(2, dn1)

    dq_sum = jnp.sum(dqkv[0].astype(F32).reshape(512, 256), axis=0, keepdims=True)
    dv_sum = jnp.sum(dqkv[2].astype(F32).reshape(512, 256), axis=0, keepdims=True)
    gap = jnp.zeros((1, 128), F32)
    pieces = []
    for zz in range(Z):
        h = slice(zz * HEAD, zz * HEAD + HEAD)
        pieces += [dq_sum[:, h], dv_sum[:, h], gap]
    sms[pl.ds(8 + 2 * q, 1), :] = jnp.concatenate(pieces, axis=1)
    u_core, u_line, u_rank = take(1), take(1), take(1)
    send(sms, smc, u_core, partner, track(sms))
    for k in range(2):
        reduce_m(0, k)
    reduce_c(1)
    reduce_e(3)
    arrive(smc, u_core)
    both = sms[...] + smc[...]
    for zz in range(Z):
        smx[0, zz] = both[:, zz * 256 : zz * 256 + 256]
    o_line, o_rank = track(smz), track(smz)
    for d in range(1, Z):
        send(smx.at[0, (z + d) % Z], smz.at[d - 1], u_line, (replica, (z + d) % Z), o_line)
    for k in range(2):
        reduce_m(4, k)
    reduce_c(0)
    for k in range(2):
        reduce_m(5, k)
    reduce_d(2)
    reduce_c(4)
    reduce_d(1)
    reduce_c(5)
    reduce_d(0)
    reduce_e(2)
    reduce_d(4)
    arrive(smz, u_line)
    smx[1, 0] = smx[0, z] + smz[0] + smz[1] + smz[2]
    for k, rank in enumerate((qx, qy, qd)):
        send(smx.at[1, 0], smx.at[1, 1 + k], u_rank, dev(rank, c, z), o_rank)
    reduce_d(5)
    for w in (1, 0, 4, 5):
        reduce_e(w)
    arrive(smx.at[1, pl.ds(1, 3)], u_rank)
    sm_out[...] = smx[1, 0] + smx[1, 1] + smx[1, 2] + smx[1, 3]

    exchange_wait(out_k, e_out)
    exchange_wait(cg_k, e_cg)
    for w in (3, 2, 1, 0, 4, 5):
        reduce_f(w)
    assert counter == [ARRIVALS, SENDS], counter
    for finish in pending:
        finish()


def finish_kernel(
    live, out_k, cg_k, oq, oo, o1, o2, sm,
    out, cg, dwq, dwo, dw1, dw2, dgain, dnbias, dpbias, dfbias,
    b_out, b_cg, bq, bo, b1, b2, f_out, f_cg, fq, fo, f1, f2, isem, osem,
):
    ins, outs = [], []

    def fetch(src, dst):
        cp = pltpu.make_async_copy(src, dst, isem.at[len(ins)])
        cp.start()
        ins.append(cp)

    def store(src, dst):
        cp = pltpu.make_async_copy(src, dst, osem.at[len(outs)])
        cp.start()
        outs.append(cp)

    for h in range(2):
        fetch(o2.at[pl.ds(2 * h, 2)], b2.at[pl.ds(2 * h, 2)])
    for h in range(2):
        fetch(o1.at[:, pl.ds(128 * h, 128)], b1.at[:, pl.ds(128 * h, 128)])
    for h in range(2):
        fetch(oq.at[:, :, pl.ds(128 * h, 128)], bq.at[:, :, pl.ds(128 * h, 128)])
    fetch(oo, bo)
    fetch(cg_k, b_cg)
    fetch(out_k, b_out)

    dgain[...] = sm[0:2]
    dnbias[...] = sm[2:4]
    lane = lax.broadcasted_iota(jnp.int32, (1, 128), 1)
    rows = [sm[8 + 2 * k : 9 + 2 * k, 0:128] for k in range(RANKS)]
    turn = [pltpu.roll(r, HEAD, 1) for r in rows]
    for g in range(2):
        a, b = 2 * g, 2 * g + 1
        dpbias[0:1, g * 128 : g * 128 + 128] = jnp.where(lane < HEAD, rows[a], turn[b])
        dpbias[1:2, g * 128 : g * 128 + 128] = jnp.where(lane < HEAD, turn[a], rows[b])
    dpbias[2:4] = sm[6:8]
    for k in range(RANKS):
        dfbias[pl.ds(k * 256, 256)] = sm[9 + 2 * k : 10 + 2 * k, :].reshape(256)

    for h in range(2):
        ins[h].wait()

        def two(i, _, h=h):
            f2[pl.ds(512 * h + 64 * i, 64), :] = b2[2 * h + i // 4, strip(i % 4, 64), :].astype(F32)
            return 0

        lax.fori_loop(0, 8, two, 0)
        store(f2.at[pl.ds(512 * h, 512)], dw2.at[pl.ds(512 * h, 512)])
    for h in range(2):
        ins[2 + h].wait()

        def one(i, _, h=h):
            at = pl.ds(pl.multiple_of(128 * h + 16 * i, 16), 16)
            for k in range(RANKS):
                for zz in range(RANKS):
                    f1[at, zz * 1024 + k * 256 : zz * 1024 + k * 256 + 256] = b1[k, at, zz * 256 : zz * 256 + 256].astype(F32)
            return 0

        lax.fori_loop(0, 8, one, 0)
        store(f1.at[pl.ds(128 * h, 128)], dw1.at[pl.ds(128 * h, 128)])
    lane = lax.broadcasted_iota(jnp.int32, (16, 128), 1)
    for h in range(2):
        ins[4 + h].wait()

        def attn(i, _, h=h):
            at = pl.ds(pl.multiple_of(128 * h + 16 * i, 16), 16)
            for t in range(3):
                for m in range(2):
                    part = [bq[t, k, at, m * 128 : m * 128 + 128].astype(F32) for k in range(RANKS)]
                    turn = [pltpu.roll(p, HEAD, 1) for p in part]
                    col = t * 1024 + m * 512
                    for g in range(2):
                        a, b = 2 * g, 2 * g + 1
                        fq[at, col + g * 128 : col + g * 128 + 128] = jnp.where(lane < HEAD, part[a], turn[b])
                        fq[at, col + 256 + g * 128 : col + 384 + g * 128] = jnp.where(lane < HEAD, turn[a], part[b])
            return 0

        lax.fori_loop(0, 8, attn, 0)
        store(fq.at[pl.ds(128 * h, 128)], dwq.at[pl.ds(128 * h, 128)])
    ins[6].wait()
    fo[...] = bo[...].astype(F32).reshape(256, 1024)
    store(fo, dwo)
    ins[7].wait()
    f_cg[...] = b_cg[...].astype(F32).reshape(128, 1024)
    store(f_cg, cg)
    ins[8].wait()
    for s in range(SLOTS):
        alive = jnp.where(live[0] > s, 1.0, 0.0).astype(F32)
        f_out[s * 64 : s * 64 + 64] = (b_out[s].astype(F32) * alive).astype(BF16)
    store(f_out, out)
    for cp in outs:
        cp.wait()


def local(
    n_replica,
    clips, cotangent, live_count, w_qkv, w_out, w_fc1, w_fc2, norm_gain, norm_bias, proj_bias, fc1_bias,
):
    vm = pl.BlockSpec(memory_space=pltpu.VMEM)
    smem = pl.BlockSpec(memory_space=pltpu.SMEM)
    anyspace = pl.BlockSpec(memory_space=pl.ANY)
    shape = jax.ShapeDtypeStruct
    tile = (SLOTS, 64, 1024)
    group = (SLOTS, RANKS, 64, 1024)
    V = pltpu.VMEM
    scratch = [
        V(tile, BF16), V(tile, BF16), V(tile, BF16), V(tile, BF16), V((16, 256), F32), V((4, 16, 256), F32), V((12, 256, 128), BF16),
        V((4, 256, 768), BF16), V((4, 64, 1024), BF16), V((4, 256, 1024), BF16), V((4, 256, 1024), BF16),
        V(group, BF16), V(group, BF16), V(group, BF16), V(group, BF16),
        V((3, SLOTS, 256, 256), BF16), V((4, 2, 256, 256), F32), V((SLOTS, 256, 256), BF16),
        V(group, BF16), V(group, BF16), V(group, BF16), V(group, BF16),
        V((8, 64, 1024), BF16), V((8, 64, 1024), BF16), V((8, 64, 1024), BF16), V((8, 64, 1024), BF16),
        V((128, 1024), F32), V((128, 1024), F32), V((SLOTS, 256, 1024), F32), V((SLOTS, 256, 1024), BF16),
        V((SLOTS, 256, 1024), BF16), V((SLOTS, 256, 256), BF16), V((3, SLOTS, 256, 256), BF16),
        V((3, 4, 256, 256), BF16), V((4, 64, 1024), BF16), V((4, 256, 1024), BF16), V((4, 256, 1024), BF16),
        V((3, 4, 128, 256), BF16), V((4, 32, 1024), BF16), V((4, 128, 1024), BF16), V((4, 128, 1024), BF16),
        V((3, 4, 128, 256), BF16), V((4, 32, 1024), BF16), V((4, 128, 1024), BF16), V((4, 128, 1024), BF16),
        V((3, 128, 256), BF16), V((32, 1024), BF16), V((128, 1024), BF16), V((128, 1024), BF16),
        V(tile, BF16), V(tile, BF16), V((16, 1024), F32), V((16, 1024), F32), V((3, 16, 256), F32), V((2, 4, 16, 256), F32),
        V((4, 512, 256), F32),
        pltpu.SemaphoreType.DMA((SENDS,)), pltpu.SemaphoreType.DMA((ARRIVALS,)), pltpu.SemaphoreType.DMA((LOADS + 6,)),
    ]
    parts = pl.pallas_call(
        kernel,
        out_shape=(
            shape(tile, BF16), shape(tile, BF16), shape((3, 4, 256, 256), BF16), shape((4, 64, 1024), BF16),
            shape((4, 256, 1024), BF16), shape((4, 256, 1024), BF16), shape((16, 256), F32),
        ),
        in_specs=[anyspace, anyspace, smem, vm, vm, vm, vm, anyspace, anyspace, anyspace, anyspace],
        out_specs=(anyspace, anyspace, anyspace, anyspace, anyspace, anyspace, vm),
        scratch_shapes=scratch,
        compiler_params=pltpu.CompilerParams(
            collective_id=0, has_side_effects=True, vmem_limit_bytes=60 * 2**20
        ),
        cost_estimate=pl.CostEstimate(flops=10**10, bytes_accessed=2**25, transcendentals=2**21),
    )(clips, cotangent, live_count, norm_gain, norm_bias, proj_bias, fc1_bias, w_qkv, w_out, w_fc1, w_fc2)

    out, clips_grad, *summed = pl.pallas_call(
        finish_kernel,
        out_shape=(
            shape((128, 1024), BF16), shape((128, 1024), F32), shape((256, 3072), F32), shape((256, 1024), F32),
            shape((256, 4096), F32), shape((1024, 1024), F32), shape((2, 256), F32), shape((2, 256), F32),
            shape((4, 256), F32), shape((1024,), F32),
        ),
        in_specs=[smem] + [anyspace] * 6 + [vm],
        out_specs=[anyspace] * 6 + [vm] * 4,
        scratch_shapes=[
            V(tile, BF16), V(tile, BF16), V((3, 4, 256, 256), BF16), V((4, 64, 1024), BF16),
            V((4, 256, 1024), BF16), V((4, 256, 1024), BF16), V((128, 1024), BF16), V((128, 1024), F32),
            V((256, 3072), F32), V((256, 1024), F32), V((256, 4096), F32), V((1024, 1024), F32),
            pltpu.SemaphoreType.DMA((9,)), pltpu.SemaphoreType.DMA((9,)),
        ],
        compiler_params=pltpu.CompilerParams(vmem_limit_bytes=60 * 2**20),
        cost_estimate=pl.CostEstimate(flops=2**22, bytes_accessed=20 * 2**20, transcendentals=0),
    )(live_count, *parts)
    if n_replica > PLANE:
        groups = [list(range(i, n_replica, PLANE)) for i in range(PLANE)]
        summed = lax.psum(tuple(summed), "replica", axis_index_groups=groups)
    return (out.reshape(tile), clips_grad.reshape(tile)) + tuple(summed)


def solution(mesh):
    in_specs = (
        P("replica", "shard", None),
        P("replica", "shard", None),
        P("replica"),
        P("shard", None),
        P("shard", None),
        P("shard", None),
        P("shard", None),
        P(None, "shard"),
        P(None, "shard"),
        P(None, "shard"),
        P("shard"),
    )
    out_specs = (
        P("replica", "shard", None),
        P("replica", "shard", None),
        P("shard", None),
        P("shard", None),
        P("shard", None),
        P("shard", None),
        P(None, "shard"),
        P(None, "shard"),
        P(None, "shard"),
        P("shard"),
    )
    body = functools.partial(local, mesh.shape["replica"])
    return jax.shard_map(body, mesh=mesh, in_specs=in_specs, out_specs=out_specs, check_vma=False)
```

```python
import functools
import math

import jax
import jax.numpy as jnp
from jax import lax
from jax.experimental import pallas as pl
from jax.experimental.pallas import tpu as pltpu
from jax.sharding import PartitionSpec as P

MESH = pl.DeviceIdType.MESH
F32 = jnp.float32
BF16 = jnp.bfloat16
HEAD = 64
PLANE = 8
RANKS = 4
SLOTS = 2
ARRIVALS = 128
SENDS = 62
LOADS = 19
SCALE = 1.0 / math.sqrt(HEAD)


def mm(a, b):
    return jnp.dot(a, b, preferred_element_type=F32)


def mm_nt(a, b):
    return lax.dot_general(a, b, (((1,), (1,)), ((), ())), preferred_element_type=F32)


def mm_tn(a, b):
    return lax.dot_general(a, b, (((0,), (0,)), ((), ())), preferred_element_type=F32)


def normed(v):
    centre = v - jnp.mean(v, axis=-1, keepdims=True)
    spread = jnp.mean(centre * centre, axis=-1, keepdims=True)
    inverse = lax.rsqrt(spread + 1e-6)
    return centre * inverse, inverse


def norm_back(e, xh, inverse):
    first = jnp.mean(e, axis=-1, keepdims=True)
    second = jnp.mean(e * xh, axis=-1, keepdims=True)
    return inverse * (e - first - xh * second)


def strip(i, width=256):
    return pl.ds(pl.multiple_of(i * width, width), width)


def kernel(
    clips, cotangent, live, gains, nbias, pbias, fbias, w_qkv, w_out, w_fc1, w_fc2,
    out_k, cg_k, oq, oo, o1, o2, sm_out,
    cot, rc, cm, dmt, sml, smg, tmp, wq, wo, w1, w2,
    n1, n2, dmb, dab, qkv, probs, ob, ab, mb, d2b, d1b, ra, rm, rd2, rd1,
    h1, dh1, slope, gb, dub, dob, dqkv, gq, go, g1, g2,
    cq, co, c1, c2, zq, zo, z1, z2, fq, fo, f1, f2,
    outb, cgb, sms, smc, smz, smx, total2,
    ssem, rsem, lsem,
):
    Z = 4
    replica = lax.axis_index("replica")
    z = lax.axis_index("shard")
    r8 = replica % PLANE
    base = replica - r8
    q = r8 // 2
    c = r8 % 2
    qx = (q // 2) * 2 + (1 - q % 2)
    qy = (1 - q // 2) * 2 + q % 2
    qd = 3 - q
    lower = z // 2
    mate = 2 * lower + 1 - z % 2
    far_middle = 2 - lower
    far = 2 * (1 - lower)
    middle = jnp.logical_or(z == 1, z == 2)
    end = jnp.logical_not(middle)

    def dev(rank, core, plane):
        return (base + 2 * rank + core, plane)

    px, py, partner = dev(qx, c, z), dev(qy, c, z), dev(q, 1 - c, z)

    counter = [0, 0]

    def take(n):
        counter[0] += n
        return counter[0] - n

    early, pending = [], []

    def track(ref, when=None, into=pending):
        counter[1] += 1
        sem = counter[1] - 1

        def finish():
            pltpu.make_async_remote_copy(
                ref, ref, ssem.at[sem], rsem.at[0], device_id=partner, device_id_type=MESH
            ).wait_send()

        into.append(finish if when is None else lambda: pl.when(when)(finish))
        return sem

    def send(src, dst, sem, device, out, when=None, got=None):
        def start():
            pltpu.make_async_remote_copy(
                src, dst, ssem.at[out], rsem.at[sem], device_id=device, device_id_type=MESH
            ).start()

        if when is None:
            start()
        else:
            pl.when(when)(start)

    def arrive(dst, sem):
        pltpu.make_async_remote_copy(
            dst, dst, ssem.at[sem], rsem.at[sem], device_id=partner, device_id_type=MESH
        ).wait_recv()

    def flip(a, b):
        return (a // 2 + b // 2) % 2 * 2 + (a + b) % 2

    def target(s):
        plane = (q + 2 * s + c) % RANKS
        return flip(q, (z + plane) % RANKS), plane

    def origin(s):
        a = (z - 2 * s - c + 2 * RANKS) % RANKS
        return a, (flip(q, a) - z + RANKS) % RANKS

    moves = [target(s) for s in range(SLOTS)]
    backs = [origin(s) for s in range(SLOTS)]

    def stays(place):
        return jnp.logical_and(place[0] == q, place[1] == z)

    loads = []

    def load(src, dst):
        cp = pltpu.make_async_copy(src, dst, lsem.at[len(loads)])
        cp.start()
        loads.append(cp)

    pair = (q // 2) * 128
    for t in range(3):
        for zz in range(RANKS):
            load(w_qkv.at[:, pl.ds(pl.multiple_of(t * 1024 + zz * 256 + pair, 128), 128)], tmp.at[t * RANKS + zz])
    load(w_out.at[strip(q, HEAD), :], wo.at[z])
    load(cotangent, cot)

    barrier = pltpu.get_barrier_semaphore()
    for device in (px, py, dev(qd, c, z), partner):
        pl.semaphore_signal(barrier, inc=1, device_id=device, device_id_type=MESH)
    for d in range(1, Z):
        pl.semaphore_signal(barrier, inc=1, device_id=(replica, (z + d) % Z), device_id_type=MESH)
    count = 4 + Z - 1
    for place in moves + backs:

        @pl.when(jnp.logical_not(stays(place)))
        def _(place=place):
            pl.semaphore_signal(barrier, inc=1, device_id=dev(place[0], c, place[1]), device_id_type=MESH)

        count = count + jnp.where(stays(place), 0, 1)

    sml[...] = jnp.zeros((16, 256), F32)
    sml[0:2] = gains[...].astype(F32)
    sml[2:4] = nbias[...].astype(F32)
    sml[4:8] = pbias[...].astype(F32)
    for k in range(RANKS):
        sml[8 + k : 9 + k] = fbias[pl.ds(k * 256, 256)].astype(F32).reshape(1, 256)
    lane = lax.broadcasted_iota(jnp.int32, (8, 256), 1)
    turned = pltpu.roll(sml[0:8], (z * HEAD - q * HEAD + 256) % 256, 1)
    kept = jnp.where(jnp.logical_and(lane >= z * HEAD, lane < z * HEAD + HEAD), turned, 0.0)
    sml[12:14] = kept[4:6]

    pl.semaphore_wait(barrier, count)

    def exchange(src, dst, sem, places, into=pending):
        for s in range(SLOTS):
            to = dev(places[s][0], c, places[s][1])
            leaves = jnp.logical_not(stays(places[s]))
            send(src.at[s], dst.at[s], sem + s, to, track(src.at[s], leaves, into), when=leaves)

            @pl.when(stays(places[s]))
            def _(s=s):
                pltpu.make_async_copy(src.at[s], dst.at[s], rsem.at[sem + s]).start()

    def exchange_wait(dst, sem):
        for s in range(SLOTS):
            arrive(dst.at[s], sem + s)

    e_clips, e_cot, e_out, e_cg = take(2), take(2), take(2), take(2)
    exchange(clips, rc, e_clips, moves, early)
    s_small, o_small = take(1), track(smg.at[pl.ds(0, 3)], None, early)
    smg[z] = sml[...]
    for d in range(1, Z):
        send(sml, smg.at[z], s_small, (replica, (z + d) % Z), o_small)
    n_first = len(loads)
    for zz in range(RANKS):
        load(w_fc1.at[:, pl.ds(pl.multiple_of(zz * 1024 + q * 256, 256), 256)], w1.at[z, :, pl.ds(zz * 256, 256)])
    load(w_fc2.at[strip(q), :], w2.at[z])

    def mine(half):
        return pl.ds(pl.multiple_of(c * half, half), half)

    def theirs(half):
        return pl.ds(pl.multiple_of((1 - c) * half, half), half)

    def line(w, half):
        rows = pl.ds(0, half)
        own_sends = track(w.at[pl.ds(0, 2), rows], None, early)
        passed_on = track(w.at[pl.ds(0, 2), rows], middle, early)
        shared = track(w.at[pl.ds(0, 3), rows], None, early)
        return w, half, take(6), (own_sends, passed_on, shared)

    def line_a(way):
        w, half, sem, outs = way
        own_part = w.at[z, mine(half)]
        send(own_part, own_part, sem, (replica, mate), outs[0])
        send(own_part, own_part, sem + 1 + z % 2, (replica, far_middle), outs[0])

    def share(way, zz, when=None):
        w, half, sem, outs = way
        part = w.at[zz, mine(half)]
        send(part, part, sem + 2 + (zz - z + Z) % Z, partner, outs[2], when=when)

    def line_b(way):
        w, half, sem, outs = way
        for f in (lower, 1 - lower):

            @pl.when(middle)
            def _(f=f):
                arrive(w.at[far + f, mine(half)], sem + 1 + f)

            part = w.at[far + f, mine(half)]
            send(part, part, sem + 1 + f, (replica, mate), outs[1], when=middle)
            share(way, far + f, when=middle)

    def line_c(way):
        w, half, sem, outs = way
        arrive(w.at[mate, mine(half)], sem)
        share(way, mate)
        for f in (lower, 1 - lower):

            @pl.when(end)
            def _(f=f):
                arrive(w.at[far + f, mine(half)], sem + 1 + f)

            share(way, far + f, when=end)

    order = (z, mate, far + lower, far + 1 - lower)

    def line_d(way, k):
        w, half, sem, outs = way
        arrive(w.at[order[k], theirs(half)], sem + 2 + (order[k] - z + Z) % Z)

    ways_q = [line(wq.at[:, :, pl.ds(t * 256, 256)], 128) for t in range(3)]
    way_o = line(wo, 32)
    ways_1 = [line(w1.at[:, :, pl.ds(0, 1024)], 128) for t in range(1)]
    ways_2 = [line(w2.at[:, :, pl.ds(0, 1024)], 128) for t in range(1)]

    CUT = 2
    ROWS = 64 // CUT

    def gather(buf):
        return buf, take(2 * CUT + 1), track(buf.at[:, pl.ds(0, 3)], None, early)

    def gather_a(way):
        buf, sem, out = way
        for j in range(CUT):
            rows = pl.ds(j * ROWS, ROWS)
            send(buf.at[0, q, rows], buf.at[0, q, rows], sem + j, px, out)
            send(buf.at[1, q, rows], buf.at[1, q, rows], sem + CUT + j, py, out)
        send(buf.at[1, q], buf.at[1, q], sem + 2 * CUT, px, out)
        send(buf.at[0, q], buf.at[0, q], sem + 2 * CUT, py, out)

    def gather_b(way):
        buf, sem, out = way
        for j in range(CUT):
            rows = pl.ds(j * ROWS, ROWS)
            arrive(buf.at[0, qx, rows], sem + j)
            send(buf.at[0, qx, rows], buf.at[0, qx, rows], sem + 2 * CUT, py, out)
            arrive(buf.at[1, qy, rows], sem + CUT + j)
            send(buf.at[1, qy, rows], buf.at[1, qy, rows], sem + 2 * CUT, px, out)

    def gather_c(way):
        buf, sem, out = way
        arrive(buf.at[0], sem + 2 * CUT)

    def scatter(buf, rb):
        return buf, rb, take(3), track(rb.at[pl.ds(0, 6)], None, pending if buf is d1b else early)

    def scatter_a(way):
        buf, rb, sem, out = way
        send(buf.at[0, qd], rb.at[0], sem, px, out)
        send(buf.at[1, qd], rb.at[1], sem + 1, py, out)
        send(buf.at[0, qx], rb.at[2], sem + 2, px, out)
        send(buf.at[1, qy], rb.at[3], sem + 2, py, out)

    def scatter_b(way):
        buf, rb, sem, out = way
        arrive(rb.at[0], sem)
        rb[6] = (buf[0, qy].astype(F32) + rb[0].astype(F32)).astype(BF16)
        send(rb.at[6], rb.at[4], sem + 2, py, out)
        arrive(rb.at[1], sem + 1)
        rb[7] = (buf[1, qx].astype(F32) + rb[1].astype(F32)).astype(BF16)
        send(rb.at[7], rb.at[5], sem + 2, px, out)

    def scatter_c(way):
        buf, rb, sem, out = way
        arrive(rb.at[pl.ds(2, 4)], sem + 2)
        first = buf[0, q].astype(F32) + rb[2].astype(F32) + rb[4].astype(F32)
        second = buf[1, q].astype(F32) + rb[3].astype(F32) + rb[5].astype(F32)
        return jnp.concatenate([first, second], axis=0)

    p_n1, p_n2, p_dm, p_da = (gather(buf) for buf in (n1, n2, dmb, dab))
    p_a, p_m, p_d2, p_d1 = scatter(ab, ra), scatter(mb, rm), scatter(d2b, rd2), scatter(d1b, rd1)

    WAYS = 6
    halves = (128, 32, 128, 128, 128, 128)
    grads = (gq.at[0], go, g1, g2, gq.at[1], gq.at[2])
    cores = (cq.at[0], co, c1, c2, cq.at[1], cq.at[2])
    lines = (zq.at[0], zo, z1, z2, zq.at[1], zq.at[2])
    finals = (fq.at[0], fo, f1, f2, fq.at[1], fq.at[2])
    results = (oq.at[0], oo, o1, o2, oq.at[1], oq.at[2])
    t_core = [take(1) for _ in range(WAYS)]
    t_line = [take(3) for _ in range(WAYS)]
    t_rank = [take(3) for _ in range(WAYS)]
    t_pass = [take(1) for _ in range(WAYS)]
    stored = [None] * WAYS
    q_core = [track(cores[w]) for w in range(WAYS)]
    q_line = [track(lines[w].at[pl.ds(0, 3)]) for w in range(WAYS)]
    q_rank = [track(lines[w].at[pl.ds(0, 3)]) for w in range(WAYS)]
    q_pass = [track(cores[w]) for w in range(WAYS)]

    def reduce_a(w):
        send(grads[w].at[:, theirs(halves[w])], cores[w], t_core[w], partner, q_core[w])

    reach = (1 - lower, lower)

    def reduce_b(w):
        rows = mine(halves[w])
        arrive(cores[w], t_core[w])

        def step(zz, _):
            grads[w][zz, rows] = (grads[w][zz, rows].astype(F32) + cores[w][zz].astype(F32)).astype(BF16)
            return 0

        lax.fori_loop(0, Z, step, 0)
        for f in reach:
            send(
                grads[w].at[far + f, rows], lines[w].at[2 + f], t_line[w] + 1 + f, (replica, mate), q_line[w],
                when=end, got=middle,
            )
        send(grads[w].at[mate, rows], lines[w].at[0], t_line[w], (replica, mate), q_line[w])

    def reduce_m(w, k):
        rows = mine(halves[w])
        f = reach[k]

        @pl.when(middle)
        def _():
            arrive(lines[w].at[2 + f], t_line[w] + 1 + f)
            grads[w][far + f, rows] = (grads[w][far + f, rows].astype(F32) + lines[w][2 + f].astype(F32)).astype(BF16)

        send(grads[w].at[far + f, rows], lines[w].at[1], t_line[w], (replica, far + f), q_line[w], when=middle)

    def spots(w, rank, core):
        half = halves[w]
        first = pl.multiple_of(core * half, half)
        second = pl.multiple_of(core * half + half // 2, half // 2)
        return (
            results[w].at[rank, pl.ds(first, half // 2)],
            results[w].at[rank, pl.ds(second, half // 2)],
            results[w].at[rank, pl.ds(first, half)],
        )

    def reduce_c(w):
        half = halves[w]
        arrive(lines[w].at[pl.ds(0, 2)], t_line[w])
        total = grads[w][z, mine(half)].astype(F32)
        for k in range(2):
            total = total + lines[w][k].astype(F32)
        finals[w][...] = total.astype(BF16)
        one, two, both = spots(w, q, c)
        a, b = finals[w].at[pl.ds(0, half // 2)], finals[w].at[pl.ds(half // 2, half // 2)]
        send(a, one, t_rank[w], px, q_rank[w])
        send(b, two, t_rank[w] + 1, py, q_rank[w])
        send(b, two, t_rank[w] + 2, px, q_rank[w])
        send(a, one, t_rank[w] + 2, py, q_rank[w])
        stored[w] = pltpu.make_async_copy(finals[w], both, lsem.at[LOADS + w])
        stored[w].start()

    def reduce_d(w):
        one = spots(w, qx, c)[0]
        arrive(one, t_rank[w])
        send(one, one, t_rank[w] + 2, py, q_rank[w])
        two = spots(w, qy, c)[1]
        arrive(two, t_rank[w] + 1)
        send(two, two, t_rank[w] + 2, px, q_rank[w])

    def reduce_e(w):
        arrive(results[w].at[pl.ds(0, 2), mine(halves[w])], t_rank[w] + 2)
        stored[w].wait()
        part = results[w].at[:, mine(halves[w])]
        send(part, part, t_pass[w], partner, q_pass[w])

    def reduce_f(w):
        arrive(results[w].at[:, theirs(halves[w])], t_pass[w])

    for cp in loads[:n_first]:
        cp.wait()
    lane = lax.broadcasted_iota(jnp.int32, (256, 128), 1)
    even = q % 2 == 0
    for t in range(3):
        for m in range(2):
            left = tmp[t * RANKS + 2 * m].astype(F32)
            right = tmp[t * RANKS + 2 * m + 1].astype(F32)
            lo = jnp.where(even, left, pltpu.roll(left, HEAD, 1))
            hi = jnp.where(even, pltpu.roll(right, HEAD, 1), right)
            wq[z, :, t * 256 + m * 128 : t * 256 + m * 128 + 128] = jnp.where(lane < HEAD, lo, hi).astype(BF16)
    for way in ways_q:
        line_a(way)

    for s in range(SLOTS):
        alive = jnp.where(live[0] > s, 1.0, 0.0).astype(F32)
        cm[s] = (cot[s].astype(F32) * alive).astype(BF16)

    arrive(smg.at[pl.ds(0, 3)], s_small)

    def row(i):
        return jnp.concatenate([smg[zz, i : i + 1, :] for zz in range(Z)], axis=1)

    bias_q = smg[0, 12:13, :] + smg[1, 12:13, :] + smg[2, 12:13, :] + smg[3, 12:13, :]
    bias_v = smg[0, 13:14, :] + smg[1, 13:14, :] + smg[2, 13:14, :] + smg[3, 13:14, :]

    exchange_wait(rc, e_clips)
    x = rc[...].astype(F32).reshape(128, 1024)
    xh, _ = normed(x)
    n1[:, q] = (xh * row(0) + row(2)).astype(BF16).reshape(SLOTS, 64, 1024)
    gather_a(p_n1)
    line_b(ways_q[0])
    gather_b(p_n1)
    line_b(ways_q[1])
    line_b(ways_q[2])
    line_a(way_o)
    exchange(cm, dmt, e_cot, moves, early)
    gather_c(p_n1)
    for way in ways_q:
        line_c(way)
    line_b(way_o)
    for cp in loads[n_first:]:
        cp.wait()
    for way in ways_1:
        line_a(way)
    for way in ways_q:
        for k in range(1, Z):
            line_d(way, k)

    def qkv_step(t, _):
        bias = jnp.where(t == 0, bias_q, jnp.where(t == 2, bias_v, 0.0))
        val = mm(n1[...].reshape(512, 1024), wq[:, :, strip(t)].reshape(1024, 256)) + bias
        qkv[t] = val.astype(BF16).reshape(SLOTS, 256, 256)
        return 0

    lax.fori_loop(0, 3, qkv_step, 0)
    line_c(way_o)
    exchange_wait(dmt, e_cot)
    dmb[:, q] = dmt[...]
    gather_a(p_dm)

    def attend_pair(i):
        s = i // 2
        cols = strip(i % 2, 128)
        qq, kk, vv = qkv[0, s, :, cols], qkv[1, s, :, cols], qkv[2, s, :, cols]
        outs = []
        for j in range(2):
            h = slice(j * HEAD, j * HEAD + HEAD)
            score = mm_nt(qq[:, h], kk[:, h]) * SCALE
            e = jnp.exp(score - jnp.max(score, axis=-1, keepdims=True))
            p = e * (1.0 / jnp.sum(e, axis=-1, keepdims=True))
            probs[i, j] = p
            outs.append(mm(p.astype(BF16), vv[:, h]))
        ob[s, :, cols] = jnp.concatenate(outs, axis=1).astype(BF16)

    def attend(s, _):
        attend_pair(2 * s)
        attend_pair(2 * s + 1)
        return 0

    lax.fori_loop(0, SLOTS, attend, 0)
    for k in range(1, Z):
        line_d(way_o, k)

    def proj_step(s, _):
        val = mm(ob[s], wo[...].reshape(256, 1024))
        ab[s] = val.astype(BF16).reshape(RANKS, 64, 1024)
        return 0

    lax.fori_loop(0, SLOTS, proj_step, 0)
    scatter_a(p_a)
    gather_b(p_dm)
    scatter_b(p_a)
    for way in ways_1:
        line_b(way)
    for way in ways_2:
        line_a(way)
    a = scatter_c(p_a) + row(6)
    hh = x + a
    h1[...] = hh
    xh2, _ = normed(hh)
    n2[:, q] = (xh2 * row(1) + row(3)).astype(BF16).reshape(SLOTS, 64, 1024)
    gather_a(p_n2)
    gather_b(p_n2)
    for way in ways_1:
        line_c(way)
    for way in ways_2:
        line_b(way)
    for way in ways_1:
        for k in range(1, Z):
            line_d(way, k)
    gather_c(p_n2)

    def fc1_step(i, _):
        s = i // RANKS
        zz = i % RANKS
        cols = strip(zz)
        u = mm(n2[s].reshape(256, 1024), w1[:, :, cols].reshape(1024, 256)) + smg[zz, pl.ds(8 + q, 1), :]
        cdf = 0.5 * (1.0 + lax.erf(u * (1.0 / math.sqrt(2.0))))
        gb[s, :, cols] = (u * cdf).astype(BF16)
        slope[s, :, cols] = cdf + u * jnp.exp(-0.5 * u * u) * (1.0 / math.sqrt(2.0 * math.pi))
        return 0

    lax.fori_loop(0, SLOTS * RANKS, fc1_step, 0)
    gather_c(p_dm)

    def dw2_step(zz, _):
        g2[zz] = mm_tn(gb[:, :, strip(zz)].reshape(512, 256), dmb[...].reshape(512, 1024)).astype(BF16)
        return 0

    lax.fori_loop(0, RANKS, dw2_step, 0)
    reduce_a(3)
    for way in ways_2:
        line_c(way)

    for k in range(RANKS):
        zz = order[k]
        if k == 1:
            reduce_b(3)
        if k > 0:
            for way in ways_2:
                line_d(way, k)
        cols = strip(zz)
        dg = mm_nt(dmb[...].reshape(512, 1024), w2[zz]).reshape(SLOTS, 256, 256)
        du = (dg * slope[:, :, cols]).astype(BF16)
        dub[:, :, cols] = du

        def dn2_step(i, _, k=k, cols=cols):
            part = mm_nt(dub[:, :, cols].reshape(512, 256), w1[i, :, cols])
            if k > 0:
                part = part + total2[i]
            if k < RANKS - 1:
                total2[i] = part
            else:
                d2b[:, :, :, strip(i)] = part.astype(BF16).reshape(SLOTS, RANKS, 64, 256)
            return 0

        lax.fori_loop(0, RANKS, dn2_step, 0)
    scatter_a(p_d2)
    def m_step(s, _):
        mb[s] = mm(gb[s], w2[...].reshape(1024, 1024)).astype(BF16).reshape(RANKS, 64, 1024)
        return 0

    lax.fori_loop(0, SLOTS, m_step, 0)
    scatter_b(p_d2)
    scatter_a(p_m)

    def dw1_step(zz, _):
        g1[zz] = mm_tn(n2[:, :, :, strip(zz)].reshape(512, 256), dub[...].reshape(512, 1024)).astype(BF16)
        return 0

    lax.fori_loop(0, RANKS, dw1_step, 0)
    reduce_a(2)
    reduce_b(2)

    sms[...] = jnp.zeros((16, 1024), F32)

    def own(i, val):
        sms[i : i + 1, :] = jnp.sum(val, axis=0, keepdims=True)

    dy = dmt[...].astype(F32).reshape(128, 1024)
    own(7, dy)
    xh2, inv2 = normed(h1[...])
    dn2 = scatter_c(p_d2)
    res = dy + norm_back(dn2 * row(1), xh2, inv2)
    da = res.astype(BF16)
    dab[:, q] = da.reshape(SLOTS, 64, 1024)
    gather_a(p_da)
    for k in range(2):
        reduce_m(3, k)
    dh1[...] = res
    own(1, dn2 * xh2)
    own(3, dn2)
    own(6, da.astype(F32))
    fc1_sum = jnp.sum(dub[...].astype(F32).reshape(512, 1024), axis=0, keepdims=True)
    sms[pl.ds(9 + 2 * q, 1), :] = fc1_sum

    gather_b(p_da)
    scatter_b(p_m)
    gather_c(p_da)
    go[...] = mm_tn(ob[...].reshape(512, 256), dab[...].reshape(512, 1024)).astype(BF16).reshape(Z, HEAD, 1024)
    reduce_a(1)

    def do_step(s, _):
        dob[s] = mm_nt(dab[s].reshape(256, 1024), wo[...].reshape(256, 1024)).astype(BF16)
        return 0

    lax.fori_loop(0, SLOTS, do_step, 0)
    reduce_b(1)

    def attend_back(i, _):
        s = i // 2
        cols = strip(i % 2, 128)
        qq, kk, vv, dd = qkv[0, s, :, cols], qkv[1, s, :, cols], qkv[2, s, :, cols], dob[s, :, cols]
        dqs, dks, dvs = [], [], []
        for j in range(2):
            h = slice(j * HEAD, j * HEAD + HEAD)
            p = probs[i, j]
            dp = mm_nt(dd[:, h], vv[:, h])
            ds = (p * (dp - jnp.sum(p * dp, axis=-1, keepdims=True))).astype(BF16)
            dqs.append(mm(ds, kk[:, h]) * SCALE)
            dks.append(mm_tn(ds, qq[:, h]) * SCALE)
            dvs.append(mm_tn(p.astype(BF16), dd[:, h]))
        dqkv[0, s, :, cols] = jnp.concatenate(dqs, axis=1).astype(BF16)
        dqkv[1, s, :, cols] = jnp.concatenate(dks, axis=1).astype(BF16)
        dqkv[2, s, :, cols] = jnp.concatenate(dvs, axis=1).astype(BF16)
        return 0

    reduce_m(2, 0)
    lax.fori_loop(0, SLOTS, attend_back, 0)
    m = scatter_c(p_m) + row(7)
    outb[...] = (h1[...] + m).astype(BF16).reshape(SLOTS, 64, 1024)
    exchange(outb, out_k, e_out, backs)
    reduce_c(3)
    reduce_m(2, 1)
    lax.fori_loop(SLOTS, 2 * SLOTS, attend_back, 0)

    def dn1_step(zz, _):
        val = mm_nt(dqkv[0].reshape(512, 256), wq[zz, :, 0:256])
        val = val + mm_nt(dqkv[1].reshape(512, 256), wq[zz, :, 256:512])
        val = val + mm_nt(dqkv[2].reshape(512, 256), wq[zz, :, 512:768])
        d1b[:, :, :, strip(zz)] = val.astype(BF16).reshape(SLOTS, RANKS, 64, 256)
        return 0

    lax.fori_loop(0, RANKS, dn1_step, 0)
    scatter_a(p_d1)
    def dwq_step(zz, _):
        left = n1[:, :, :, strip(zz)].reshape(512, 256)
        for t in range(3):
            gq[t, zz] = mm_tn(left, dqkv[t].reshape(512, 256)).astype(BF16)
        return 0

    lax.fori_loop(0, RANKS, dwq_step, 0)
    for w in (0, 4, 5):
        reduce_a(w)

    for k in range(2):
        reduce_m(1, k)
    dq_sum = jnp.sum(dqkv[0].astype(F32).reshape(512, 256), axis=0, keepdims=True)
    dv_sum = jnp.sum(dqkv[2].astype(F32).reshape(512, 256), axis=0, keepdims=True)
    gap = jnp.zeros((1, 128), F32)
    pieces = []
    for zz in range(Z):
        h = slice(zz * HEAD, zz * HEAD + HEAD)
        pieces += [dq_sum[:, h], dv_sum[:, h], gap]
    sms[pl.ds(8 + 2 * q, 1), :] = jnp.concatenate(pieces, axis=1)
    scatter_b(p_d1)
    reduce_c(2)
    for w in (0, 4, 5):
        reduce_b(w)
    reduce_d(3)
    xh, inv = normed(rc[...].astype(F32).reshape(128, 1024))

    dn1 = scatter_c(p_d1)
    cgb[...] = (dh1[...] + norm_back(dn1 * row(0), xh, inv)).astype(BF16).reshape(SLOTS, 64, 1024)
    exchange(cgb, cg_k, e_cg, backs)
    own(0, dn1 * xh)
    own(2, dn1)

    u_core, u_line, u_rank = take(1), take(1), take(1)
    send(sms, smc, u_core, partner, track(sms))
    for k in range(2):
        reduce_m(0, k)
    for k in range(2):
        reduce_m(4, k)
    reduce_c(1)
    reduce_c(0)
    reduce_e(3)
    arrive(smc, u_core)
    both = sms[...] + smc[...]
    for zz in range(Z):
        smx[0, zz] = both[:, zz * 256 : zz * 256 + 256]
    o_line, o_rank = track(smz), track(smz)
    for d in range(1, Z):
        send(smx.at[0, (z + d) % Z], smz.at[d - 1], u_line, (replica, (z + d) % Z), o_line)
    for k in range(2):
        reduce_m(5, k)
    for finish in early:
        finish()
    reduce_d(2)
    reduce_c(4)
    reduce_d(1)
    reduce_c(5)
    reduce_d(0)
    reduce_e(2)
    reduce_d(4)
    arrive(smz, u_line)
    smx[1, 0] = smx[0, z] + smz[0] + smz[1] + smz[2]
    for k, rank in enumerate((qx, qy, qd)):
        send(smx.at[1, 0], smx.at[1, 1 + k], u_rank, dev(rank, c, z), o_rank)
    reduce_d(5)
    for w in (1, 0, 4, 5):
        reduce_e(w)
    arrive(smx.at[1, pl.ds(1, 3)], u_rank)
    sm_out[...] = smx[1, 0] + smx[1, 1] + smx[1, 2] + smx[1, 3]

    exchange_wait(out_k, e_out)
    exchange_wait(cg_k, e_cg)
    for w in (3, 2, 1, 0, 4, 5):
        reduce_f(w)
    assert counter == [ARRIVALS, SENDS], counter
    for finish in pending:
        finish()


def finish_kernel(
    live, out_k, cg_k, oq, oo, o1, o2, sm,
    out, cg, dwq, dwo, dw1, dw2, dgain, dnbias, dpbias, dfbias,
    b_out, b_cg, bq, bo, b1, b2, f_out, f_cg, fq, fo, f1, f2, isem, osem,
):
    ins, outs = [], []

    def fetch(src, dst):
        cp = pltpu.make_async_copy(src, dst, isem.at[len(ins)])
        cp.start()
        ins.append(cp)

    def store(src, dst):
        cp = pltpu.make_async_copy(src, dst, osem.at[len(outs)])
        cp.start()
        outs.append(cp)

    for h in range(2):
        fetch(o2.at[pl.ds(2 * h, 2)], b2.at[pl.ds(2 * h, 2)])
    for h in range(2):
        fetch(o1.at[:, pl.ds(128 * h, 128)], b1.at[:, pl.ds(128 * h, 128)])
    for h in range(2):
        fetch(oq.at[:, :, pl.ds(128 * h, 128)], bq.at[:, :, pl.ds(128 * h, 128)])
    fetch(oo, bo)
    fetch(cg_k, b_cg)
    fetch(out_k, b_out)

    dgain[...] = sm[0:2]
    dnbias[...] = sm[2:4]
    lane = lax.broadcasted_iota(jnp.int32, (1, 128), 1)
    rows = [sm[8 + 2 * k : 9 + 2 * k, 0:128] for k in range(RANKS)]
    turn = [pltpu.roll(r, HEAD, 1) for r in rows]
    for g in range(2):
        a, b = 2 * g, 2 * g + 1
        dpbias[0:1, g * 128 : g * 128 + 128] = jnp.where(lane < HEAD, rows[a], turn[b])
        dpbias[1:2, g * 128 : g * 128 + 128] = jnp.where(lane < HEAD, turn[a], rows[b])
    dpbias[2:4] = sm[6:8]
    for k in range(RANKS):
        dfbias[pl.ds(k * 256, 256)] = sm[9 + 2 * k : 10 + 2 * k, :].reshape(256)

    for h in range(2):
        ins[h].wait()

        def two(i, _, h=h):
            f2[pl.ds(512 * h + 64 * i, 64), :] = b2[2 * h + i // 4, strip(i % 4, 64), :].astype(F32)
            return 0

        lax.fori_loop(0, 8, two, 0)
        store(f2.at[pl.ds(512 * h, 512)], dw2.at[pl.ds(512 * h, 512)])
    for h in range(2):
        ins[2 + h].wait()

        def one(i, _, h=h):
            at = pl.ds(pl.multiple_of(128 * h + 16 * i, 16), 16)
            for k in range(RANKS):
                for zz in range(RANKS):
                    f1[at, zz * 1024 + k * 256 : zz * 1024 + k * 256 + 256] = b1[k, at, zz * 256 : zz * 256 + 256].astype(F32)
            return 0

        lax.fori_loop(0, 8, one, 0)
        store(f1.at[pl.ds(128 * h, 128)], dw1.at[pl.ds(128 * h, 128)])
    lane = lax.broadcasted_iota(jnp.int32, (16, 128), 1)
    for h in range(2):
        ins[4 + h].wait()

        def attn(i, _, h=h):
            at = pl.ds(pl.multiple_of(128 * h + 16 * i, 16), 16)
            for t in range(3):
                for m in range(2):
                    part = [bq[t, k, at, m * 128 : m * 128 + 128].astype(F32) for k in range(RANKS)]
                    turn = [pltpu.roll(p, HEAD, 1) for p in part]
                    col = t * 1024 + m * 512
                    for g in range(2):
                        a, b = 2 * g, 2 * g + 1
                        fq[at, col + g * 128 : col + g * 128 + 128] = jnp.where(lane < HEAD, part[a], turn[b])
                        fq[at, col + 256 + g * 128 : col + 384 + g * 128] = jnp.where(lane < HEAD, turn[a], part[b])
            return 0

        lax.fori_loop(0, 8, attn, 0)
        store(fq.at[pl.ds(128 * h, 128)], dwq.at[pl.ds(128 * h, 128)])
    ins[6].wait()
    fo[...] = bo[...].astype(F32).reshape(256, 1024)
    store(fo, dwo)
    ins[7].wait()
    f_cg[...] = b_cg[...].astype(F32).reshape(128, 1024)
    store(f_cg, cg)
    ins[8].wait()
    for s in range(SLOTS):
        alive = jnp.where(live[0] > s, 1.0, 0.0).astype(F32)
        f_out[s * 64 : s * 64 + 64] = (b_out[s].astype(F32) * alive).astype(BF16)
    store(f_out, out)
    for cp in outs:
        cp.wait()


def local(
    n_replica,
    clips, cotangent, live_count, w_qkv, w_out, w_fc1, w_fc2, norm_gain, norm_bias, proj_bias, fc1_bias,
):
    vm = pl.BlockSpec(memory_space=pltpu.VMEM)
    smem = pl.BlockSpec(memory_space=pltpu.SMEM)
    anyspace = pl.BlockSpec(memory_space=pl.ANY)
    shape = jax.ShapeDtypeStruct
    tile = (SLOTS, 64, 1024)
    group = (SLOTS, RANKS, 64, 1024)
    V = pltpu.VMEM
    scratch = [
        V(tile, BF16), V(tile, BF16), V(tile, BF16), V(tile, BF16), V((16, 256), F32), V((4, 16, 256), F32), V((12, 256, 128), BF16),
        V((4, 256, 768), BF16), V((4, 64, 1024), BF16), V((4, 256, 1024), BF16), V((4, 256, 1024), BF16),
        V(group, BF16), V(group, BF16), V(group, BF16), V(group, BF16),
        V((3, SLOTS, 256, 256), BF16), V((4, 2, 256, 256), F32), V((SLOTS, 256, 256), BF16),
        V(group, BF16), V(group, BF16), V(group, BF16), V(group, BF16),
        V((8, 64, 1024), BF16), V((8, 64, 1024), BF16), V((8, 64, 1024), BF16), V((8, 64, 1024), BF16),
        V((128, 1024), F32), V((128, 1024), F32), V((SLOTS, 256, 1024), F32), V((SLOTS, 256, 1024), BF16),
        V((SLOTS, 256, 1024), BF16), V((SLOTS, 256, 256), BF16), V((3, SLOTS, 256, 256), BF16),
        V((3, 4, 256, 256), BF16), V((4, 64, 1024), BF16), V((4, 256, 1024), BF16), V((4, 256, 1024), BF16),
        V((3, 4, 128, 256), BF16), V((4, 32, 1024), BF16), V((4, 128, 1024), BF16), V((4, 128, 1024), BF16),
        V((3, 4, 128, 256), BF16), V((4, 32, 1024), BF16), V((4, 128, 1024), BF16), V((4, 128, 1024), BF16),
        V((3, 128, 256), BF16), V((32, 1024), BF16), V((128, 1024), BF16), V((128, 1024), BF16),
        V(tile, BF16), V(tile, BF16), V((16, 1024), F32), V((16, 1024), F32), V((3, 16, 256), F32), V((2, 4, 16, 256), F32),
        V((4, 512, 256), F32),
        pltpu.SemaphoreType.DMA((SENDS,)), pltpu.SemaphoreType.DMA((ARRIVALS,)), pltpu.SemaphoreType.DMA((LOADS + 6,)),
    ]
    parts = pl.pallas_call(
        kernel,
        out_shape=(
            shape(tile, BF16), shape(tile, BF16), shape((3, 4, 256, 256), BF16), shape((4, 64, 1024), BF16),
            shape((4, 256, 1024), BF16), shape((4, 256, 1024), BF16), shape((16, 256), F32),
        ),
        in_specs=[anyspace, anyspace, smem, vm, vm, vm, vm, anyspace, anyspace, anyspace, anyspace],
        out_specs=(anyspace, anyspace, anyspace, anyspace, anyspace, anyspace, vm),
        scratch_shapes=scratch,
        compiler_params=pltpu.CompilerParams(
            collective_id=0, has_side_effects=True, vmem_limit_bytes=60 * 2**20
        ),
        cost_estimate=pl.CostEstimate(flops=10**10, bytes_accessed=2**25, transcendentals=2**21),
    )(clips, cotangent, live_count, norm_gain, norm_bias, proj_bias, fc1_bias, w_qkv, w_out, w_fc1, w_fc2)

    out, clips_grad, *summed = pl.pallas_call(
        finish_kernel,
        out_shape=(
            shape((128, 1024), BF16), shape((128, 1024), F32), shape((256, 3072), F32), shape((256, 1024), F32),
            shape((256, 4096), F32), shape((1024, 1024), F32), shape((2, 256), F32), shape((2, 256), F32),
            shape((4, 256), F32), shape((1024,), F32),
        ),
        in_specs=[smem] + [anyspace] * 6 + [vm],
        out_specs=[anyspace] * 6 + [vm] * 4,
        scratch_shapes=[
            V(tile, BF16), V(tile, BF16), V((3, 4, 256, 256), BF16), V((4, 64, 1024), BF16),
            V((4, 256, 1024), BF16), V((4, 256, 1024), BF16), V((128, 1024), BF16), V((128, 1024), F32),
            V((256, 3072), F32), V((256, 1024), F32), V((256, 4096), F32), V((1024, 1024), F32),
            pltpu.SemaphoreType.DMA((9,)), pltpu.SemaphoreType.DMA((9,)),
        ],
        compiler_params=pltpu.CompilerParams(vmem_limit_bytes=60 * 2**20),
        cost_estimate=pl.CostEstimate(flops=2**22, bytes_accessed=20 * 2**20, transcendentals=0),
    )(live_count, *parts)
    if n_replica > PLANE:
        groups = [list(range(i, n_replica, PLANE)) for i in range(PLANE)]
        summed = lax.psum(tuple(summed), "replica", axis_index_groups=groups)
    return (out.reshape(tile), clips_grad.reshape(tile)) + tuple(summed)


def solution(mesh):
    in_specs = (
        P("replica", "shard", None),
        P("replica", "shard", None),
        P("replica"),
        P("shard", None),
        P("shard", None),
        P("shard", None),
        P("shard", None),
        P(None, "shard"),
        P(None, "shard"),
        P(None, "shard"),
        P("shard"),
    )
    out_specs = (
        P("replica", "shard", None),
        P("replica", "shard", None),
        P("shard", None),
        P("shard", None),
        P("shard", None),
        P("shard", None),
        P(None, "shard"),
        P(None, "shard"),
        P(None, "shard"),
        P("shard"),
    )
    body = functools.partial(local, mesh.shape["replica"])
    return jax.shard_map(body, mesh=mesh, in_specs=in_specs, out_specs=out_specs, check_vma=False)
```

```python
import functools
import math

import jax
import jax.numpy as jnp
from jax import lax
from jax.experimental import pallas as pl
from jax.experimental.pallas import tpu as pltpu
from jax.sharding import PartitionSpec as P

MESH = pl.DeviceIdType.MESH
F32 = jnp.float32
BF16 = jnp.bfloat16
HEAD = 64
PLANE = 8
RANKS = 4
SLOTS = 2
ARRIVALS = 128
SENDS = 62
LOADS = 19
SCALE = 1.0 / math.sqrt(HEAD)


def mm(a, b):
    return jnp.dot(a, b, preferred_element_type=F32)


def mm_nt(a, b):
    return lax.dot_general(a, b, (((1,), (1,)), ((), ())), preferred_element_type=F32)


def mm_tn(a, b):
    return lax.dot_general(a, b, (((0,), (0,)), ((), ())), preferred_element_type=F32)


def normed(v):
    centre = v - jnp.mean(v, axis=-1, keepdims=True)
    spread = jnp.mean(centre * centre, axis=-1, keepdims=True)
    inverse = lax.rsqrt(spread + 1e-6)
    return centre * inverse, inverse


def norm_back(e, xh, inverse):
    first = jnp.mean(e, axis=-1, keepdims=True)
    second = jnp.mean(e * xh, axis=-1, keepdims=True)
    return inverse * (e - first - xh * second)


def strip(i, width=256):
    return pl.ds(pl.multiple_of(i * width, width), width)


def kernel(
    clips, cotangent, live, gains, nbias, pbias, fbias, w_qkv, w_out, w_fc1, w_fc2,
    out_k, cg_k, oq, oo, o1, o2, sm_out,
    cot, rc, cm, dmt, sml, smg, tmp, wq, wo, w1, w2,
    n1, n2, dmb, dab, qkv, probs, ob, ab, mb, d2b, d1b, ra, rm, rd2, rd1,
    h1, dh1, slope, gb, dub, dob, dqkv, gq, go, g1, g2,
    cq, co, c1, c2, zq, zo, z1, z2, fq, fo, f1, f2,
    outb, cgb, sms, smc, smz, smx, total2,
    ssem, rsem, lsem,
):
    Z = 4
    replica = lax.axis_index("replica")
    z = lax.axis_index("shard")
    r8 = replica % PLANE
    base = replica - r8
    q = r8 // 2
    c = r8 % 2
    qx = (q // 2) * 2 + (1 - q % 2)
    qy = (1 - q // 2) * 2 + q % 2
    qd = 3 - q
    lower = z // 2
    mate = 2 * lower + 1 - z % 2
    far_middle = 2 - lower
    far = 2 * (1 - lower)
    middle = jnp.logical_or(z == 1, z == 2)
    end = jnp.logical_not(middle)

    def dev(rank, core, plane):
        return (base + 2 * rank + core, plane)

    px, py, partner = dev(qx, c, z), dev(qy, c, z), dev(q, 1 - c, z)

    counter = [0, 0]

    def take(n):
        counter[0] += n
        return counter[0] - n

    early, pending = [], []

    def track(ref, when=None, into=pending):
        counter[1] += 1
        sem = counter[1] - 1

        def finish():
            pltpu.make_async_remote_copy(
                ref, ref, ssem.at[sem], rsem.at[0], device_id=partner, device_id_type=MESH
            ).wait_send()

        into.append(finish if when is None else lambda: pl.when(when)(finish))
        return sem

    def send(src, dst, sem, device, out, when=None, got=None):
        def start():
            pltpu.make_async_remote_copy(
                src, dst, ssem.at[out], rsem.at[sem], device_id=device, device_id_type=MESH
            ).start()

        if when is None:
            start()
        else:
            pl.when(when)(start)

    def arrive(dst, sem):
        pltpu.make_async_remote_copy(
            dst, dst, ssem.at[sem], rsem.at[sem], device_id=partner, device_id_type=MESH
        ).wait_recv()

    def flip(a, b):
        return (a // 2 + b // 2) % 2 * 2 + (a + b) % 2

    def target(s):
        plane = (q + 2 * s + c) % RANKS
        return flip(q, (z + plane) % RANKS), plane

    def origin(s):
        a = (z - 2 * s - c + 2 * RANKS) % RANKS
        return a, (flip(q, a) - z + RANKS) % RANKS

    moves = [target(s) for s in range(SLOTS)]
    backs = [origin(s) for s in range(SLOTS)]

    def stays(place):
        return jnp.logical_and(place[0] == q, place[1] == z)

    loads = []

    def load(src, dst):
        cp = pltpu.make_async_copy(src, dst, lsem.at[len(loads)])
        cp.start()
        loads.append(cp)

    pair = (q // 2) * 128
    for t in range(3):
        for zz in range(RANKS):
            load(w_qkv.at[:, pl.ds(pl.multiple_of(t * 1024 + zz * 256 + pair, 128), 128)], tmp.at[t * RANKS + zz])
    load(w_out.at[strip(q, HEAD), :], wo.at[z])
    load(cotangent, cot)

    barrier = pltpu.get_barrier_semaphore()
    for device in (px, py, dev(qd, c, z), partner):
        pl.semaphore_signal(barrier, inc=1, device_id=device, device_id_type=MESH)
    for d in range(1, Z):
        pl.semaphore_signal(barrier, inc=1, device_id=(replica, (z + d) % Z), device_id_type=MESH)
    count = 4 + Z - 1
    for place in moves + backs:

        @pl.when(jnp.logical_not(stays(place)))
        def _(place=place):
            pl.semaphore_signal(barrier, inc=1, device_id=dev(place[0], c, place[1]), device_id_type=MESH)

        count = count + jnp.where(stays(place), 0, 1)

    sml[...] = jnp.zeros((16, 256), F32)
    sml[0:2] = gains[...].astype(F32)
    sml[2:4] = nbias[...].astype(F32)
    sml[4:8] = pbias[...].astype(F32)
    for k in range(RANKS):
        sml[8 + k : 9 + k] = fbias[pl.ds(k * 256, 256)].astype(F32).reshape(1, 256)
    lane = lax.broadcasted_iota(jnp.int32, (8, 256), 1)
    turned = pltpu.roll(sml[0:8], (z * HEAD - q * HEAD + 256) % 256, 1)
    kept = jnp.where(jnp.logical_and(lane >= z * HEAD, lane < z * HEAD + HEAD), turned, 0.0)
    sml[12:14] = kept[4:6]

    pl.semaphore_wait(barrier, count)

    def exchange(src, dst, sem, places, into=pending):
        for s in range(SLOTS):
            to = dev(places[s][0], c, places[s][1])
            leaves = jnp.logical_not(stays(places[s]))
            send(src.at[s], dst.at[s], sem + s, to, track(src.at[s], leaves, into), when=leaves)

            @pl.when(stays(places[s]))
            def _(s=s):
                pltpu.make_async_copy(src.at[s], dst.at[s], rsem.at[sem + s]).start()

    def exchange_wait(dst, sem):
        for s in range(SLOTS):
            arrive(dst.at[s], sem + s)

    e_clips, e_cot, e_out, e_cg = take(2), take(2), take(2), take(2)
    exchange(clips, rc, e_clips, moves, early)
    s_small, o_small = take(1), track(smg.at[pl.ds(0, 3)], None, early)
    smg[z] = sml[...]
    for d in range(1, Z):
        send(sml, smg.at[z], s_small, (replica, (z + d) % Z), o_small)
    n_first = len(loads)
    for zz in range(RANKS):
        load(w_fc1.at[:, pl.ds(pl.multiple_of(zz * 1024 + q * 256, 256), 256)], w1.at[z, :, pl.ds(zz * 256, 256)])
    load(w_fc2.at[strip(q), :], w2.at[z])

    def mine(half):
        return pl.ds(pl.multiple_of(c * half, half), half)

    def theirs(half):
        return pl.ds(pl.multiple_of((1 - c) * half, half), half)

    def line(w, half):
        rows = pl.ds(0, half)
        own_sends = track(w.at[pl.ds(0, 2), rows], None, early)
        passed_on = track(w.at[pl.ds(0, 2), rows], middle, early)
        shared = track(w.at[pl.ds(0, 3), rows], None, early)
        return w, half, take(6), (own_sends, passed_on, shared)

    def line_a(way):
        w, half, sem, outs = way
        own_part = w.at[z, mine(half)]
        send(own_part, own_part, sem, (replica, mate), outs[0])
        send(own_part, own_part, sem + 1 + z % 2, (replica, far_middle), outs[0])

    def share(way, zz, when=None):
        w, half, sem, outs = way
        part = w.at[zz, mine(half)]
        send(part, part, sem + 2 + (zz - z + Z) % Z, partner, outs[2], when=when)

    def line_b(way):
        w, half, sem, outs = way
        for f in (lower, 1 - lower):

            @pl.when(middle)
            def _(f=f):
                arrive(w.at[far + f, mine(half)], sem + 1 + f)

            part = w.at[far + f, mine(half)]
            send(part, part, sem + 1 + f, (replica, mate), outs[1], when=middle)
            share(way, far + f, when=middle)

    def line_c(way):
        w, half, sem, outs = way
        arrive(w.at[mate, mine(half)], sem)
        share(way, mate)
        for f in (lower, 1 - lower):

            @pl.when(end)
            def _(f=f):
                arrive(w.at[far + f, mine(half)], sem + 1 + f)

            share(way, far + f, when=end)

    order = (z, mate, far + lower, far + 1 - lower)

    def line_d(way, k):
        w, half, sem, outs = way
        arrive(w.at[order[k], theirs(half)], sem + 2 + (order[k] - z + Z) % Z)

    ways_q = [line(wq.at[:, :, pl.ds(t * 256, 256)], 128) for t in range(3)]
    way_o = line(wo, 32)
    ways_1 = [line(w1.at[:, :, pl.ds(0, 1024)], 128) for t in range(1)]
    ways_2 = [line(w2.at[:, :, pl.ds(0, 1024)], 128) for t in range(1)]

    CUT = 2
    ROWS = 64 // CUT

    def gather(buf):
        return buf, take(2 * CUT + 1), track(buf.at[:, pl.ds(0, 3)], None, early)

    def gather_a(way):
        buf, sem, out = way
        for j in range(CUT):
            rows = pl.ds(j * ROWS, ROWS)
            send(buf.at[0, q, rows], buf.at[0, q, rows], sem + j, px, out)
            send(buf.at[1, q, rows], buf.at[1, q, rows], sem + CUT + j, py, out)
        send(buf.at[1, q], buf.at[1, q], sem + 2 * CUT, px, out)
        send(buf.at[0, q], buf.at[0, q], sem + 2 * CUT, py, out)

    def gather_b(way):
        buf, sem, out = way
        for j in range(CUT):
            rows = pl.ds(j * ROWS, ROWS)
            arrive(buf.at[0, qx, rows], sem + j)
            send(buf.at[0, qx, rows], buf.at[0, qx, rows], sem + 2 * CUT, py, out)
            arrive(buf.at[1, qy, rows], sem + CUT + j)
            send(buf.at[1, qy, rows], buf.at[1, qy, rows], sem + 2 * CUT, px, out)

    def gather_c(way):
        buf, sem, out = way
        arrive(buf.at[0], sem + 2 * CUT)

    def scatter(buf, rb):
        return buf, rb, take(3), track(rb.at[pl.ds(0, 6)], None, pending if buf is d1b else early)

    def scatter_a(way):
        buf, rb, sem, out = way
        send(buf.at[0, qd], rb.at[0], sem, px, out)
        send(buf.at[1, qd], rb.at[1], sem + 1, py, out)
        send(buf.at[0, qx], rb.at[2], sem + 2, px, out)
        send(buf.at[1, qy], rb.at[3], sem + 2, py, out)

    def scatter_b(way):
        buf, rb, sem, out = way
        arrive(rb.at[0], sem)
        rb[6] = (buf[0, qy].astype(F32) + rb[0].astype(F32)).astype(BF16)
        send(rb.at[6], rb.at[4], sem + 2, py, out)
        arrive(rb.at[1], sem + 1)
        rb[7] = (buf[1, qx].astype(F32) + rb[1].astype(F32)).astype(BF16)
        send(rb.at[7], rb.at[5], sem + 2, px, out)

    def scatter_c(way):
        buf, rb, sem, out = way
        arrive(rb.at[pl.ds(2, 4)], sem + 2)
        first = buf[0, q].astype(F32) + rb[2].astype(F32) + rb[4].astype(F32)
        second = buf[1, q].astype(F32) + rb[3].astype(F32) + rb[5].astype(F32)
        return jnp.concatenate([first, second], axis=0)

    p_n1, p_n2, p_dm, p_da = (gather(buf) for buf in (n1, n2, dmb, dab))
    p_a, p_m, p_d2, p_d1 = scatter(ab, ra), scatter(mb, rm), scatter(d2b, rd2), scatter(d1b, rd1)

    WAYS = 6
    halves = (128, 32, 128, 128, 128, 128)
    grads = (gq.at[0], go, g1, g2, gq.at[1], gq.at[2])
    cores = (cq.at[0], co, c1, c2, cq.at[1], cq.at[2])
    lines = (zq.at[0], zo, z1, z2, zq.at[1], zq.at[2])
    finals = (fq.at[0], fo, f1, f2, fq.at[1], fq.at[2])
    results = (oq.at[0], oo, o1, o2, oq.at[1], oq.at[2])
    t_core = [take(1) for _ in range(WAYS)]
    t_line = [take(3) for _ in range(WAYS)]
    t_rank = [take(3) for _ in range(WAYS)]
    t_pass = [take(1) for _ in range(WAYS)]
    stored = [None] * WAYS
    q_core = [track(cores[w]) for w in range(WAYS)]
    q_line = [track(lines[w].at[pl.ds(0, 3)]) for w in range(WAYS)]
    q_rank = [track(lines[w].at[pl.ds(0, 3)]) for w in range(WAYS)]
    q_pass = [track(cores[w]) for w in range(WAYS)]

    def reduce_a(w):
        send(grads[w].at[:, theirs(halves[w])], cores[w], t_core[w], partner, q_core[w])

    reach = (1 - lower, lower)

    def reduce_b(w):
        rows = mine(halves[w])
        arrive(cores[w], t_core[w])

        def step(zz, _):
            grads[w][zz, rows] = (grads[w][zz, rows].astype(F32) + cores[w][zz].astype(F32)).astype(BF16)
            return 0

        lax.fori_loop(0, Z, step, 0)
        for f in reach:
            send(
                grads[w].at[far + f, rows], lines[w].at[2 + f], t_line[w] + 1 + f, (replica, mate), q_line[w],
                when=end, got=middle,
            )
        send(grads[w].at[mate, rows], lines[w].at[0], t_line[w], (replica, mate), q_line[w])

    def reduce_m(w, k):
        rows = mine(halves[w])
        f = reach[k]

        @pl.when(middle)
        def _():
            arrive(lines[w].at[2 + f], t_line[w] + 1 + f)
            grads[w][far + f, rows] = (grads[w][far + f, rows].astype(F32) + lines[w][2 + f].astype(F32)).astype(BF16)

        send(grads[w].at[far + f, rows], lines[w].at[1], t_line[w], (replica, far + f), q_line[w], when=middle)

    def spots(w, rank, core):
        half = halves[w]
        first = pl.multiple_of(core * half, half)
        second = pl.multiple_of(core * half + half // 2, half // 2)
        return (
            results[w].at[rank, pl.ds(first, half // 2)],
            results[w].at[rank, pl.ds(second, half // 2)],
            results[w].at[rank, pl.ds(first, half)],
        )

    def reduce_c(w):
        half = halves[w]
        arrive(lines[w].at[pl.ds(0, 2)], t_line[w])
        total = grads[w][z, mine(half)].astype(F32)
        for k in range(2):
            total = total + lines[w][k].astype(F32)
        finals[w][...] = total.astype(BF16)
        one, two, both = spots(w, q, c)
        a, b = finals[w].at[pl.ds(0, half // 2)], finals[w].at[pl.ds(half // 2, half // 2)]
        send(a, one, t_rank[w], px, q_rank[w])
        send(b, two, t_rank[w] + 1, py, q_rank[w])
        send(b, two, t_rank[w] + 2, px, q_rank[w])
        send(a, one, t_rank[w] + 2, py, q_rank[w])
        stored[w] = pltpu.make_async_copy(finals[w], both, lsem.at[LOADS + w])
        stored[w].start()

    def reduce_d(w):
        one = spots(w, qx, c)[0]
        arrive(one, t_rank[w])
        send(one, one, t_rank[w] + 2, py, q_rank[w])
        two = spots(w, qy, c)[1]
        arrive(two, t_rank[w] + 1)
        send(two, two, t_rank[w] + 2, px, q_rank[w])

    def reduce_e(w):
        arrive(results[w].at[pl.ds(0, 2), mine(halves[w])], t_rank[w] + 2)
        stored[w].wait()
        part = results[w].at[:, mine(halves[w])]
        send(part, part, t_pass[w], partner, q_pass[w])

    def reduce_f(w):
        arrive(results[w].at[:, theirs(halves[w])], t_pass[w])

    for cp in loads[:n_first]:
        cp.wait()
    lane = lax.broadcasted_iota(jnp.int32, (256, 128), 1)
    even = q % 2 == 0
    for t in range(3):
        for m in range(2):
            left = tmp[t * RANKS + 2 * m].astype(F32)
            right = tmp[t * RANKS + 2 * m + 1].astype(F32)
            lo = jnp.where(even, left, pltpu.roll(left, HEAD, 1))
            hi = jnp.where(even, pltpu.roll(right, HEAD, 1), right)
            wq[z, :, t * 256 + m * 128 : t * 256 + m * 128 + 128] = jnp.where(lane < HEAD, lo, hi).astype(BF16)
    for way in ways_q:
        line_a(way)

    for s in range(SLOTS):
        alive = jnp.where(live[0] > s, 1.0, 0.0).astype(F32)
        cm[s] = (cot[s].astype(F32) * alive).astype(BF16)

    arrive(smg.at[pl.ds(0, 3)], s_small)

    def row(i):
        return jnp.concatenate([smg[zz, i : i + 1, :] for zz in range(Z)], axis=1)

    bias_q = smg[0, 12:13, :] + smg[1, 12:13, :] + smg[2, 12:13, :] + smg[3, 12:13, :]
    bias_v = smg[0, 13:14, :] + smg[1, 13:14, :] + smg[2, 13:14, :] + smg[3, 13:14, :]

    exchange_wait(rc, e_clips)
    x = rc[...].astype(F32).reshape(128, 1024)
    xh, _ = normed(x)
    n1[:, q] = (xh * row(0) + row(2)).astype(BF16).reshape(SLOTS, 64, 1024)
    gather_a(p_n1)
    line_b(ways_q[0])
    gather_b(p_n1)
    line_b(ways_q[1])
    line_b(ways_q[2])
    line_a(way_o)
    exchange(cm, dmt, e_cot, moves, early)
    gather_c(p_n1)
    for way in ways_q:
        line_c(way)
    line_b(way_o)
    for cp in loads[n_first:]:
        cp.wait()
    for way in ways_1:
        line_a(way)
    for way in ways_q:
        for k in range(1, Z):
            line_d(way, k)

    def qkv_step(t, _):
        bias = jnp.where(t == 0, bias_q, jnp.where(t == 2, bias_v, 0.0))
        val = mm(n1[...].reshape(512, 1024), wq[:, :, strip(t)].reshape(1024, 256)) + bias
        qkv[t] = val.astype(BF16).reshape(SLOTS, 256, 256)
        return 0

    lax.fori_loop(0, 3, qkv_step, 0)
    line_c(way_o)
    exchange_wait(dmt, e_cot)
    dmb[:, q] = dmt[...]
    gather_a(p_dm)

    def attend_pair(i):
        s = i // 2
        cols = strip(i % 2, 128)
        qq, kk, vv = qkv[0, s, :, cols], qkv[1, s, :, cols], qkv[2, s, :, cols]
        outs = []
        for j in range(2):
            h = slice(j * HEAD, j * HEAD + HEAD)
            score = mm_nt(qq[:, h], kk[:, h]) * SCALE
            e = jnp.exp(score - jnp.max(score, axis=-1, keepdims=True))
            p = e * (1.0 / jnp.sum(e, axis=-1, keepdims=True))
            probs[i, j] = p
            outs.append(mm(p.astype(BF16), vv[:, h]))
        ob[s, :, cols] = jnp.concatenate(outs, axis=1).astype(BF16)

    def attend(s, _):
        attend_pair(2 * s)
        attend_pair(2 * s + 1)
        return 0

    lax.fori_loop(0, SLOTS, attend, 0)
    for k in range(1, Z):
        line_d(way_o, k)

    def proj_step(s, _):
        val = mm(ob[s], wo[...].reshape(256, 1024))
        ab[s] = val.astype(BF16).reshape(RANKS, 64, 1024)
        return 0

    lax.fori_loop(0, SLOTS, proj_step, 0)
    scatter_a(p_a)
    gather_b(p_dm)
    scatter_b(p_a)
    for way in ways_1:
        line_b(way)
    for way in ways_2:
        line_a(way)
    a = scatter_c(p_a) + row(6)
    hh = x + a
    h1[...] = hh
    xh2, _ = normed(hh)
    n2[:, q] = (xh2 * row(1) + row(3)).astype(BF16).reshape(SLOTS, 64, 1024)
    gather_a(p_n2)
    gather_b(p_n2)
    for way in ways_1:
        line_c(way)
    for way in ways_2:
        line_b(way)
    for way in ways_1:
        for k in range(1, Z):
            line_d(way, k)
    gather_c(p_n2)

    def fc1_step(i, _):
        s = i // RANKS
        zz = i % RANKS
        cols = strip(zz)
        u = mm(n2[s].reshape(256, 1024), w1[:, :, cols].reshape(1024, 256)) + smg[zz, pl.ds(8 + q, 1), :]
        cdf = 0.5 * (1.0 + lax.erf(u * (1.0 / math.sqrt(2.0))))
        gb[s, :, cols] = (u * cdf).astype(BF16)
        slope[s, :, cols] = cdf + u * jnp.exp(-0.5 * u * u) * (1.0 / math.sqrt(2.0 * math.pi))
        return 0

    lax.fori_loop(0, SLOTS * RANKS, fc1_step, 0)
    gather_c(p_dm)

    def dw2_step(zz, _):
        g2[zz] = mm_tn(gb[:, :, strip(zz)].reshape(512, 256), dmb[...].reshape(512, 1024)).astype(BF16)
        return 0

    lax.fori_loop(0, RANKS, dw2_step, 0)
    reduce_a(3)
    for way in ways_2:
        line_c(way)

    for k in range(RANKS):
        zz = order[k]
        if k == 1:
            reduce_b(3)
        if k > 0:
            for way in ways_2:
                line_d(way, k)
        cols = strip(zz)
        dg = mm_nt(dmb[...].reshape(512, 1024), w2[zz]).reshape(SLOTS, 256, 256)
        du = (dg * slope[:, :, cols]).astype(BF16)
        dub[:, :, cols] = du

        def dn2_step(i, _, k=k, cols=cols):
            part = mm_nt(dub[:, :, cols].reshape(512, 256), w1[i, :, cols])
            if k > 0:
                part = part + total2[i]
            if k < RANKS - 1:
                total2[i] = part
            else:
                d2b[:, :, :, strip(i)] = part.astype(BF16).reshape(SLOTS, RANKS, 64, 256)
            return 0

        lax.fori_loop(0, RANKS, dn2_step, 0)
    scatter_a(p_d2)
    def m_step(s, _):
        mb[s] = mm(gb[s], w2[...].reshape(1024, 1024)).astype(BF16).reshape(RANKS, 64, 1024)
        return 0

    lax.fori_loop(0, SLOTS, m_step, 0)
    scatter_b(p_d2)
    scatter_a(p_m)

    def dw1_step(zz, _):
        g1[zz] = mm_tn(n2[:, :, :, strip(zz)].reshape(512, 256), dub[...].reshape(512, 1024)).astype(BF16)
        return 0

    lax.fori_loop(0, RANKS, dw1_step, 0)
    reduce_a(2)
    reduce_b(2)

    sms[...] = jnp.zeros((16, 1024), F32)

    def own(i, val):
        sms[i : i + 1, :] = jnp.sum(val, axis=0, keepdims=True)

    dy = dmt[...].astype(F32).reshape(128, 1024)
    own(7, dy)
    xh2, inv2 = normed(h1[...])
    dn2 = scatter_c(p_d2)
    res = dy + norm_back(dn2 * row(1), xh2, inv2)
    da = res.astype(BF16)
    dab[:, q] = da.reshape(SLOTS, 64, 1024)
    gather_a(p_da)
    for k in range(2):
        reduce_m(3, k)
    dh1[...] = res
    gather_b(p_da)
    own(1, dn2 * xh2)
    own(3, dn2)
    own(6, da.astype(F32))
    fc1_sum = jnp.sum(dub[...].astype(F32).reshape(512, 1024), axis=0, keepdims=True)
    sms[pl.ds(9 + 2 * q, 1), :] = fc1_sum

    scatter_b(p_m)
    gather_c(p_da)
    def do_step(s, _):
        dob[s] = mm_nt(dab[s].reshape(256, 1024), wo[...].reshape(256, 1024)).astype(BF16)
        return 0

    lax.fori_loop(0, SLOTS, do_step, 0)

    def attend_back(i, _):
        s = i // 2
        cols = strip(i % 2, 128)
        qq, kk, vv, dd = qkv[0, s, :, cols], qkv[1, s, :, cols], qkv[2, s, :, cols], dob[s, :, cols]
        dqs, dks, dvs = [], [], []
        for j in range(2):
            h = slice(j * HEAD, j * HEAD + HEAD)
            p = probs[i, j]
            dp = mm_nt(dd[:, h], vv[:, h])
            ds = (p * (dp - jnp.sum(p * dp, axis=-1, keepdims=True))).astype(BF16)
            dqs.append(mm(ds, kk[:, h]) * SCALE)
            dks.append(mm_tn(ds, qq[:, h]) * SCALE)
            dvs.append(mm_tn(p.astype(BF16), dd[:, h]))
        dqkv[0, s, :, cols] = jnp.concatenate(dqs, axis=1).astype(BF16)
        dqkv[1, s, :, cols] = jnp.concatenate(dks, axis=1).astype(BF16)
        dqkv[2, s, :, cols] = jnp.concatenate(dvs, axis=1).astype(BF16)
        return 0

    reduce_m(2, 0)
    lax.fori_loop(0, SLOTS, attend_back, 0)
    m = scatter_c(p_m) + row(7)
    outb[...] = (h1[...] + m).astype(BF16).reshape(SLOTS, 64, 1024)
    exchange(outb, out_k, e_out, backs)
    reduce_c(3)
    reduce_m(2, 1)
    go[...] = mm_tn(ob[...].reshape(512, 256), dab[...].reshape(512, 1024)).astype(BF16).reshape(Z, HEAD, 1024)
    reduce_a(1)

    lax.fori_loop(SLOTS, 2 * SLOTS, attend_back, 0)

    def dn1_step(zz, _):
        val = mm_nt(dqkv[0].reshape(512, 256), wq[zz, :, 0:256])
        val = val + mm_nt(dqkv[1].reshape(512, 256), wq[zz, :, 256:512])
        val = val + mm_nt(dqkv[2].reshape(512, 256), wq[zz, :, 512:768])
        d1b[:, :, :, strip(zz)] = val.astype(BF16).reshape(SLOTS, RANKS, 64, 256)
        return 0

    lax.fori_loop(0, RANKS, dn1_step, 0)
    reduce_b(1)
    scatter_a(p_d1)
    def dwq_step(zz, _):
        left = n1[:, :, :, strip(zz)].reshape(512, 256)
        for t in range(3):
            gq[t, zz] = mm_tn(left, dqkv[t].reshape(512, 256)).astype(BF16)
        return 0

    lax.fori_loop(0, RANKS, dwq_step, 0)
    for w in (0, 4, 5):
        reduce_a(w)

    for k in range(2):
        reduce_m(1, k)
    dq_sum = jnp.sum(dqkv[0].astype(F32).reshape(512, 256), axis=0, keepdims=True)
    dv_sum = jnp.sum(dqkv[2].astype(F32).reshape(512, 256), axis=0, keepdims=True)
    gap = jnp.zeros((1, 128), F32)
    pieces = []
    for zz in range(Z):
        h = slice(zz * HEAD, zz * HEAD + HEAD)
        pieces += [dq_sum[:, h], dv_sum[:, h], gap]
    sms[pl.ds(8 + 2 * q, 1), :] = jnp.concatenate(pieces, axis=1)
    scatter_b(p_d1)
    reduce_c(2)
    for w in (0, 4, 5):
        reduce_b(w)
    reduce_d(3)
    xh, inv = normed(rc[...].astype(F32).reshape(128, 1024))

    dn1 = scatter_c(p_d1)
    cgb[...] = (dh1[...] + norm_back(dn1 * row(0), xh, inv)).astype(BF16).reshape(SLOTS, 64, 1024)
    exchange(cgb, cg_k, e_cg, backs)
    own(0, dn1 * xh)
    own(2, dn1)

    u_core, u_line, u_rank = take(1), take(1), take(1)
    send(sms, smc, u_core, partner, track(sms))
    for k in range(2):
        reduce_m(0, k)
    for k in range(2):
        reduce_m(4, k)
    reduce_c(1)
    reduce_c(0)
    arrive(smc, u_core)
    both = sms[...] + smc[...]
    for zz in range(Z):
        smx[0, zz] = both[:, zz * 256 : zz * 256 + 256]
    o_line, o_rank = track(smz), track(smz)
    for d in range(1, Z):
        send(smx.at[0, (z + d) % Z], smz.at[d - 1], u_line, (replica, (z + d) % Z), o_line)
    for k in range(2):
        reduce_m(5, k)
    for finish in early:
        finish()
    reduce_d(2)
    reduce_c(4)
    reduce_d(1)
    reduce_c(5)
    reduce_e(3)
    reduce_d(0)
    reduce_e(2)
    reduce_d(4)
    arrive(smz, u_line)
    smx[1, 0] = smx[0, z] + smz[0] + smz[1] + smz[2]
    for k, rank in enumerate((qx, qy, qd)):
        send(smx.at[1, 0], smx.at[1, 1 + k], u_rank, dev(rank, c, z), o_rank)
    reduce_d(5)
    for w in (1, 0, 4, 5):
        reduce_e(w)
    arrive(smx.at[1, pl.ds(1, 3)], u_rank)
    sm_out[...] = smx[1, 0] + smx[1, 1] + smx[1, 2] + smx[1, 3]

    exchange_wait(out_k, e_out)
    exchange_wait(cg_k, e_cg)
    for w in (3, 2, 1, 0, 4, 5):
        reduce_f(w)
    assert counter == [ARRIVALS, SENDS], counter
    for finish in pending:
        finish()


def finish_kernel(
    live, out_k, cg_k, oq, oo, o1, o2, sm,
    out, cg, dwq, dwo, dw1, dw2, dgain, dnbias, dpbias, dfbias,
    b_out, b_cg, bq, bo, b1, b2, f_out, f_cg, fq, fo, f1, f2, isem, osem,
):
    ins, outs = [], []

    def fetch(src, dst):
        cp = pltpu.make_async_copy(src, dst, isem.at[len(ins)])
        cp.start()
        ins.append(cp)

    def store(src, dst):
        cp = pltpu.make_async_copy(src, dst, osem.at[len(outs)])
        cp.start()
        outs.append(cp)

    for h in range(2):
        fetch(o2.at[pl.ds(2 * h, 2)], b2.at[pl.ds(2 * h, 2)])
    for h in range(2):
        fetch(o1.at[:, pl.ds(128 * h, 128)], b1.at[:, pl.ds(128 * h, 128)])
    for h in range(2):
        fetch(oq.at[:, :, pl.ds(128 * h, 128)], bq.at[:, :, pl.ds(128 * h, 128)])
    fetch(oo, bo)
    fetch(cg_k, b_cg)
    fetch(out_k, b_out)

    dgain[...] = sm[0:2]
    dnbias[...] = sm[2:4]
    lane = lax.broadcasted_iota(jnp.int32, (1, 128), 1)
    rows = [sm[8 + 2 * k : 9 + 2 * k, 0:128] for k in range(RANKS)]
    turn = [pltpu.roll(r, HEAD, 1) for r in rows]
    for g in range(2):
        a, b = 2 * g, 2 * g + 1
        dpbias[0:1, g * 128 : g * 128 + 128] = jnp.where(lane < HEAD, rows[a], turn[b])
        dpbias[1:2, g * 128 : g * 128 + 128] = jnp.where(lane < HEAD, turn[a], rows[b])
    dpbias[2:4] = sm[6:8]
    for k in range(RANKS):
        dfbias[pl.ds(k * 256, 256)] = sm[9 + 2 * k : 10 + 2 * k, :].reshape(256)

    for h in range(2):
        ins[h].wait()

        def two(i, _, h=h):
            f2[pl.ds(512 * h + 64 * i, 64), :] = b2[2 * h + i // 4, strip(i % 4, 64), :].astype(F32)
            return 0

        lax.fori_loop(0, 8, two, 0)
        store(f2.at[pl.ds(512 * h, 512)], dw2.at[pl.ds(512 * h, 512)])
    for h in range(2):
        ins[2 + h].wait()

        def one(i, _, h=h):
            at = pl.ds(pl.multiple_of(128 * h + 16 * i, 16), 16)
            for k in range(RANKS):
                for zz in range(RANKS):
                    f1[at, zz * 1024 + k * 256 : zz * 1024 + k * 256 + 256] = b1[k, at, zz * 256 : zz * 256 + 256].astype(F32)
            return 0

        lax.fori_loop(0, 8, one, 0)
        store(f1.at[pl.ds(128 * h, 128)], dw1.at[pl.ds(128 * h, 128)])
    lane = lax.broadcasted_iota(jnp.int32, (16, 128), 1)
    for h in range(2):
        ins[4 + h].wait()

        def attn(i, _, h=h):
            at = pl.ds(pl.multiple_of(128 * h + 16 * i, 16), 16)
            for t in range(3):
                for m in range(2):
                    part = [bq[t, k, at, m * 128 : m * 128 + 128].astype(F32) for k in range(RANKS)]
                    turn = [pltpu.roll(p, HEAD, 1) for p in part]
                    col = t * 1024 + m * 512
                    for g in range(2):
                        a, b = 2 * g, 2 * g + 1
                        fq[at, col + g * 128 : col + g * 128 + 128] = jnp.where(lane < HEAD, part[a], turn[b])
                        fq[at, col + 256 + g * 128 : col + 384 + g * 128] = jnp.where(lane < HEAD, turn[a], part[b])
            return 0

        lax.fori_loop(0, 8, attn, 0)
        store(fq.at[pl.ds(128 * h, 128)], dwq.at[pl.ds(128 * h, 128)])
    ins[6].wait()
    fo[...] = bo[...].astype(F32).reshape(256, 1024)
    store(fo, dwo)
    ins[7].wait()
    f_cg[...] = b_cg[...].astype(F32).reshape(128, 1024)
    store(f_cg, cg)
    ins[8].wait()
    for s in range(SLOTS):
        alive = jnp.where(live[0] > s, 1.0, 0.0).astype(F32)
        f_out[s * 64 : s * 64 + 64] = (b_out[s].astype(F32) * alive).astype(BF16)
    store(f_out, out)
    for cp in outs:
        cp.wait()


def local(
    n_replica,
    clips, cotangent, live_count, w_qkv, w_out, w_fc1, w_fc2, norm_gain, norm_bias, proj_bias, fc1_bias,
):
    vm = pl.BlockSpec(memory_space=pltpu.VMEM)
    smem = pl.BlockSpec(memory_space=pltpu.SMEM)
    anyspace = pl.BlockSpec(memory_space=pl.ANY)
    shape = jax.ShapeDtypeStruct
    tile = (SLOTS, 64, 1024)
    group = (SLOTS, RANKS, 64, 1024)
    V = pltpu.VMEM
    scratch = [
        V(tile, BF16), V(tile, BF16), V(tile, BF16), V(tile, BF16), V((16, 256), F32), V((4, 16, 256), F32), V((12, 256, 128), BF16),
        V((4, 256, 768), BF16), V((4, 64, 1024), BF16), V((4, 256, 1024), BF16), V((4, 256, 1024), BF16),
        V(group, BF16), V(group, BF16), V(group, BF16), V(group, BF16),
        V((3, SLOTS, 256, 256), BF16), V((4, 2, 256, 256), F32), V((SLOTS, 256, 256), BF16),
        V(group, BF16), V(group, BF16), V(group, BF16), V(group, BF16),
        V((8, 64, 1024), BF16), V((8, 64, 1024), BF16), V((8, 64, 1024), BF16), V((8, 64, 1024), BF16),
        V((128, 1024), F32), V((128, 1024), F32), V((SLOTS, 256, 1024), F32), V((SLOTS, 256, 1024), BF16),
        V((SLOTS, 256, 1024), BF16), V((SLOTS, 256, 256), BF16), V((3, SLOTS, 256, 256), BF16),
        V((3, 4, 256, 256), BF16), V((4, 64, 1024), BF16), V((4, 256, 1024), BF16), V((4, 256, 1024), BF16),
        V((3, 4, 128, 256), BF16), V((4, 32, 1024), BF16), V((4, 128, 1024), BF16), V((4, 128, 1024), BF16),
        V((3, 4, 128, 256), BF16), V((4, 32, 1024), BF16), V((4, 128, 1024), BF16), V((4, 128, 1024), BF16),
        V((3, 128, 256), BF16), V((32, 1024), BF16), V((128, 1024), BF16), V((128, 1024), BF16),
        V(tile, BF16), V(tile, BF16), V((16, 1024), F32), V((16, 1024), F32), V((3, 16, 256), F32), V((2, 4, 16, 256), F32),
        V((4, 512, 256), F32),
        pltpu.SemaphoreType.DMA((SENDS,)), pltpu.SemaphoreType.DMA((ARRIVALS,)), pltpu.SemaphoreType.DMA((LOADS + 6,)),
    ]
    parts = pl.pallas_call(
        kernel,
        out_shape=(
            shape(tile, BF16), shape(tile, BF16), shape((3, 4, 256, 256), BF16), shape((4, 64, 1024), BF16),
            shape((4, 256, 1024), BF16), shape((4, 256, 1024), BF16), shape((16, 256), F32),
        ),
        in_specs=[anyspace, anyspace, smem, vm, vm, vm, vm, anyspace, anyspace, anyspace, anyspace],
        out_specs=(anyspace, anyspace, anyspace, anyspace, anyspace, anyspace, vm),
        scratch_shapes=scratch,
        compiler_params=pltpu.CompilerParams(
            collective_id=0, has_side_effects=True, vmem_limit_bytes=60 * 2**20
        ),
        cost_estimate=pl.CostEstimate(flops=10**10, bytes_accessed=2**25, transcendentals=2**21),
    )(clips, cotangent, live_count, norm_gain, norm_bias, proj_bias, fc1_bias, w_qkv, w_out, w_fc1, w_fc2)

    out, clips_grad, *summed = pl.pallas_call(
        finish_kernel,
        out_shape=(
            shape((128, 1024), BF16), shape((128, 1024), F32), shape((256, 3072), F32), shape((256, 1024), F32),
            shape((256, 4096), F32), shape((1024, 1024), F32), shape((2, 256), F32), shape((2, 256), F32),
            shape((4, 256), F32), shape((1024,), F32),
        ),
        in_specs=[smem] + [anyspace] * 6 + [vm],
        out_specs=[anyspace] * 6 + [vm] * 4,
        scratch_shapes=[
            V(tile, BF16), V(tile, BF16), V((3, 4, 256, 256), BF16), V((4, 64, 1024), BF16),
            V((4, 256, 1024), BF16), V((4, 256, 1024), BF16), V((128, 1024), BF16), V((128, 1024), F32),
            V((256, 3072), F32), V((256, 1024), F32), V((256, 4096), F32), V((1024, 1024), F32),
            pltpu.SemaphoreType.DMA((9,)), pltpu.SemaphoreType.DMA((9,)),
        ],
        compiler_params=pltpu.CompilerParams(vmem_limit_bytes=60 * 2**20),
        cost_estimate=pl.CostEstimate(flops=2**22, bytes_accessed=20 * 2**20, transcendentals=0),
    )(live_count, *parts)
    if n_replica > PLANE:
        groups = [list(range(i, n_replica, PLANE)) for i in range(PLANE)]
        summed = lax.psum(tuple(summed), "replica", axis_index_groups=groups)
    return (out.reshape(tile), clips_grad.reshape(tile)) + tuple(summed)


def solution(mesh):
    in_specs = (
        P("replica", "shard", None),
        P("replica", "shard", None),
        P("replica"),
        P("shard", None),
        P("shard", None),
        P("shard", None),
        P("shard", None),
        P(None, "shard"),
        P(None, "shard"),
        P(None, "shard"),
        P("shard"),
    )
    out_specs = (
        P("replica", "shard", None),
        P("replica", "shard", None),
        P("shard", None),
        P("shard", None),
        P("shard", None),
        P("shard", None),
        P(None, "shard"),
        P(None, "shard"),
        P(None, "shard"),
        P("shard"),
    )
    body = functools.partial(local, mesh.shape["replica"])
    return jax.shard_map(body, mesh=mesh, in_specs=in_specs, out_specs=out_specs, check_vma=False)
```
